32 devices in a mesh: rows: 16 (over z, x, core), cols: 2 (over y).
Axes of the slice: x: 2, y: 2, z: 4, core: 2. Of those that a mesh axis runs over, the one named last changes fastest.
Arguments:
- tokens: bfloat16 [512, 32, 768], P('rows', 'cols'), may hold values from -6 to 6
- image_ids: int32 [512, 32], P('rows', 'cols'), may hold values from 0 to 135, as said below
- joined_weight: bfloat16 [768, 5376], replicated, may hold values from -0.21875 to 0.21875
- hidden_bias: float32 [3072], replicated, may hold values from -3 to 3
- mixer_weight: bfloat16 [768, 768], replicated, may hold values from -0.875 to 0.875
- dense_weight: bfloat16 [3072, 768], replicated, may hold values from -0.15625 to 0.15625
- output_bias: float32 [768], replicated, may hold values from -3 to 3
- norm_gain: float32 [768], replicated, may hold values from 0.5 to 1.5
- query_gain: float32 [64], replicated, may hold values from 0.8 to 2
- key_gain: float32 [64], replicated, may hold values from 0.8 to 2
- cotangent: bfloat16 [512, 32, 768], P('rows', 'cols'), may hold values from -6 to 6
Outputs:
- result: bfloat16 [512, 32, 768], P('rows', 'cols')
- tokens_grad: bfloat16 [512, 32, 768], P('rows', 'cols')
- joined_grad: float32 [768, 5376], P('rows', 'cols')
- hidden_grad: float32 [3072], replicated
- mixer_grad: float32 [768, 768], P('rows', 'cols')
- dense_grad: float32 [3072, 768], P('rows', 'cols')
- output_grad: float32 [768], replicated
- norm_grad: float32 [768], replicated
- query_grad: float32 [64], replicated
- key_grad: float32 [64], replicated
The draws below stay inside these ranges and needn't reach their ends.
Inputs may be any that keep to these rules, and one draw needn't show every extreme that they name: `image_ids`: patches of one id form one axis-aligned rectangle of at most 32 by 32 patches (one image).
All inputs are finite; a program needn't handle non-finite values.
Results may differ from the reference program's by a relative error of at most 0.015.
Values may be sent and summed in bfloat16 or wider, within the bound.
No kernel may reach another device: no remote copies, remote signals or barrier semaphores. Data moves between devices by JAX's collectives and lax.ppermute only.
A program may use at most 192 MiB of HBM per device.

```python
import jax
import jax.numpy as jnp
from jax import lax

D = 768
H = 12
HD = 64
FF = 3072
TR = 32
RADIUS = 3
CANVAS = 32
NR = 512
NC = 32


def bump_cuts(values):
    return jnp.where(values % (CANVAS // 4) == CANVAS // 8, values + 1, values)


def draw_image_ids(key, part):
    key = jax.random.fold_in(key, 11)
    layout_key, row_key, col_key = jax.random.split(key, 3)
    leading = CANVAS - CANVAS // 8
    across_count = NC // CANVAS + 1
    canvases = (NR // CANVAS + 1) * across_count
    layouts = jax.random.randint(layout_key, (canvases,), 0, 4)
    layouts = layouts.at[0].set(0).at[canvases - 1].set(3)
    row_cuts = bump_cuts(jax.random.randint(row_key, (canvases,), 2, CANVAS - 1)).at[canvases - 1].set(2)
    col_cuts = bump_cuts(jax.random.randint(col_key, (canvases,), 2, CANVAS - 1)).at[canvases - 1].set(2)
    row_place = jnp.arange(NR, dtype=jnp.int32) + leading
    col_place = jnp.arange(NC, dtype=jnp.int32) + leading
    canvas = (row_place // CANVAS)[:, None] * across_count + (col_place // CANVAS)[None, :]
    below_cut = ((row_place % CANVAS)[:, None] >= row_cuts[canvas]).astype(jnp.int32)
    beyond_cut = ((col_place % CANVAS)[None, :] >= col_cuts[canvas]).astype(jnp.int32)
    chosen = layouts[canvas]
    quarter = chosen % 2 * below_cut + 2 * (chosen // 2) * beyond_cut
    return (canvas * 4 + quarter).astype(jnp.int32)


def levels(stream_key, dims, cuts, smallest, largest):
    loudness, own = 1.0, jax.random.fold_in(stream_key, 6)
    for dim, blocks in cuts:
        draws = jnp.exp(jax.random.uniform(jax.random.fold_in(own, dim), (blocks,), jnp.float32, smallest / len(cuts), largest / len(cuts)))
        loudness = loudness * jnp.repeat(draws, dims[dim] // blocks).reshape([-1 if axis == dim else 1 for axis in range(len(dims))])
    return loudness


def normal_values(rng, dims, scale, limit, cuts=(), kind=jnp.bfloat16):
    array = jax.random.normal(rng, dims, jnp.float32) * scale
    if len(cuts) > 0:
        array = levels(rng, dims, cuts, -0.22, 0.18) * array
    return jnp.clip(array, min=-limit, max=limit).astype(kind)


def setup_inputs(seed: int = 0) -> dict:
    key_of = jax.random.split(jax.random.key(seed), 12)
    tokens = normal_values(key_of[0], (NR, NC, D), 1.0, 6.0, ((0, 16), (1, 2)))
    image_ids = draw_image_ids(jax.random.fold_in(key_of[11], 71), 0)
    joined_weight = normal_values(key_of[2], (D, 3 * D + FF), D ** -0.5, 0.21875)
    hidden_bias = normal_values(key_of[3], (FF,), 0.5, 3.0, (), jnp.float32)
    mixer_weight = normal_values(key_of[4], (D, D), (D // 16) ** -0.5, 0.875)
    dense_weight = normal_values(key_of[5], (FF, D), (FF // 2) ** -0.5, 0.15625)
    output_bias = normal_values(key_of[6], (D,), 0.5, 3.0, (), jnp.float32)
    norm_gain = jnp.clip(1.0 + 0.1 * jax.random.normal(key_of[7], (D,), jnp.float32), 0.5, 1.5)
    query_gain = jnp.clip(jax.random.uniform(key_of[8], (HD,), jnp.float32, 0.8, 2.0), 0.8, 2.0)
    key_gain = jnp.clip(jax.random.uniform(key_of[9], (HD,), jnp.float32, 0.8, 2.0), 0.8, 2.0)
    cotangent = normal_values(key_of[10], (NR, NC, D), 1.0, 6.0, ((0, 16), (1, 2)))
    return dict(tokens=tokens, image_ids=image_ids, joined_weight=joined_weight, hidden_bias=hidden_bias, mixer_weight=mixer_weight, dense_weight=dense_weight, output_bias=output_bias, norm_gain=norm_gain, query_gain=query_gain, key_gain=key_gain, cotangent=cotangent)


EPSILON = 1e-06

@jax.custom_vjp
def low(v):
    return lax.optimization_barrier(v.astype(jnp.bfloat16)).astype(jnp.float32)

@jax.custom_vjp
def low_back(v):
    return v

def low_keep(v):
    return (low(v), None)

def low_pass(kept, grad):
    return (grad,)

def back_keep(v):
    return (v, None)

def back_low(kept, grad):
    return (low(grad),)
low.defvjp(low_keep, low_pass)
low_back.defvjp(back_keep, back_low)

def layer_norm(values, gains):
    center = values - lax.optimization_barrier(jnp.mean(values, axis=-1, keepdims=True))
    spread = lax.optimization_barrier(jnp.mean(center * center, axis=-1, keepdims=True))
    return center * lax.rsqrt(spread + EPSILON) * gains

def attend_block(query_block, key_window, value_window, id_window, id_block):
    span = 2 * RADIUS + 1
    score_list = []
    mask_list = []
    for row_off in range(span):
        for col_off in range(span):
            key_slice = key_window[row_off:row_off + TR, col_off:col_off + NC]
            score_list.append(lax.optimization_barrier(jnp.sum(query_block * key_slice, axis=-1)))
            mask_list.append(id_window[row_off:row_off + TR, col_off:col_off + NC] == id_block)
    scores = low_back(jnp.stack(score_list) * HD ** (-0.5))
    allowed = jnp.stack(mask_list)[..., None]
    scores = jnp.where(allowed, scores, -1e+30)
    highest = lax.optimization_barrier(jnp.max(scores, axis=0, keepdims=True))
    weights = jnp.where(allowed, jnp.exp(scores - highest), 0.0)
    probs = low(weights / lax.optimization_barrier(jnp.sum(weights, axis=0, keepdims=True)))
    mixed = jnp.zeros(query_block.shape, jnp.float32)
    position = 0
    for row_off in range(span):
        for col_off in range(span):
            value_slice = value_window[row_off:row_off + TR, col_off:col_off + NC]
            mixed = mixed + probs[position][..., None] * value_slice
            position = position + 1
    return mixed

def attend(queries, keys, values, image_ids):
    pad_spec = ((RADIUS, RADIUS), (RADIUS, RADIUS), (0, 0), (0, 0))
    keys_padded = jnp.pad(keys, pad_spec)
    values_padded = jnp.pad(values, pad_spec)
    ids_padded = jnp.pad(image_ids, RADIUS, constant_values=-1)
    blocks = NR // TR
    window = TR + 2 * RADIUS
    query_blocks = queries.reshape(blocks, TR, NC, H, HD)
    id_blocks = image_ids.reshape(blocks, TR, NC)
    starts = (jnp.arange(blocks) * TR).astype(jnp.int32)

    @jax.checkpoint
    def one_block(inputs):
        query_block, id_block, start = inputs
        key_window = lax.dynamic_slice_in_dim(keys_padded, start, window, 0)
        value_window = lax.dynamic_slice_in_dim(values_padded, start, window, 0)
        id_window = lax.dynamic_slice_in_dim(ids_padded, start, window, 0)
        return attend_block(query_block, key_window, value_window, id_window, id_block)
    return lax.map(one_block, (query_blocks, id_blocks, starts)).reshape(NR, NC, H, HD)

def forward(inputs, joined_weight, hidden_bias, mixer_weight, dense_weight, output_bias, norm_gain, query_gain, key_gain, image_ids):
    highest = lax.Precision.HIGHEST
    normed = low(layer_norm(inputs, norm_gain))
    joined = low_back(jnp.einsum('rcd,de->rce', normed, joined_weight, precision=highest))
    query_part = joined[..., :D].reshape(NR, NC, H, HD)
    key_part = joined[..., D:2 * D].reshape(NR, NC, H, HD)
    values = low(joined[..., 2 * D:3 * D]).reshape(NR, NC, H, HD)
    queries = low(layer_norm(query_part, query_gain))
    keys = low(layer_norm(key_part, key_gain))
    hidden = low(jax.nn.gelu(joined[..., 3 * D:] + hidden_bias, approximate=True))
    mixed = low(low_back(attend(queries, keys, values, image_ids).reshape(NR, NC, D)))
    branches = jnp.einsum('rcd,de->rce', mixed, mixer_weight, precision=highest)
    branches = branches + jnp.einsum('rcf,fe->rce', hidden, dense_weight, precision=highest)
    return inputs + branches + output_bias

def reference(tokens, image_ids, joined_weight, hidden_bias, mixer_weight, dense_weight, output_bias, norm_gain, query_gain, key_gain, cotangent):
    floats = [member.astype(jnp.float32) for member in (tokens, joined_weight, hidden_bias, mixer_weight, dense_weight, output_bias, norm_gain, query_gain, key_gain)]

    def layer(*params):
        return forward(*params, image_ids)
    outcome, pullback = jax.vjp(layer, *floats)
    grads = pullback(cotangent.astype(jnp.float32))
    return (outcome.astype(jnp.bfloat16), grads[0].astype(jnp.bfloat16), grads[1], grads[2], grads[3], grads[4], grads[5], grads[6], grads[7], grads[8])
```

```python
import functools

import jax
import jax.numpy as jnp
from jax import lax
from jax.experimental import pallas as pl
from jax.experimental.pallas import tpu as pltpu
from jax.sharding import PartitionSpec as P

H = 12
HD = 64
RADIUS = 3
EPSILON = 1e-06
BF = jnp.bfloat16
F32 = jnp.float32
MIB = 1024 * 1024

UNIT = 192
STRIP = 4
KEYS = 256
HALO_SLOTS = 8


def mm(a, b, ca=1, cb=0):
    return lax.dot_general(a, b, (((ca,), (cb,)), ((), ())), preferred_element_type=F32)


def call(kernel, scalars, ins, outs, grid=(1,), scratch=(), flops=0, vmem=48):
    def spec(value, block, index):
        if block is None:
            zeros = (0,) * len(value.shape)
            return pl.BlockSpec(value.shape, lambda *a: zeros)
        return pl.BlockSpec(block, index)

    return pl.pallas_call(
        kernel,
        grid_spec=pltpu.PrefetchScalarGridSpec(
            num_scalar_prefetch=1,
            grid=grid,
            in_specs=[spec(*entry) for entry in ins],
            out_specs=[spec(*entry) for entry in outs],
            scratch_shapes=list(scratch),
        ),
        out_shape=[entry[0] for entry in outs],
        compiler_params=pltpu.CompilerParams(vmem_limit_bytes=vmem * MIB),
        cost_estimate=pl.CostEstimate(flops=flops, bytes_accessed=4 * MIB, transcendentals=0),
    )(scalars, *[entry[0] for entry in ins])


def whole(x):
    return (x, None, None)


def out(shape, dtype):
    return (jax.ShapeDtypeStruct(shape, dtype), None, None)


def head_means(width):
    row = lax.broadcasted_iota(jnp.int32, (width, width), 0)
    col = lax.broadcasted_iota(jnp.int32, (width, width), 1)
    return jnp.where(row // HD == col // HD, 1.0 / HD, 0.0).astype(BF)


def per_head(x, means):
    width = means.shape[0]
    parts = [mm(x[:, j : j + width].astype(BF), means) for j in range(0, x.shape[1], width)]
    return jnp.concatenate(parts, axis=1)


def weights_kernel(sc, w_ref, b_ref, w_out, b_out):
    for core in range(2):

        @pl.when(sc[0] == core)
        def _():
            lo, hi = core * UNIT, (2 + core) * UNIT
            w = w_ref[...]
            w_out[...] = jnp.concatenate([w[:, lo : lo + UNIT], w[:, hi : hi + UNIT]], axis=1)
            b = b_ref[...]
            b_out[...] = jnp.concatenate([b[:, lo : lo + UNIT], b[:, hi : hi + UNIT]], axis=1)


def project_kernel(
    sc, xo, xt, wq, wk, wv, gain, qg, kg, normed, qs, kv, qhat, khat, qrs, krs, *, own
):
    means = head_means(2 * HD)
    block = 256
    for half, ref in enumerate((xo, xt)):
        for i in range(own // block):
            x = ref[i * block : (i + 1) * block, :].astype(F32)
            place = (sc[0] if half == 0 else 1 - sc[0]) * own + i * block
            rows = pl.ds(pl.multiple_of(place, block), block)
            center = x - jnp.mean(x, axis=1, keepdims=True)
            spread = jnp.mean(center * center, axis=1, keepdims=True)
            n = (center * lax.rsqrt(spread + EPSILON) * gain[...]).astype(BF)
            normed[rows, :] = n
            for w, hat_ref, rs_ref, gains in ((wq, qhat, qrs, qg), (wk, khat, krs, kg)):
                part = mm(n, w[...])
                center = part - per_head(part, means)
                rs = lax.rsqrt(per_head(center * center, means) + EPSILON)
                hat = center * rs
                hat_ref[rows, :] = hat.astype(BF)
                rs_ref[rows, :] = rs.astype(BF)
                low = (hat * gains[...]).astype(BF)
                if w is wq:
                    qs[rows, :] = low * jnp.asarray(HD**-0.5, BF)
                else:
                    kv[rows, :384] = low
            kv[rows, 384:] = mm(n, wv[...]).astype(BF)


def cotangent_kernel(sc, go, gt, mixer, g_out, gm, gsum, *, own):
    for half, ref in enumerate((go, gt)):
        place = (sc[0] if half == 0 else 1 - sc[0]) * own
        rows = pl.ds(pl.multiple_of(place, own), own)
        g = ref[...]
        g_out[rows, :] = g
        gm[rows, :] = mm(g, mixer[...], 1, 1).astype(BF)
    gsum[...] = jnp.sum(go[...].astype(F32), axis=0, keepdims=True)


def hidden_kernel(sc, n_ref, g_ref, wf, wd, bias, hidden, gpre, hsum):
    pre = mm(n_ref[...], wf[...]) + bias[...]
    wide = wd.shape[0] * UNIT
    gd = mm(g_ref[...], wd[...].reshape(wide, wd.shape[-1]), 1, 1)
    a, b = 0.7978845608, 0.044715
    sq = pre * pre
    t = jnp.tanh(a * pre * (1.0 + b * sq))
    half = 0.5 * (1.0 + t)
    hidden[...] = (pre * half).astype(BF)
    slope = half + (0.5 * a) * pre * (1.0 - t * t) * (1.0 + 3.0 * b * sq)
    gp = gd * slope
    gpre[...] = gp.astype(BF)

    @pl.when(pl.program_id(0) == 0)
    def _():
        hsum[...] = jnp.zeros_like(hsum)

    hsum[...] += jnp.sum(gp, axis=0, keepdims=True)


def dense_grad_kernel(sc, h_ref, g_ref, keep, send, scr):
    wide, d = scr.shape
    step = wide // 3
    half = d // 2
    for j in range(3):
        scr[j * step : (j + 1) * step, :] = mm(
            h_ref[:, j * step : (j + 1) * step], g_ref[...], 0, 0
        ).astype(BF)
    near = pl.ds(pl.multiple_of(sc[1] * half, 128), half)
    far = pl.ds(pl.multiple_of((1 - sc[1]) * half, 128), half)
    for rel in range(8):
        rows = pl.ds(pl.multiple_of(sc[2 + rel] * UNIT, 64), UNIT)
        keep[rel] = scr[rows, near]
        send[rel] = scr[rows, far]


def joined_grad_kernel(sc, n_ref, gp_ref, keep, send, scr):
    step = scr.shape[1] // 3
    for j in range(3):
        scr[:, j * step : (j + 1) * step] = mm(
            n_ref[...], gp_ref[:, j * step : (j + 1) * step], 0, 0
        ).astype(BF)
    size = scr.shape[0] // 8
    for rel in range(8):
        rows = pl.ds(pl.multiple_of(sc[2 + rel] * size, 32), size)
        if rel < 4:
            keep[rel] = scr[rows, :]
        else:
            send[rel - 4] = scr[rows, :]


def back_kernel(sc, h_ref, gp_ref, wf, wd, p_keep, p_send, g_keep, g_send, scr, *, own):
    wide = wd.shape[0] * UNIT
    dense = wd[...].reshape(wide, wd.shape[-1])
    mine = pl.ds(pl.multiple_of(sc[0] * own, own), own)
    other = pl.ds(pl.multiple_of((1 - sc[0]) * own, own), own)
    p_keep[...] = mm(h_ref[mine, :], dense)
    p_send[...] = mm(h_ref[other, :], dense).astype(BF)
    g_keep[...] = mm(gp_ref[mine, :], wf[...], 1, 1)
    g_send[...] = mm(gp_ref[other, :], wf[...], 1, 1)


def edge_picks(rows, first, count):
    msg = lax.broadcasted_iota(jnp.int32, (count, rows), 0)
    tok = lax.broadcasted_iota(jnp.int32, (count, rows), 1)
    return jnp.where(tok == msg // 3 * 16 + first + msg % 3, 1.0, 0.0).astype(BF)


def slot_places(count, slots, first):
    slot = lax.broadcasted_iota(jnp.int32, (slots, count), 0)
    msg = lax.broadcasted_iota(jnp.int32, (slots, count), 1)
    return jnp.where(slot == msg // 3 * HALO_SLOTS + first + msg % 3, 1.0, 0.0).astype(BF)


def extend_kernel(sc, kv, top, bottom, ko, left_msg, right_msg):
    edge = top.shape[0]
    own = kv.shape[0]
    ko[:edge, :] = top[...]
    ko[edge : edge + own, :] = kv[...]
    ko[edge + own :, :] = bottom[...]
    count = left_msg.shape[0]
    left_msg[...] = mm(edge_picks(ko.shape[0], 0, count), ko[...]).astype(BF)
    right_msg[...] = mm(edge_picks(ko.shape[0], 13, count), ko[...]).astype(BF)


def slots_kernel(sc, left, right, kh):
    count, slots = left.shape[0], kh.shape[0]
    kh[...] = (
        mm(slot_places(count, slots, 0), left[...]) + mm(slot_places(count, slots, 3), right[...])
    ).astype(BF)


def mask_kernel(sc, ids, bias):
    lane = lax.broadcasted_iota(jnp.int32, (STRIP * 16, KEYS), 1)
    query = lax.broadcasted_iota(jnp.int32, (STRIP * 16, KEYS), 0)
    inner = lane < 160
    halo = lane - 160
    slot = halo % HALO_SLOTS
    key_row = jnp.where(inner, lane // 16, halo // HALO_SLOTS)
    key_col = jnp.where(inner, lane % 16, jnp.where(slot < 3, slot - 3, slot + 13))
    row_gap = key_row - query // 16
    col_gap = key_col - query % 16
    reach = (
        (row_gap >= 0)
        & (row_gap <= 2 * RADIUS)
        & (col_gap >= -RADIUS)
        & (col_gap <= RADIUS)
        & (inner | (slot < 6))
    )
    itself = inner & (row_gap == RADIUS) & (col_gap == 0)
    lane16 = lax.broadcasted_iota(jnp.int32, (16, KEYS), 1)
    window = jnp.zeros((16, KEYS), F32)
    for i in range(STRIP + 2 * RADIUS):
        part = jnp.concatenate(
            [ids[pl.ds(i, 16, stride=STRIP), :], jnp.zeros((16, KEYS - 128), F32)], axis=1
        )
        own = jnp.where(lane16 < 16, part, 0.0)
        side = jnp.where(lane16 >= 16, part, 0.0)
        if i > 0:
            own = pltpu.roll(own, 16 * i, 1)
        side = pltpu.roll(side, 144 + HALO_SLOTS * i, 1)
        window = window + own + side
    for s in range(16):
        row = jnp.broadcast_to(window[s : s + 1, :], (STRIP * 16, KEYS))
        mine = jnp.sum(jnp.where(itself, row, 0.0), axis=1, keepdims=True)
        bias[s * 64 : (s + 1) * 64, :] = jnp.where(reach & (row == mine), 0.0, -1e30).astype(BF)


def attention_kernel(sc, q_ref, gm_ref, ko_k, ko_v, kh_k, kh_v, bias, mixed, dq, dko_k, dko_v, dkh_k, dkh_v):
    for ref in (dko_k, dko_v, dkh_k, dkh_v):
        ref[...] = jnp.zeros_like(ref)
    lane = lax.broadcasted_iota(jnp.int32, (64, 128), 1)
    low = lane < HD
    zero = jnp.zeros((64, 128), BF)

    def pair(x):
        return jnp.concatenate([jnp.where(low, x, zero), jnp.where(low, zero, x)], axis=0)

    for s in range(16):
        rows = slice(s * 64, (s + 1) * 64)
        inner = slice(s * 64, s * 64 + 160)
        side = slice(s * 32, s * 32 + 96)
        q2, gm2 = pair(q_ref[rows, :]), pair(gm_ref[rows, :])
        k = jnp.concatenate([ko_k[inner, :], kh_k[side, :]], axis=0)
        v = jnp.concatenate([ko_v[inner, :], kh_v[side, :]], axis=0)
        b = bias[rows, :].astype(F32)
        weights = jnp.exp(mm(q2, k, 1, 1) + jnp.concatenate([b, b], axis=0))
        probs = weights * (1.0 / jnp.sum(weights, axis=1, keepdims=True))
        probs_low = probs.astype(BF)
        o = mm(probs_low, v)
        mixed[rows, :] = jnp.where(low, o[:64], o[64:]).astype(BF)
        dp = mm(gm2, v, 1, 1)
        balance = jnp.sum(probs * dp, axis=1, keepdims=True)
        ds = (probs * (dp - balance)).astype(BF)
        d = mm(ds, k)
        dq[rows, :] = jnp.where(low, d[:64], d[64:]) * (HD**-0.5)
        dk = mm(ds, q2, 0, 0)
        dv = mm(probs_low, gm2, 0, 0)
        dko_k[inner, :] += dk[:160]
        dkh_k[side, :] += dk[160:]
        dko_v[inner, :] += dv[:160]
        dkh_v[side, :] += dv[160:]


def unslot_kernel(sc, dkh, to_left, to_right):
    count, slots = to_left.shape[0], dkh.shape[0]
    low = dkh[...].astype(BF)
    to_left[...] = mm(slot_places(count, slots, 0), low, 0, 0).astype(BF)
    to_right[...] = mm(slot_places(count, slots, 3), low, 0, 0).astype(BF)


def fold_kernel(sc, dko, from_left, from_right, to_up, to_down, center):
    count, rows = from_left.shape[0], dko.shape[0]
    edge = to_up.shape[0]
    total = (
        dko[...]
        + mm(edge_picks(rows, 0, count), from_left[...], 0, 0)
        + mm(edge_picks(rows, 13, count), from_right[...], 0, 0)
    )
    to_up[...] = total[:edge].astype(BF)
    to_down[...] = total[rows - edge :].astype(BF)
    center[...] = total[edge : rows - edge]


def qkv_back_kernel(
    sc, dq, dkv, from_up, from_down, qhat, khat, qrs, krs, qg, kg, n_ref, gj, keep, send, sums, scr
):
    means = head_means(2 * HD)
    tokens = dq.shape[0]
    edge = from_up.shape[0]
    block = 256
    width = dq.shape[1]
    totals = [jnp.zeros((1, width), F32), jnp.zeros((1, width), F32)]
    for i in range(tokens // block):
        rows = slice(i * block, (i + 1) * block)
        grads = dkv[rows, :]
        if i == 0:
            grads = jnp.concatenate([grads[:edge] + from_up[...].astype(F32), grads[edge:]], axis=0)
        if i == tokens // block - 1:
            grads = jnp.concatenate(
                [grads[:-edge], grads[-edge:] + from_down[...].astype(F32)], axis=0
            )
        pieces = (
            (dq[rows, :], qhat, qrs, qg),
            (grads[:, :width], khat, krs, kg),
        )
        for n, (grad, hat_ref, rs_ref, gains) in enumerate(pieces):
            hat = hat_ref[rows, :].astype(F32)
            totals[n] = totals[n] + jnp.sum(grad * hat, axis=0, keepdims=True)
            u = gains[...] * grad
            back = (u - per_head(u, means) - hat * per_head(u * hat, means)) * rs_ref[rows, :].astype(F32)
            gj[rows, n * width : (n + 1) * width] = back.astype(BF)
        gj[rows, 2 * width :] = grads[:, width:].astype(BF)
    sums[:, :width] = totals[0]
    sums[:, width:] = totals[1]
    for j in range(3):
        cols = slice(j * width, (j + 1) * width)
        scr[:, cols] = mm(n_ref[...], gj[:, cols], 0, 0).astype(BF)
    size = scr.shape[0] // 8
    for rel in range(8):
        rows = pl.ds(pl.multiple_of(sc[2 + rel] * size, 32), size)
        if rel < 4:
            keep[rel] = scr[rows, :]
        else:
            send[rel - 4] = scr[rows, :]


def normed_back_kernel(sc, gj, wq, wk, wv, keep_in, send_in, keep, send, *, own):
    mine = pl.ds(pl.multiple_of(sc[0] * own, own), own)
    other = pl.ds(pl.multiple_of((1 - sc[0]) * own, own), own)
    width = wq.shape[1]
    for rows, before, after in ((mine, keep_in, keep), (other, send_in, send)):
        total = before[...]
        for j, w in enumerate((wq, wk, wv)):
            total = total + mm(gj[rows, j * width : (j + 1) * width], w[...], 1, 1)
        after[...] = total.astype(after.dtype)


def mixer_grad_kernel(sc, mixed, other, g_ref, keep, send, scr):
    width = mixed.shape[1]
    mine = pl.ds(pl.multiple_of(sc[0] * width, 128), width)
    theirs = pl.ds(pl.multiple_of((1 - sc[0]) * width, 128), width)
    scr[mine, :] = mm(mixed[...], g_ref[...], 0, 0).astype(BF)
    scr[theirs, :] = mm(other[...], g_ref[...], 0, 0).astype(BF)
    half = scr.shape[1] // 2
    near = pl.ds(pl.multiple_of(sc[1] * half, 128), half)
    far = pl.ds(pl.multiple_of((1 - sc[1]) * half, 128), half)
    size = scr.shape[0] // 16
    for rel in range(8):
        rows = pl.ds(pl.multiple_of((2 * sc[2 + rel] + sc[0]) * size, 16), size)
        keep[rel] = scr[rows, near]
        send[rel] = scr[rows, far]


def result_kernel(sc, x, mixed, other, mixer_a, mixer_b, keep, received, bias, result, *, own):
    mine = pl.ds(pl.multiple_of(sc[0] * own, own), own)
    total = x[...].astype(F32) + bias[...] + keep[...] + received[...].astype(F32)
    total = total + mm(mixed[mine, :], mixer_a[...]) + mm(other[mine, :], mixer_b[...])
    result[...] = total.astype(BF)


def tokens_grad_kernel(sc, x_ref, g_ref, keep, received, gain, grad, gsum):
    x = x_ref[...].astype(F32)
    gn = keep[...] + received[...].astype(F32)
    center = x - jnp.mean(x, axis=1, keepdims=True)
    rs = lax.rsqrt(jnp.mean(center * center, axis=1, keepdims=True) + EPSILON)
    hat = center * rs
    gsum[...] = jnp.sum(gn * hat, axis=0, keepdims=True)
    u = gain[...] * gn
    back = u - jnp.mean(u, axis=1, keepdims=True) - hat * jnp.mean(u * hat, axis=1, keepdims=True)
    grad[...] = (g_ref[...].astype(F32) + back * rs).astype(BF)


def assemble_kernel(sc, mine, theirs, final):
    width = 384
    for core in range(2):
        first, second = (mine, theirs) if core == 0 else (theirs, mine)
        for col in range(2):

            @pl.when((sc[0] == core) & (sc[1] == col))
            def _():
                a, b = first[...].astype(F32), second[...].astype(F32)
                pieces = []
                if col == 0:
                    for j in range(3):
                        pieces += [a[:, j * width : (j + 1) * width], b[:, j * width : (j + 1) * width]]
                    pieces += [a[:, 3 * width :], b[:, 3 * width :]]
                else:
                    for j in range(7):
                        pieces += [a[:, j * UNIT : (j + 1) * UNIT], b[:, j * UNIT : (j + 1) * UNIT]]
                final[...] = jnp.concatenate(pieces, axis=1)


def per_device(
    tokens,
    image_ids,
    joined_weight,
    hidden_bias,
    mixer_weight,
    dense_weight,
    output_bias,
    norm_gain,
    query_gain,
    key_gain,
    cotangent,
):
    tile_rows, tile_cols, d = tokens.shape
    own = tile_rows * tile_cols
    chip = 2 * own
    ff = dense_weight.shape[0]
    width = d // 2
    row_count, col_count = lax.axis_size("rows"), lax.axis_size("cols")
    fast = (row_count, col_count) == (16, 2)
    row, col = lax.axis_index("rows"), lax.axis_index("cols")
    core, place = row % 2, row // 2

    def pairs(move):
        listed = []
        for i in range(row_count):
            target = move(i // 2, i % 2)
            if target is not None and 0 <= target[0] < row_count // 2:
                listed.append((i, 2 * target[0] + target[1]))
        return listed

    core_swap = pairs(lambda r, c: (r, 1 - c))
    down = pairs(lambda r, c: (r + 1, c))
    up = pairs(lambda r, c: (r - 1, c))
    x_swap = pairs(lambda r, c: (r ^ 1, c))

    def turn(by):
        return pairs(lambda r, c: ((r + 2 * by) % (row_count // 2), c))

    def swap(x):
        return lax.ppermute(x, "rows", core_swap)

    rightward = [(i, i + 1) for i in range(col_count - 1)]
    leftward = [(i + 1, i) for i in range(col_count - 1)]
    col_swap = rightward + leftward

    def exchange_cols(to_left, to_right):
        if col_count == 2:
            got = lax.ppermute(jnp.where(col == 0, to_right, to_left), "cols", col_swap)
            none = jnp.zeros_like(got)
            return jnp.where(col == 1, got, none), jnp.where(col == 0, got, none)
        return (
            lax.ppermute(to_right, "cols", rightward),
            lax.ppermute(to_left, "cols", leftward),
        )

    if fast:
        z, x = place // 2, place % 2
        dests = [2 * ((z + k % 4) % 4) + (x ^ (k // 4)) for k in range(8)]
        side = col
    else:
        dests = [jnp.int32(k) for k in range(8)]
        side = jnp.int32(0)
    sc = jnp.stack([core, side] + dests).astype(jnp.int32)

    x_own = tokens.reshape(own, d)
    g_own = cotangent.reshape(own, d)
    x_other, g_other = swap(x_own), swap(g_own)
    ids_own = image_ids + 1
    ids_other = swap(ids_own)

    gain = norm_gain.reshape(1, d)
    qg = jnp.tile(query_gain.reshape(1, HD), (1, H // 2))
    kg = jnp.tile(key_gain.reshape(1, HD), (1, H // 2))

    def joined_block(k):
        return (joined_weight, (d, width), lambda i, s: (0, 2 * k + s[0]))

    dense_blocks = dense_weight.reshape(ff // (2 * UNIT), 2, UNIT, d)
    dense_block = (dense_blocks, (ff // (2 * UNIT), None, UNIT, d), lambda i, s: (0, s[0], 0, 0))

    half_ff = ff // 2
    wf, bias_f = call(
        weights_kernel,
        sc,
        [
            (joined_weight, (d, 4 * UNIT), lambda i, s: (0, 3 + i)),
            (hidden_bias.reshape(1, ff), (1, 4 * UNIT), lambda i, s: (0, i)),
        ],
        [
            (jax.ShapeDtypeStruct((d, half_ff), BF), (d, 2 * UNIT), lambda i, s: (0, i)),
            (jax.ShapeDtypeStruct((1, half_ff), F32), (1, 2 * UNIT), lambda i, s: (0, i)),
        ],
        grid=(ff // (4 * UNIT),),
    )

    normed, qs, kv, qhat, khat, qrs, krs = call(
        functools.partial(project_kernel, own=own),
        sc,
        [whole(x_own), whole(x_other)]
        + [joined_block(k) for k in range(3)]
        + [whole(gain), whole(qg), whole(kg)],
        [out((chip, d), BF), out((chip, width), BF), out((chip, d), BF)]
        + [out((chip, width), BF)] * 4,
        flops=2 * chip * d * 3 * width,
    )

    edge = RADIUS * tile_cols
    kv_top = lax.ppermute(kv[chip - edge :], "rows", down)
    kv_bottom = lax.ppermute(kv[:edge], "rows", up)
    ids = jnp.where(
        core == 0,
        jnp.concatenate([ids_own, ids_other], axis=0),
        jnp.concatenate([ids_other, ids_own], axis=0),
    )
    ids_top = lax.ppermute(ids[2 * tile_rows - RADIUS :], "rows", down)
    ids_bottom = lax.ppermute(ids[:RADIUS], "rows", up)
    ids_ext = jnp.concatenate([ids_top, ids, ids_bottom], axis=0)
    ext_rows = 2 * tile_rows + 2 * RADIUS
    count = 224
    slots = 576
    ko, to_left, to_right = call(
        extend_kernel,
        sc,
        [whole(kv), whole(kv_top), whole(kv_bottom)],
        [out((ext_rows * tile_cols, d), BF), out((count, d), BF), out((count, d), BF)],
        flops=2 * 10**8,
    )
    from_left, from_right = exchange_cols(to_left, to_right)
    id_left, id_right = exchange_cols(ids_ext[:, :RADIUS], ids_ext[:, tile_cols - RADIUS :])
    ids_all = jnp.concatenate([ids_ext, id_left, id_right], axis=1).astype(F32)
    ids_all = jnp.pad(ids_all, ((0, 80 - ext_rows), (0, 128 - ids_all.shape[1])))
    (mask,) = call(mask_kernel, sc, [whole(ids_all)], [out((chip, KEYS), BF)])
    (kh,) = call(
        slots_kernel, sc, [whole(from_left), whole(from_right)], [out((slots, d), BF)], flops=10**8
    )

    g, gm, gsum = call(
        functools.partial(cotangent_kernel, own=own),
        sc,
        [
            whole(g_own),
            whole(g_other),
            (mixer_weight, (width, d), lambda i, s: (s[0], 0)),
        ],
        [out((chip, d), BF), out((chip, width), BF), out((1, d), F32)],
        flops=2 * chip * d * width,
    )

    block = 256
    hidden, gpre, hsum = call(
        hidden_kernel,
        sc,
        [
            (normed, (block, d), lambda i, s: (i, 0)),
            (g, (block, d), lambda i, s: (i, 0)),
            whole(wf),
            dense_block,
            whole(bias_f),
        ],
        [
            (jax.ShapeDtypeStruct((chip, half_ff), BF), (block, half_ff), lambda i, s: (i, 0)),
            (jax.ShapeDtypeStruct((chip, half_ff), BF), (block, half_ff), lambda i, s: (i, 0)),
            out((1, half_ff), F32),
        ],
        grid=(chip // block,),
        flops=4 * chip * d * half_ff,
    )
    d_keep, d_send = call(
        dense_grad_kernel,
        sc,
        [whole(hidden), whole(g)],
        [out((8, UNIT, width), BF)] * 2,
        scratch=[pltpu.VMEM((half_ff, d), BF)],
        flops=2 * chip * d * half_ff,
    )
    jf_keep, jf_send = call(
        joined_grad_kernel,
        sc,
        [whole(normed), whole(gpre)],
        [out((4, d // 8, half_ff), BF)] * 2,
        scratch=[pltpu.VMEM((d, half_ff), BF)],
        flops=2 * chip * d * half_ff,
    )
    p_keep, p_send, gn_keep, gn_send = call(
        functools.partial(back_kernel, own=own),
        sc,
        [whole(hidden), whole(gpre), whole(wf), dense_block],
        [out((own, d), F32), out((own, d), BF), out((own, d), F32), out((own, d), F32)],
        scratch=[pltpu.VMEM((8, 128), F32)],
        flops=4 * chip * d * half_ff,
    )
    p_received = swap(p_send)

    def lane_block(x, shift=0):
        return (x, (x.shape[0], 128), lambda i, s: (0, i + shift))

    def lane_out(rows, lanes, dtype):
        return (jax.ShapeDtypeStruct((rows, lanes), dtype), (rows, 128), lambda i, s: (0, i))

    ko_rows = ext_rows * tile_cols
    mixed, dq, dko_k, dko_v, dkh_k, dkh_v = call(
        attention_kernel,
        sc,
        [
            lane_block(qs),
            lane_block(gm),
            lane_block(ko),
            lane_block(ko, 3),
            lane_block(kh),
            lane_block(kh, 3),
            whole(mask),
        ],
        [
            lane_out(chip, width, BF),
            lane_out(chip, width, F32),
            lane_out(ko_rows, width, F32),
            lane_out(ko_rows, width, F32),
            lane_out(slots, width, F32),
            lane_out(slots, width, F32),
        ],
        grid=(3,),
        flops=10**10,
    )
    dko = jnp.concatenate([dko_k, dko_v], axis=1)
    dkh = jnp.concatenate([dkh_k, dkh_v], axis=1)
    mixed_other = swap(mixed)

    back_left, back_right = call(
        unslot_kernel, sc, [whole(dkh)], [out((count, d), BF)] * 2, flops=10**8
    )
    got_left, got_right = exchange_cols(back_left, back_right)
    to_up, to_down, dkv = call(
        fold_kernel,
        sc,
        [whole(dko), whole(got_left), whole(got_right)],
        [out((edge, d), BF), out((edge, d), BF), out((chip, d), F32)],
        flops=2 * 10**8,
    )
    from_down = lax.ppermute(to_up, "rows", up)
    from_up = lax.ppermute(to_down, "rows", down)

    m_keep, m_send = call(
        mixer_grad_kernel,
        sc,
        [whole(mixed), whole(mixed_other), whole(g)],
        [out((8, d // 16, width), BF)] * 2,
        scratch=[pltpu.VMEM((d, d), BF)],
        flops=2 * chip * d * d,
    )
    (result,) = call(
        functools.partial(result_kernel, own=own),
        sc,
        [
            whole(x_own),
            whole(mixed),
            whole(mixed_other),
            (mixer_weight, (width, d), lambda i, s: (s[0], 0)),
            (mixer_weight, (width, d), lambda i, s: (1 - s[0], 0)),
            whole(p_keep),
            whole(p_received),
            whole(output_bias.reshape(1, d)),
        ],
        [out((own, d), BF)],
        flops=2 * own * d * d,
    )

    gj, jq_keep, jq_send, qksum = call(
        qkv_back_kernel,
        sc,
        [whole(v) for v in (dq, dkv, from_up, from_down, qhat, khat, qrs, krs, qg, kg, normed)],
        [out((chip, 3 * width), BF)]
        + [out((4, d // 8, 3 * width), BF)] * 2
        + [out((1, 2 * width), F32)],
        scratch=[pltpu.VMEM((d, 3 * width), BF)],
        flops=2 * chip * d * 3 * width,
    )
    gn_keep, gn_send = call(
        functools.partial(normed_back_kernel, own=own),
        sc,
        [whole(gj)] + [joined_block(k) for k in range(3)] + [whole(gn_keep), whole(gn_send)],
        [out((own, d), F32), out((own, d), BF)],
        flops=2 * chip * d * 3 * width,
    )
    gn_received = swap(gn_send)
    tokens_grad, normsum = call(
        tokens_grad_kernel,
        sc,
        [whole(x_own), whole(g_own), whole(gn_keep), whole(gn_received), whole(gain)],
        [out((own, d), BF), out((1, d), F32)],
    )

    spread = jnp.zeros((ff // (2 * UNIT), 2, UNIT), F32)
    hpart = hsum.reshape(ff // (2 * UNIT), 1, UNIT)
    is_core = (jnp.arange(2) == core).reshape(1, 2, 1)
    hpart = jnp.where(is_core, hpart, spread).reshape(ff)
    qk_heads = qksum.reshape(2, H // 2, HD).sum(axis=1).reshape(2 * HD)
    small = jnp.concatenate([hpart, gsum.reshape(d), normsum.reshape(d), qk_heads])

    def add(a, b):
        return (a.astype(F32) + b.astype(F32)).astype(BF)

    if fast:
        small = jnp.pad(small, (0, 5120 - small.shape[0])).reshape(40, 128)
        small = small + swap(small)
        small = small + lax.ppermute(small, "rows", x_swap)
        small = small + lax.ppermute(small, "cols", col_swap)
        small = small + lax.ppermute(small, "rows", pairs(lambda r, c: (r ^ 2, c)))
        small = small + lax.ppermute(small, "rows", pairs(lambda r, c: (r ^ 4, c)))
        small = small.reshape(-1)

        def reduce_rows(keep, send):
            kept = add(keep, lax.ppermute(send, "rows", x_swap))
            total = kept[0].astype(F32)
            for by in range(1, 4):
                total = total + lax.ppermute(kept[by], "rows", turn(by)).astype(F32)
            return total

        def reduce_cols(keep, send):
            kept = add(keep, lax.ppermute(send, "cols", col_swap))
            return kept[:4], kept[4:]

        dense_sum = reduce_rows(*reduce_cols(d_keep, d_send))
        jf = reduce_rows(jf_keep, jf_send)
        mixer_sum = reduce_rows(*reduce_cols(m_keep, m_send))
        jq = reduce_rows(jq_keep, jq_send)
        joined = jnp.concatenate([jq, jf], axis=1).astype(BF)
        half = joined.shape[1] // 2
        first, second = joined[:, :half], joined[:, half:]
        got = lax.ppermute(jnp.where(col == 0, second, first), "cols", col_swap)
        kept = add(jnp.where(col == 0, first, second), got)
        part = d // 16
        mine = jnp.where(core == 0, kept[:part], kept[part:])
        theirs = swap(jnp.where(core == 0, kept[part:], kept[:part]))
        (joined_sum,) = call(
            assemble_kernel,
            sc,
            [whole(mine), whole(theirs)],
            [out((part, 2 * half), F32)],
        )
    else:
        small = lax.psum(small, ("rows", "cols"))

        def spread_core(x, axis):
            x = jnp.expand_dims(x, axis)
            is_mine = jnp.arange(2).reshape([2 if i == axis else 1 for i in range(x.ndim)]) == core
            return jnp.where(is_mine, x, jnp.zeros_like(x))

        def reduce(x):
            x = lax.psum_scatter(x, "rows", scatter_dimension=0, tiled=True)
            return lax.psum_scatter(x, "cols", scatter_dimension=1, tiled=True).astype(F32)

        dense_sum = reduce(spread_core(jnp.concatenate([d_keep, d_send], axis=2), 1).reshape(ff, d))
        mixer_sum = reduce(spread_core(jnp.concatenate([m_keep, m_send], axis=2), 1).reshape(d, d))
        jq = jnp.concatenate([jq_keep, jq_send], axis=0).reshape(d, 3, width)
        jf = jnp.concatenate([jf_keep, jf_send], axis=0).reshape(d, ff // (2 * UNIT), UNIT)
        joined = [spread_core(jq, 2).reshape(d, 3 * d), spread_core(jf, 2).reshape(d, ff)]
        joined_sum = reduce(jnp.concatenate(joined, axis=1))

    hidden_sum = small[:ff]
    output_sum = small[ff : ff + d]
    gain_sum = small[ff + d : ff + 2 * d]
    query_sum = small[ff + 2 * d : ff + 2 * d + HD]
    key_sum = small[ff + 2 * d + HD : ff + 2 * d + 2 * HD]
    shape = (tile_rows, tile_cols, d)
    return (
        result.reshape(shape),
        tokens_grad.reshape(shape),
        joined_sum,
        hidden_sum,
        mixer_sum,
        dense_sum,
        output_sum,
        gain_sum,
        query_sum,
        key_sum,
    )


def solution(mesh):
    tiles, everywhere, blocks = P("rows", "cols", None), P(), P("rows", "cols")
    return jax.shard_map(
        per_device,
        mesh=mesh,
        in_specs=(tiles, blocks) + (everywhere,) * 8 + (tiles,),
        out_specs=(tiles, tiles, blocks, P(), blocks, blocks, P(), P(), P(), P()),
        check_vma=False,
    )
```

```python
import functools

import jax
import jax.numpy as jnp
from jax import lax
from jax.experimental import pallas as pl
from jax.experimental.pallas import tpu as pltpu
from jax.sharding import PartitionSpec as P

H = 12
HD = 64
RADIUS = 3
EPSILON = 1e-06
BF = jnp.bfloat16
F32 = jnp.float32
MIB = 1024 * 1024

UNIT = 192
STRIP = 4
KEYS = 256
HALO_SLOTS = 8


def mm(a, b, ca=1, cb=0):
    return lax.dot_general(a, b, (((ca,), (cb,)), ((), ())), preferred_element_type=F32)


def call(kernel, scalars, ins, outs, scratch=(), vmem=12, after=(), grid=1, work=5 * 10**9):
    ins = [entry if isinstance(entry, tuple) else (entry, None, None) for entry in ins]

    def spec(_, block, index):
        if block is None:
            return pl.BlockSpec(memory_space=pltpu.VMEM)
        return pl.BlockSpec(block, index)

    def placed(x, block, _):
        return x if block is None else pltpu.with_memory_space_constraint(x, pltpu.HBM)

    def run(sc, *refs):
        kernel(sc, *refs[: len(ins)], *refs[len(ins) + len(after) :])

    step = pl.pallas_call(
        run,
        name=getattr(kernel, "func", kernel).__name__,
        grid_spec=pltpu.PrefetchScalarGridSpec(
            num_scalar_prefetch=1,
            grid=(grid,),
            in_specs=[spec(*entry) for entry in ins]
            + [pl.BlockSpec(memory_space=pl.ANY)] * len(after),
            out_specs=[pl.BlockSpec(memory_space=pltpu.VMEM)] * len(outs),
            scratch_shapes=list(scratch),
        ),
        out_shape=list(outs),
        compiler_params=pltpu.CompilerParams(vmem_limit_bytes=vmem * MIB),
        cost_estimate=pl.CostEstimate(flops=work, bytes_accessed=0, transcendentals=0),
    )
    return list(step(scalars, *[placed(*entry) for entry in ins], *after))


def out(shape, dtype=BF):
    return jax.ShapeDtypeStruct(shape, dtype)


def aligned(start, size, unit):
    return pl.ds(pl.multiple_of(start, unit), size)


def head_means(width):
    row = lax.broadcasted_iota(jnp.int32, (width, width), 0)
    col = lax.broadcasted_iota(jnp.int32, (width, width), 1)
    return jnp.where(row // HD == col // HD, 1.0 / HD, 0.0).astype(BF)


def per_head(x, means):
    width = means.shape[0]
    parts = [mm(x[:, j : j + width].astype(BF), means) for j in range(0, x.shape[1], width)]
    return jnp.concatenate(parts, axis=1)


CORE, SIDE, ON_LEFT, ODD, DEST = 0, 1, 2, 3, 4


def weights_kernel(sc, joined, qkv, dense, bias, wf, wqkv, wd, b_out):
    i = pl.program_id(0)
    size = 2 * UNIT
    cols = aligned(i * size, size, 128)
    for core in range(2):

        @pl.when(sc[CORE] == core)
        def _():
            lo, hi = core * UNIT, (2 + core) * UNIT
            w = joined[...]
            wf[:, cols] = jnp.concatenate([w[:, lo : lo + UNIT], w[:, hi : hi + UNIT]], axis=1)
            b = bias[...]
            b_out[:, cols] = jnp.concatenate([b[:, lo : lo + UNIT], b[:, hi : hi + UNIT]], axis=1)

    @pl.when(i < 3)
    def _():
        wqkv[:, cols] = qkv[...]

    wd[cols, :] = dense[...].reshape(size, wd.shape[1])


def split_ids(ids):
    high = jnp.floor(ids * (1.0 / 256))
    return [(ids - 256.0 * high).astype(BF), high.astype(BF)]


def joined_ids(low, high):
    return low.astype(F32) + 256.0 * high.astype(F32)


def row_messages(sc, top, bottom):
    odd = sc[ODD] == 1
    return jnp.where(odd, top, bottom), jnp.where(odd, bottom, top)


def project_kernel(
    sc, xo, xt, io, it, wqkv, gain, qg, kg, normed, qs, kv, hats, roots, ids, row_a, row_b
):
    means = head_means(4 * HD)
    own = xo.shape[0]
    width = qs.shape[1]
    heads = width // HD
    gains = jnp.concatenate([qg[...]] * heads + [kg[...]] * heads, axis=1)
    block = 256
    for half, ref in enumerate((xo, xt)):
        start = (sc[CORE] if half == 0 else 1 - sc[CORE]) * own
        for i in range(own // block):
            x = ref[i * block : (i + 1) * block, :].astype(F32)
            rows = aligned(start + i * block, block, block)
            center = x - jnp.mean(x, axis=1, keepdims=True)
            spread = jnp.mean(center * center, axis=1, keepdims=True)
            n = (center * lax.rsqrt(spread + EPSILON) * gain[...]).astype(BF)
            normed[rows, :] = n
            part = mm(n, wqkv[:, : 2 * width])
            center = part - per_head(part, means)
            root = lax.rsqrt(per_head(center * center, means) + EPSILON)
            hat = center * root
            hats[rows, :] = hat.astype(BF)
            roots[rows, :] = root.astype(BF)
            low = (hat * gains).astype(BF)
            qs[rows, :] = low[:, :width] * jnp.asarray(HD**-0.5, BF)
            values = mm(n, wqkv[:, 2 * width :]).astype(BF)
            for p in range(width // 128):
                kv[rows, 256 * p : 256 * p + 128] = low[:, width + 128 * p : width + 128 * p + 128]
                kv[rows, 256 * p + 128 : 256 * p + 256] = values[:, 128 * p : 128 * p + 128]
    edge, chip = RADIUS * io.shape[1], kv.shape[0]
    row_a[:edge, :], row_b[:edge, :] = row_messages(sc, kv[:edge, :], kv[chip - edge :, :])
    size = io.shape[0]
    for half, ref in enumerate((io, it)):
        start = (sc[CORE] if half == 0 else 1 - sc[CORE]) * size
        value = ref[...].astype(F32) + 1.0
        zeros = jnp.zeros((size, ids.shape[1] - value.shape[1]), F32)
        ids[aligned(start, size, size), :] = jnp.concatenate([value, zeros], axis=1)
    zeros = jnp.zeros((16 - 8, 128), BF)
    id_a, id_b = row_messages(sc, ids[:8, :], ids[2 * size - 8 :, :])
    for ref, values in ((row_a, id_a), (row_b, id_b)):
        ref[edge:, :] = jnp.zeros((16, ref.shape[1]), BF)
        for j, piece in enumerate(split_ids(values)):
            ref[edge:, 128 * j : 128 * j + 128] = jnp.concatenate([piece, zeros], axis=0)


def cotangent_kernel(sc, go, gt, mixer, g_out, gm, gsum):
    own = go.shape[0]
    for half, ref in enumerate((go, gt)):
        start = (sc[CORE] if half == 0 else 1 - sc[CORE]) * own
        rows = aligned(start, own, own)
        g = ref[...]
        g_out[rows, :] = g
        gm[rows, :] = mm(g, mixer[...], 1, 1).astype(BF)
    gsum[...] = jnp.sum(go[...].astype(F32), axis=0, keepdims=True)


def hidden_kernel(sc, n_ref, g_ref, wf, wd, bias, hidden, gpre, hsum):
    wide = wf.shape[1]
    dense = wd[...]
    block = 256
    total = jnp.zeros((1, wide), F32)
    for i in range(n_ref.shape[0] // block):
        rows = slice(i * block, (i + 1) * block)
        pre = mm(n_ref[rows, :], wf[...]) + bias[...]
        gd = mm(g_ref[rows, :], dense, 1, 1)
        a, b = 0.7978845608, 0.044715
        sq = pre * pre
        t = jnp.tanh(a * pre * (1.0 + b * sq))
        half = 0.5 * (1.0 + t)
        hidden[rows, :] = (pre * half).astype(BF)
        slope = half + (0.5 * a) * pre * (1.0 - t * t) * (1.0 + 3.0 * b * sq)
        gp = gd * slope
        gpre[rows, :] = gp.astype(BF)
        total = total + jnp.sum(gp, axis=0, keepdims=True)
    hsum[...] = total


def dense_grad_kernel(sc, h_ref, g_ref, near_keep, near_send, far_keep, far_send, scr):
    wide, d = scr.shape
    step = wide // 3
    half = d // 2
    for j in range(3):
        cols = slice(j * step, (j + 1) * step)
        scr[cols, :] = mm(h_ref[:, cols], g_ref[...], 0, 0).astype(BF)
    mine = aligned(sc[SIDE] * half, half, 128)
    other = aligned((1 - sc[SIDE]) * half, half, 128)
    for rel in range(8):
        rows = aligned(sc[DEST + rel] * UNIT, UNIT, 64)
        keep, send = (near_keep, near_send) if rel < 4 else (far_keep, far_send)
        keep[rel % 4] = scr[rows, mine]
        send[rel % 4] = scr[rows, other]


def scatter_rows(sc, scr, keeps, send_a, send_b):
    size = scr.shape[0] // 8
    for rel in range(8):
        rows = aligned(sc[DEST + rel] * size, size, 32)
        if rel < 4:
            keeps[rel][...] = scr[rows, :]
        elif rel in (5, 6):
            send_a[rel - 5] = scr[rows, :]
        else:
            send_b[0 if rel == 7 else 1] = scr[rows, :]


def joined_grad_kernel(sc, n_ref, gp_ref, k0, k1, k2, k3, send_a, send_b, scr):
    step = scr.shape[1] // 3
    for j in range(3):
        cols = slice(j * step, (j + 1) * step)
        scr[:, cols] = mm(n_ref[...], gp_ref[:, cols], 0, 0).astype(BF)
    scatter_rows(sc, scr, (k0, k1, k2, k3), send_a, send_b)


def back_output_kernel(sc, h_ref, wd, keep, send):
    own = keep.shape[0]
    dense = wd[...]
    keep[...] = mm(h_ref[aligned(sc[CORE] * own, own, own), :], dense).astype(BF)
    send[...] = mm(h_ref[aligned((1 - sc[CORE]) * own, own, own), :], dense).astype(BF)


def back_normed_kernel(sc, gp_ref, wf, keep, send):
    own = keep.shape[0]
    mine, theirs = gp_ref[aligned(sc[CORE] * own, own, own), :], gp_ref[aligned((1 - sc[CORE]) * own, own, own), :]
    keep[...] = mm(mine, wf[...], 1, 1).astype(BF)
    send[...] = mm(theirs, wf[...], 1, 1).astype(BF)


def edge_picks(rows, first, count):
    msg = lax.broadcasted_iota(jnp.int32, (count, rows), 0)
    tok = lax.broadcasted_iota(jnp.int32, (count, rows), 1)
    return jnp.where(tok == msg // 3 * 16 + first + msg % 3, 1.0, 0.0).astype(BF)


def slot_places(count, slots, first):
    slot = lax.broadcasted_iota(jnp.int32, (slots, count), 0)
    msg = lax.broadcasted_iota(jnp.int32, (slots, count), 1)
    return jnp.where(slot == msg // 3 * HALO_SLOTS + first + msg % 3, 1.0, 0.0).astype(BF)


def extend_kernel(sc, *refs, edges):
    kv, row_a, row_b, ids, ko, ids_ext, *msgs = refs
    edge, own = row_a.shape[0] - 16, kv.shape[0]
    top, bottom = row_messages(sc, row_a[...], row_b[...])
    ko[:edge, :] = top[:edge]
    ko[edge : edge + own, :] = kv[...]
    ko[edge + own :, :] = bottom[:edge]
    size = ids.shape[0]
    ids_ext[...] = jnp.zeros_like(ids_ext)
    ids_ext[:RADIUS, :] = joined_ids(top[edge:, :128], top[edge:, 128:256])[8 - RADIUS : 8]
    ids_ext[RADIUS : RADIUS + size, :] = ids[...]
    ids_ext[RADIUS + size : 2 * RADIUS + size, :] = joined_ids(
        bottom[edge:, :128], bottom[edge:, 128:256]
    )[:RADIUS]
    count = msgs[0].shape[0] - 16
    for msg, first in zip(msgs, edges):
        left, right = ids_ext[...], pltpu.roll(ids_ext[...], 128 - 13, 1)
        if first is None:
            shifted = jnp.where(sc[ON_LEFT] == 1, right, left)
            first = 13 * sc[ON_LEFT]
        else:
            shifted = right if first else left
        msg[:count, :] = mm(edge_picks(ko.shape[0], first, count), ko[...]).astype(BF)
        msg[count:, :] = jnp.zeros((16, msg.shape[1]), BF)
        turned = jnp.transpose(shifted)[:8]
        msg[count:, : turned.shape[1]] = jnp.concatenate(split_ids(turned), axis=0)


def slots_kernel(sc, *refs, places):
    moves = len(places)
    msgs, ids_ext, kh, mask, ids = refs[:moves], *refs[moves:]
    count = msgs[0].shape[0] - 16
    total = 0.0
    all_ids = ids_ext[...]
    for msg, first in zip(msgs, places):
        pieces = msg[count:, :128]
        turned = jnp.transpose(joined_ids(pieces[:8], pieces[8:]))[: ids.shape[0]]
        turned = jnp.concatenate(
            [turned[:, :RADIUS], jnp.zeros((ids.shape[0], 128 - RADIUS), F32)], axis=1
        )
        left, right = pltpu.roll(turned, 16, 1), pltpu.roll(turned, 19, 1)
        if first is None:
            all_ids = all_ids + jnp.where(sc[ON_LEFT] == 1, right, left)
            first = 3 * sc[ON_LEFT]
        else:
            all_ids = all_ids + (right if first else left)
        total = total + mm(slot_places(count, kh.shape[0], first), msg[:count, :])
    kh[...] = total.astype(BF)
    ids[...] = all_ids
    write_mask(ids, mask)


def write_mask(ids, bias):
    lane = lax.broadcasted_iota(jnp.int32, (STRIP * 16, KEYS), 1)
    query = lax.broadcasted_iota(jnp.int32, (STRIP * 16, KEYS), 0)
    inner = lane < 160
    halo = lane - 160
    slot = halo % HALO_SLOTS
    key_row = jnp.where(inner, lane // 16, halo // HALO_SLOTS)
    key_col = jnp.where(inner, lane % 16, jnp.where(slot < 3, slot - 3, slot + 13))
    row_gap = key_row - query // 16
    col_gap = key_col - query % 16
    reach = (
        (row_gap >= 0)
        & (row_gap <= 2 * RADIUS)
        & (col_gap >= -RADIUS)
        & (col_gap <= RADIUS)
        & (inner | (slot < 6))
    )
    itself = inner & (row_gap == RADIUS) & (col_gap == 0)
    lane16 = lax.broadcasted_iota(jnp.int32, (16, KEYS), 1)
    window = jnp.zeros((16, KEYS), F32)
    for i in range(STRIP + 2 * RADIUS):
        part = jnp.concatenate(
            [ids[pl.ds(i, 16, stride=STRIP), :], jnp.zeros((16, KEYS - 128), F32)], axis=1
        )
        own = jnp.where(lane16 < 16, part, 0.0)
        side = jnp.where(lane16 >= 16, part, 0.0)
        if i > 0:
            own = pltpu.roll(own, 16 * i, 1)
        side = pltpu.roll(side, 144 + HALO_SLOTS * i, 1)
        window = window + own + side
    for s in range(16):
        row = jnp.broadcast_to(window[s : s + 1, :], (STRIP * 16, KEYS))
        mine = jnp.sum(jnp.where(itself, row, 0.0), axis=1, keepdims=True)
        bias[s * 64 : (s + 1) * 64, :] = jnp.where(reach & (row == mine), 0.0, -1e30).astype(BF)


def attention_kernel(sc, q_ref, gm_ref, ko, kh, bias, mixed, dq, dko_out, dkh_out, dko, dkh, *, pair):
    dko[...] = jnp.zeros_like(dko)
    dkh[...] = jnp.zeros_like(dkh)
    lane = lax.broadcasted_iota(jnp.int32, (64, 128), 1)
    low = lane < HD
    zero = jnp.zeros((64, 128), BF)
    lanes = slice(128 * pair, 128 * pair + 128)
    k_lanes = slice(256 * pair, 256 * pair + 128)
    v_lanes = slice(256 * pair + 128, 256 * pair + 256)

    def both(x):
        return jnp.concatenate([jnp.where(low, x, zero), jnp.where(low, zero, x)], axis=0)

    for s in range(16):
        rows = slice(s * 64, (s + 1) * 64)
        inner = slice(s * 64, s * 64 + 160)
        side = slice(s * 32, s * 32 + 96)
        q2, gm2 = both(q_ref[rows, lanes]), both(gm_ref[rows, lanes])
        k = jnp.concatenate([ko[inner, k_lanes], kh[side, k_lanes]], axis=0)
        v = jnp.concatenate([ko[inner, v_lanes], kh[side, v_lanes]], axis=0)
        b = bias[rows, :].astype(F32)
        weights = jnp.exp(mm(q2, k, 1, 1) + jnp.concatenate([b, b], axis=0))
        probs = weights * (1.0 / jnp.sum(weights, axis=1, keepdims=True))
        probs_low = probs.astype(BF)
        o = mm(probs_low, v)
        mixed[rows, :] = jnp.where(low, o[:64], o[64:]).astype(BF)
        dp = mm(gm2, v, 1, 1)
        balance = jnp.sum(probs * dp, axis=1, keepdims=True)
        ds = (probs * (dp - balance)).astype(BF)
        d = mm(ds, k)
        dq[rows, :] = (jnp.where(low, d[:64], d[64:]) * (HD**-0.5)).astype(BF)
        dk = mm(ds, q2, 0, 0)
        dv = mm(probs_low, gm2, 0, 0)
        dko[inner, :128] += dk[:160]
        dkh[side, :128] += dk[160:]
        dko[inner, 128:] += dv[:160]
        dkh[side, 128:] += dv[160:]
    dko_out[...] = dko[...].astype(BF)
    dkh_out[...] = dkh[...].astype(BF)


def unslot_kernel(sc, *refs, parts, places):
    dkh, msgs = refs[:parts], refs[parts:]
    for msg, first in zip(msgs, places):
        first = 3 * sc[ON_LEFT] if first is None else first
        places_of = slot_places(msg.shape[0], dkh[0].shape[0], first)
        for p, ref in enumerate(dkh):
            msg[:, 256 * p : 256 * p + 256] = mm(places_of, ref[...], 0, 0).astype(BF)


def fold_kernel(sc, *refs, parts, counts, edges):
    dko, refs = refs[:parts], refs[parts:]
    groups, refs = refs[: len(counts) * len(edges)], refs[len(counts) * len(edges) :]
    row_a, row_b, center = refs
    rows = dko[0].shape[0]
    edge = row_a.shape[0]
    count = groups[0].shape[0]
    picks = []
    for first in edges:
        picks.append(edge_picks(rows, 13 * sc[ON_LEFT] if first is None else first, count))
    p = 0
    for n, size in enumerate(counts):
        for j in range(size):
            total = dko[p][...].astype(F32)
            for e, pick in enumerate(picks):
                msg = groups[n * len(edges) + e]
                total = total + mm(pick, msg[:, 256 * j : 256 * j + 256], 0, 0)
            lanes = slice(256 * p, 256 * p + 256)
            low = total.astype(BF)
            row_a[:, lanes], row_b[:, lanes] = row_messages(sc, low[:edge], low[rows - edge :])
            center[:, lanes] = low[edge : rows - edge]
            p += 1


def norm_back(grad, hat, root, gains, means):
    u = gains * grad
    back = u - per_head(u, means) - hat * per_head(u * hat, means)
    return (back * root).astype(BF), jnp.sum(grad * hat, axis=0, keepdims=True)


def q_back_kernel(sc, dq0, dq1, dq2, hats, roots, qg, n_ref, gj, sums, *blocks):
    *blocks, scr = blocks
    means = head_means(2 * HD)
    width = gj.shape[1]
    gains = jnp.concatenate([qg[...]] * (width // HD), axis=1)
    block = 256
    totals = jnp.zeros((1, width), F32)
    for i in range(gj.shape[0] // block):
        rows = slice(i * block, (i + 1) * block)
        grad = jnp.concatenate([dq0[rows, :], dq1[rows, :], dq2[rows, :]], axis=1).astype(F32)
        hat, root = hats[rows, :width].astype(F32), roots[rows, :width].astype(F32)
        gj[rows, :], total = norm_back(grad, hat, root, gains, means)
        totals = totals + total
    sums[...] = totals
    scr[...] = mm(n_ref[...], gj[...], 0, 0).astype(BF)
    size = scr.shape[0] // 8
    for rel in range(8):
        blocks[rel // 4][rel % 4] = scr[aligned(sc[DEST + rel] * size, size, 32), :]


def kv_back_kernel(sc, dkv, row_a, row_b, hats, roots, kg, n_ref, gj, sums, k0, k1, k2, k3, send_a, send_b, scr):
    means = head_means(2 * HD)
    tokens = dkv.shape[0]
    edge = row_a.shape[0]
    width = hats.shape[1] // 2
    gains = jnp.concatenate([kg[...]] * (width // HD), axis=1)
    block = 256
    top, bottom = row_messages(sc, row_a[...].astype(F32), row_b[...].astype(F32))
    totals = jnp.zeros((1, width), F32)
    for i in range(tokens // block):
        rows = slice(i * block, (i + 1) * block)
        grads = dkv[rows, :].astype(F32)
        if i == 0:
            grads = jnp.concatenate([grads[:edge] + top, grads[edge:]], axis=0)
        if i == tokens // block - 1:
            grads = jnp.concatenate([grads[:-edge], grads[-edge:] + bottom], axis=0)
        grad = jnp.concatenate(
            [grads[:, 256 * p : 256 * p + 128] for p in range(width // 128)], axis=1
        )
        hat, root = hats[rows, width:].astype(F32), roots[rows, width:].astype(F32)
        gj[rows, :width], total = norm_back(grad, hat, root, gains, means)
        totals = totals + total
        for p in range(width // 128):
            gj[rows, width + 128 * p : width + 128 * p + 128] = grads[
                :, 256 * p + 128 : 256 * p + 256
            ].astype(BF)
    sums[...] = totals
    for j in range(2):
        cols = slice(j * width, (j + 1) * width)
        scr[:, cols] = mm(n_ref[...], gj[:, cols], 0, 0).astype(BF)
    scatter_rows(sc, scr, (k0, k1, k2, k3), send_a, send_b)


def normed_back_kernel(sc, gq, gkv, wqkv, keep_in, send_in, keep, send):
    own = keep.shape[0]
    width = gq.shape[1]
    for start, before, after in ((sc[CORE], keep_in, keep), (1 - sc[CORE], send_in, send)):
        rows = aligned(start * own, own, own)
        total = before[...].astype(F32) + mm(gq[rows, :], wqkv[:, :width], 1, 1)
        total = total + mm(gkv[rows, :], wqkv[:, width:], 1, 1)
        after[...] = total.astype(after.dtype)


def mixer_grad_kernel(sc, m0, m1, m2, o0, o1, o2, g_ref, near_keep, far_keep, send, scr):
    width = 3 * m0.shape[1]
    for start, refs in ((sc[CORE], (m0, m1, m2)), (1 - sc[CORE], (o0, o1, o2))):
        values = jnp.concatenate([ref[...] for ref in refs], axis=1)
        scr[aligned(start * width, width, 128), :] = mm(values, g_ref[...], 0, 0).astype(BF)
    half = scr.shape[1] // 2
    mine = aligned(sc[SIDE] * half, half, 128)
    theirs = aligned((1 - sc[SIDE]) * half, half, 128)
    size = scr.shape[0] // 16
    for rel in range(8):
        rows = aligned((2 * sc[DEST + rel] + sc[CORE]) * size, size, 16)
        (near_keep if rel < 4 else far_keep)[rel % 4] = scr[rows, mine]
        send[rel] = scr[rows, theirs]


def result_kernel(sc, x, m0, m1, m2, o0, o1, o2, mixer_a, mixer_b, keep, received, bias, result):
    own = x.shape[0]
    mine = aligned(sc[CORE] * own, own, own)
    total = x[...].astype(F32) + bias[...] + keep[...].astype(F32) + received[...].astype(F32)
    for refs, mixer in (((m0, m1, m2), mixer_a), ((o0, o1, o2), mixer_b)):
        total = total + mm(jnp.concatenate([ref[mine, :] for ref in refs], axis=1), mixer[...])
    result[...] = total.astype(BF)


def tokens_grad_kernel(sc, x_ref, g_ref, keep, received, gain, grad, gsum):
    x = x_ref[...].astype(F32)
    gn = keep[...].astype(F32) + received[...].astype(F32)
    center = x - jnp.mean(x, axis=1, keepdims=True)
    rs = lax.rsqrt(jnp.mean(center * center, axis=1, keepdims=True) + EPSILON)
    hat = center * rs
    gsum[...] = jnp.sum(gn * hat, axis=0, keepdims=True)
    u = gain[...] * gn
    back = u - jnp.mean(u, axis=1, keepdims=True) - hat * jnp.mean(u * hat, axis=1, keepdims=True)
    grad[...] = (g_ref[...].astype(F32) + back * rs).astype(BF)


def wide_sum(terms):
    total = terms[0].astype(F32)
    for term in terms[1:]:
        total = total + term.astype(F32)
    return total


def sum_kernel(sc, *refs, plan):
    count = len(refs) - len(plan)
    for target, groups in zip(refs[count:], plan):
        values = []
        for terms in groups:
            values.append(wide_sum([refs[n][...] if k is None else refs[n][k] for n, k in terms]))
        target[...] = jnp.concatenate(values, axis=-2).astype(target.dtype)


def joined_sides_kernel(sc, *refs):
    q, kv, f, keep, send = refs[0], refs[1:5], refs[5:9], refs[9], refs[10]
    total = jnp.concatenate(
        [q[...], wide_sum([r[...] for r in kv]), wide_sum([r[...] for r in f])], axis=1
    )
    half = total.shape[1] // 2
    parts = (total[:, :half], total[:, half:])
    for side in range(2):

        @pl.when(sc[SIDE] == side)
        def _():
            keep[...] = parts[side]
            send[...] = parts[1 - side].astype(BF)


def joined_cores_kernel(sc, kept, received, mine, send, scr):
    scr[...] = kept[...] + received[...].astype(F32)
    size = mine.shape[0]
    mine[...] = scr[aligned(sc[CORE] * size, size, 8), :]
    send[...] = scr[aligned((1 - sc[CORE]) * size, size, 8), :].astype(BF)


def assemble_kernel(sc, mine, theirs, final):
    width = 384
    for core in range(2):
        first, second = (mine, theirs) if core == 0 else (theirs, mine)
        for side in range(2):

            @pl.when((sc[CORE] == core) & (sc[SIDE] == side))
            def _():
                a, b = first[...].astype(F32), second[...].astype(F32)
                size, count = (width, 3) if side == 0 else (UNIT, 7)
                cuts = [slice(j * size, (j + 1) * size) for j in range(count)]
                if side == 0:
                    cuts.append(slice(3 * width, a.shape[1]))
                final[...] = jnp.concatenate([x[:, cut] for cut in cuts for x in (a, b)], axis=1)


def pack_kernel(sc, hsum, gsum, nsum, qsum, ksum, small):
    small[...] = jnp.zeros_like(small)
    row = 2 * hsum.shape[1] // 128
    for ref in (gsum, nsum, qsum, ksum):
        for j in range(ref.shape[1] // 128):
            small[row : row + 1, :] = ref[:, 128 * j : 128 * j + 128]
            row += 1
    count = hsum.shape[1] // 128
    for j in range(count):
        small[pl.ds(sc[CORE] * count + j, 1), :] = hsum[:, 128 * j : 128 * j + 128]


def unpack_kernel(sc, small, hidden, output, norm, query, key):
    count = hidden.shape[1] // 256
    cores = []
    for core in range(2):
        rows = [small[core * count + j : core * count + j + 1, :] for j in range(count)]
        cores.append(jnp.concatenate(rows, axis=1))
    blocks = []
    for j in range(cores[0].shape[1] // UNIT):
        blocks += [x[:, j * UNIT : (j + 1) * UNIT] for x in cores]
    hidden[...] = jnp.concatenate(blocks, axis=1)
    row = 2 * count
    for ref in (output, norm):
        for j in range(ref.shape[1] // 128):
            ref[:, 128 * j : 128 * j + 128] = small[row : row + 1, :]
            row += 1
    for ref in (query, key):
        total = jnp.sum(small[row : row + 3, :], axis=0, keepdims=True)
        ref[...] = total[:, :HD] + total[:, HD:]
        row += 3


def per_device(
    tokens,
    image_ids,
    joined_weight,
    hidden_bias,
    mixer_weight,
    dense_weight,
    output_bias,
    norm_gain,
    query_gain,
    key_gain,
    cotangent,
):
    tile_rows, tile_cols, d = tokens.shape
    own = tile_rows * tile_cols
    chip = 2 * own
    ff = dense_weight.shape[0]
    half_ff = ff // 2
    width = d // 2
    row_count, col_count = lax.axis_size("rows"), lax.axis_size("cols")
    fast = (row_count, col_count) == (16, 2)
    row, col = lax.axis_index("rows"), lax.axis_index("cols")
    core, place = row % 2, row // 2

    def pairs(move):
        listed = []
        for i in range(row_count):
            target = move(i // 2, i % 2)
            if 0 <= target[0] < row_count // 2:
                listed.append((i, 2 * target[0] + target[1]))
        return listed

    core_swap = pairs(lambda r, c: (r, 1 - c))
    x_swap = pairs(lambda r, c: (r ^ 1, c))

    def turn(x, by):
        return lax.ppermute(x, "rows", pairs(lambda r, c: ((r + 2 * by) % (row_count // 2), c)))

    def swap(x):
        return lax.ppermute(x, "rows", core_swap)

    def cross_x(x):
        return lax.ppermute(x, "rows", x_swap)

    rightward = [(i, i + 1) for i in range(col_count - 1)]
    leftward = [(i + 1, i) for i in range(col_count - 1)]
    col_swap = rightward + leftward

    def cross_cols(x):
        return lax.ppermute(x, "cols", col_swap)

    if col_count == 2:
        col_moves = [(None, col_swap, None, col_swap)]
    else:
        col_moves = [(0, leftward, 3, rightward), (13, rightward, 0, leftward)]
    edges = tuple(move[0] for move in col_moves)
    places = tuple(move[2] for move in col_moves)

    if fast:
        z, x = place // 2, place % 2
        dests = [2 * ((z + k % 4) % 4) + (x ^ (k // 4)) for k in range(8)]
        side = col
    else:
        dests = [jnp.int32(k) for k in range(8)]
        side = jnp.int32(0)
    sc = jnp.stack([core, side, (col == 0).astype(jnp.int32), place % 2] + dests)
    sc = sc.astype(jnp.int32)

    def swap_rows(a, b):
        odd_swap = pairs(lambda r, c: (r - 1 + 2 * (r % 2), c))
        return cross_x(a), lax.ppermute(b, "rows", odd_swap)

    x_own = tokens.reshape(own, d)
    g_own = cotangent.reshape(own, d)
    x_other, g_other = swap(x_own), swap(g_own)
    ids_other = swap(image_ids)

    gain = norm_gain.reshape(1, d)
    qg, kg = query_gain.reshape(1, HD), key_gain.reshape(1, HD)

    def mixer_block(which):
        return (mixer_weight, (width, d), lambda i, s: ((s[CORE] + which) % 2, 0))

    steps = ff // (4 * UNIT)
    dense_blocks = dense_weight.reshape(2 * steps, 2, UNIT, d)
    wf, wqkv, wd, bias_f = call(
        weights_kernel,
        sc,
        [
            (joined_weight, (d, 4 * UNIT), lambda i, s: (0, 3 + i)),
            (joined_weight, (d, width), lambda i, s: (0, 2 * jnp.minimum(i, 2) + s[CORE])),
            (dense_blocks, (2, None, UNIT, d), lambda i, s: (i, s[CORE], 0, 0)),
            (hidden_bias.reshape(1, ff), (1, 4 * UNIT), lambda i, s: (0, i)),
        ],
        [out((d, half_ff)), out((d, 3 * width)), out((half_ff, d)), out((1, half_ff), F32)],
        grid=steps,
    )

    edge = RADIUS * tile_cols
    normed, qs, kv, hats, roots, ids, row_a, row_b = call(
        project_kernel,
        sc,
        [x_own, x_other, image_ids, ids_other, wqkv, gain, qg, kg],
        [out((chip, d)), out((chip, width)), out((chip, d)), out((chip, d)), out((chip, d))]
        + [out((2 * tile_rows, 128), F32)]
        + [out((edge + 16, d))] * 2,
    )

    row_a, row_b = swap_rows(row_a, row_b)
    ext_rows = 2 * tile_rows + 2 * RADIUS

    g, gm, gsum = call(
        cotangent_kernel,
        sc,
        [g_own, g_other, mixer_block(0)],
        [out((chip, d)), out((chip, width)), out((1, d), F32)],
        after=[normed],
    )

    hidden, gpre, hsum = call(
        hidden_kernel,
        sc,
        [normed, g, wf, wd, bias_f],
        [out((chip, half_ff)), out((chip, half_ff)), out((1, half_ff), F32)],
    )

    count, slots, ko_rows, id_rows = 224, 576, ext_rows * tile_cols, 80
    moves = len(col_moves)
    ko, ids_ext, *msgs = call(
        functools.partial(extend_kernel, edges=edges),
        sc,
        [kv, row_a, row_b, ids],
        [out((ko_rows, d)), out((id_rows, 128), F32)] + [out((count + 16, d))] * moves,
        after=[hsum],
    )
    got = [lax.ppermute(msg, "cols", move[1]) for msg, move in zip(msgs, col_moves)]

    part = d // 8
    *jf_keep, jf_send_a, jf_send_b = call(
        joined_grad_kernel,
        sc,
        [normed, gpre],
        [out((part, half_ff))] * 4 + [out((2, part, half_ff))] * 2,
        scratch=[pltpu.VMEM((d, half_ff), BF)],
        after=[msgs[0]],
    )
    p_keep, p_send = call(
        back_output_kernel,
        sc,
        [hidden, wd],
        [out((own, d)), out((own, d))],
        after=[jf_send_a],
    )
    p_received = swap(p_send)
    kh, mask = call(
        functools.partial(slots_kernel, places=places),
        sc,
        got + [ids_ext],
        [out((slots, d)), out((chip, KEYS))],
        scratch=[pltpu.VMEM((id_rows, 128), F32)],
        after=[p_send],
    )
    near_keep, near_send, far_keep, far_send = call(
        dense_grad_kernel,
        sc,
        [hidden, g],
        [out((4, UNIT, width))] * 4,
        scratch=[pltpu.VMEM((half_ff, d), BF)],
        after=[kh],
    )

    def sums(arrays, plan, dtype=BF, after=(), work=10**9):
        shapes = []
        for groups in plan:
            parts = []
            for terms in groups:
                n, k = terms[0]
                parts.append(arrays[n].shape if k is None else arrays[n].shape[1:])
            rows = sum(p[-2] for p in parts)
            shapes.append(out(parts[0][:-2] + (rows, parts[0][-1]), dtype))
        return call(
            functools.partial(sum_kernel, plan=plan), sc, arrays, shapes, after=after, work=work
        )

    mixed, mixed_other, dq, dko, dkh = [], [], [], [], []
    wait = [far_send]
    if fast:
        jf_got_a = cross_x(jf_send_a)
        far_got, near_got = cross_cols(far_send), cross_cols(near_send)
    for pair in range(3):
        if fast and pair == 1:
            jf_1, jf_2 = sums(
                [jf_keep[1], jf_keep[2], jf_got_a],
                [[[(0, None), (2, 0)]], [[(1, None), (2, 1)]]],
                after=dq[-1:],
            )
            jf_t1, jf_t2 = turn(jf_1, 1), turn(jf_2, 2)
            wait = [jf_1]
        if fast and pair == 2:
            (far,) = sums([far_keep, far_got], [[[(0, None), (1, None)]]], after=dq[-1:])
            far_x = cross_x(far)
            wait = [far]
        results = call(
            functools.partial(attention_kernel, pair=pair),
            sc,
            [qs, gm, ko, kh, mask],
            [out((chip, 128)), out((chip, 128)), out((ko_rows, 256)), out((slots, 256))],
            scratch=[pltpu.VMEM((ko_rows, 256), F32), pltpu.VMEM((slots, 256), F32)],
            after=dq[-1:] + wait,
            work=10**10,
        )
        for values, value in zip((mixed, dq, dko, dkh), results):
            values.append(value)
        mixed_other.append(swap(results[0]))

    msgs = call(
        functools.partial(unslot_kernel, parts=3, places=places),
        sc,
        dkh,
        [out((count, d))] * moves,
        work=10**9,
    )
    back_got = [lax.ppermute(msg, "cols", move[3]) for msg, move in zip(msgs, col_moves)]

    wait = [msgs[0]]
    if fast:
        jf_got_b = cross_x(jf_send_b)
    gq, qsum, q_keep, q_send = call(
        q_back_kernel,
        sc,
        dq + [hats, roots, qg, normed],
        [out((chip, width)), out((1, width), F32)] + [out((4, part, width))] * 2,
        scratch=[pltpu.VMEM((d, width), BF)],
        after=wait,
    )
    m_near, m_far, m_send = call(
        mixer_grad_kernel,
        sc,
        mixed + mixed_other + [g],
        [out((4, d // 16, width))] * 2 + [out((8, d // 16, width))],
        scratch=[pltpu.VMEM((d, d), BF)],
        after=[q_send],
    )
    if fast:
        m_got = cross_cols(m_send)

    row_a, row_b, dkv = call(
        functools.partial(fold_kernel, parts=3, counts=(3,), edges=edges),
        sc,
        dko + back_got,
        [out((edge, d)), out((edge, d)), out((chip, d))],
        after=[m_send],
    )
    row_a, row_b = swap_rows(row_a, row_b)

    wait = [dkv]
    if fast:
        dense = sums(
            [near_keep, near_got, far_x],
            [[[(0, k), (1, k), (2, k)]] for k in range(4)],
            after=wait,
        )
        dense_turned = [turn(dense[k], k) for k in range(1, 4)]
        wait = [dense[0]]
    gn_keep, gn_send = call(
        back_normed_kernel,
        sc,
        [gpre, wf],
        [out((own, d)), out((own, d))],
        after=wait,
    )
    wait = [gn_send]
    if fast:
        (mq,) = sums(
            [m_far, m_got[4:], q_send],
            [[[(0, None), (1, None)], [(2, None)]]],
            after=wait,
        )
        mq_x = cross_x(mq)
        wait = [mq, jf_t1, jf_t2]

    gkv, ksum, *jkv_keep, jkv_send_a, jkv_send_b = call(
        kv_back_kernel,
        sc,
        [dkv, row_a, row_b, hats, roots, kg, normed],
        [out((chip, d)), out((1, width), F32)]
        + [out((part, d))] * 4
        + [out((2, part, d))] * 2,
        scratch=[pltpu.VMEM((d, d), BF)],
        after=wait,
    )
    wait = []
    if fast:
        jkv_got_a, jkv_got_b = cross_x(jkv_send_a), cross_x(jkv_send_b)
        jf_3, jf_0 = sums(
            [jf_keep[3], jf_keep[0], jf_got_b],
            [[[(0, None), (2, 0)]], [[(1, None), (2, 1)]]],
            after=[ksum],
        )
        jf_t3 = turn(jf_3, 3)
        wait = [jf_3]
    gn_keep, gn_send = call(
        normed_back_kernel,
        sc,
        [gq, gkv, wqkv, gn_keep, gn_send],
        [out((own, d)), out((own, d))],
        after=wait,
    )
    gn_received = swap(gn_send)
    wait = [gn_send]
    if fast:
        mq_parts = sums(
            [m_near, m_got, q_keep, mq_x[:, : d // 16], mq_x[:, d // 16 :]],
            [[[(0, k), (1, k), (3, k)], [(2, k), (4, k)]] for k in range(4)],
            after=wait,
        )
        mq_turned = [turn(mq_parts[k], k) for k in range(1, 4)]
        wait = [mq_parts[0]]
    tokens_grad, normsum = call(
        tokens_grad_kernel,
        sc,
        [x_own, g_own, gn_keep, gn_received, gain],
        [out((own, d)), out((1, d), F32)],
        after=wait,
    )
    if fast:
        jkv_1, jkv_2 = sums(
            [jkv_keep[1], jkv_keep[2], jkv_got_a],
            [[[(0, None), (2, 0)]], [[(1, None), (2, 1)]]],
            after=[normsum],
        )
        jkv_3, jkv_0 = sums(
            [jkv_keep[3], jkv_keep[0], jkv_got_b],
            [[[(0, None), (2, 0)]], [[(1, None), (2, 1)]]],
            after=[jkv_1],
        )
        jkv_turned = [turn(jkv_1, 1), turn(jkv_2, 2), turn(jkv_3, 3)]

    (small,) = call(
        pack_kernel, sc, [hsum, gsum, normsum, qsum, ksum], [out((48, 128), F32)], work=10**8
    )
    if fast:
        small = small + swap(small)
        small = small + cross_x(small)
        small = small + cross_cols(small)
        small = small + lax.ppermute(small, "rows", pairs(lambda r, c: (r ^ 2, c)))
        small = small + lax.ppermute(small, "rows", pairs(lambda r, c: (r ^ 4, c)))
    else:
        small = lax.psum(small, ("rows", "cols"))
    small_sums = call(
        unpack_kernel,
        sc,
        [small],
        [out((1, n), F32) for n in (ff, d, d, HD, HD)],
        work=10**8,
    )
    hidden_sum, output_sum, gain_sum, query_sum, key_sum = [v.reshape(-1) for v in small_sums]

    (result,) = call(
        result_kernel,
        sc,
        [x_own, *mixed, *mixed_other, mixer_block(0), mixer_block(1), p_keep, p_received]
        + [output_bias.reshape(1, d)],
        [out((own, d))],
        after=[jkv_3] if fast else [],
    )

    if fast:
        (dense_sum,) = sums(dense[:1] + dense_turned, [[[(k, None) for k in range(4)]]], F32)
        (mq_sum,) = sums(mq_parts[:1] + mq_turned, [[[(k, None) for k in range(4)]]], F32)
        mixer_sum = mq_sum[: d // 16]
        half = (3 * width + half_ff) // 2
        kept, sent = call(
            joined_sides_kernel,
            sc,
            [mq_sum[d // 16 :], jkv_0, *jkv_turned, jf_0, jf_t1, jf_t2, jf_t3],
            [out((part, half), F32), out((part, half))],
        )
        mine, sent = call(
            joined_cores_kernel,
            sc,
            [kept, cross_cols(sent)],
            [out((part // 2, half), F32), out((part // 2, half))],
            scratch=[pltpu.VMEM((part, half), F32)],
        )
        (joined_sum,) = call(
            assemble_kernel, sc, [mine, swap(sent)], [out((part // 2, 2 * half), F32)]
        )
    else:

        def spread_core(x, axis):
            x = jnp.expand_dims(x, axis)
            is_mine = jnp.arange(2).reshape([2 if i == axis else 1 for i in range(x.ndim)]) == core
            return jnp.where(is_mine, x, jnp.zeros_like(x))

        def reduce(x):
            x = lax.psum_scatter(x, "rows", scatter_dimension=0, tiled=True)
            return lax.psum_scatter(x, "cols", scatter_dimension=1, tiled=True).astype(F32)

        def in_order(keep, send_a, send_b):
            return jnp.concatenate(
                [jnp.stack(keep), send_b[1:], send_a, send_b[:1]], axis=0
            ).reshape(d, keep[0].shape[1])

        dense = [jnp.concatenate(v, axis=2) for v in ((near_keep, near_send), (far_keep, far_send))]
        dense_sum = reduce(spread_core(jnp.concatenate(dense, axis=0), 1).reshape(ff, d))
        mixer = jnp.concatenate([jnp.concatenate([m_near, m_far], axis=0), m_send], axis=2)
        mixer_sum = reduce(spread_core(mixer, 1).reshape(d, d))
        jq = jnp.concatenate([q_keep, q_send], axis=0).reshape(d, 1, width)
        jkv = in_order(jkv_keep, jkv_send_a, jkv_send_b).reshape(d, 2, width)
        jf = in_order(jf_keep, jf_send_a, jf_send_b).reshape(d, ff // (2 * UNIT), UNIT)
        qkv = spread_core(jnp.concatenate([jq, jkv], axis=1), 2).reshape(d, 3 * d)
        joined_sum = reduce(jnp.concatenate([qkv, spread_core(jf, 2).reshape(d, ff)], axis=1))

    shape = (tile_rows, tile_cols, d)
    return (
        result.reshape(shape),
        tokens_grad.reshape(shape),
        joined_sum,
        hidden_sum,
        mixer_sum,
        dense_sum,
        output_sum,
        gain_sum,
        query_sum,
        key_sum,
    )


def solution(mesh):
    tiles, everywhere, blocks = P("rows", "cols", None), P(), P("rows", "cols")
    return jax.shard_map(
        per_device,
        mesh=mesh,
        in_specs=(tiles, blocks) + (everywhere,) * 8 + (tiles,),
        out_specs=(tiles, tiles, blocks, P(), blocks, blocks, P(), P(), P(), P()),
        check_vma=False,
    )
```

```python
import functools
import types

import jax
import jax.numpy as jnp
from jax import lax
from jax.experimental import pallas as pl
from jax.experimental.pallas import tpu as pltpu
from jax.sharding import PartitionSpec as P

H = 12
HD = 64
RADIUS = 3
EPSILON = 1e-06
BF = jnp.bfloat16
F32 = jnp.float32
MIB = 1024 * 1024

UNIT = 192
STRIP = 4
KEYS = 256
HALO_SLOTS = 8
MIXER_ROWS = 32
SPARE = 64
GROUP = 8
Z_ORDER = (1, 3, 0, 2)


def mm(a, b, ca=1, cb=0):
    return lax.dot_general(a, b, (((ca,), (cb,)), ((), ())), preferred_element_type=F32)


HBM = "hbm"


def kernel_name(kernel):
    while isinstance(kernel, functools.partial):
        kernel = kernel.args[0] if kernel.args else kernel.func
    return kernel.__name__


def call(kernel, scalars, ins, outs, scratch=(), vmem=16, after=(), grid=1, work=0):
    ins = [entry if isinstance(entry, tuple) else (entry, None, None) for entry in ins]
    outs = [entry if isinstance(entry, tuple) else (entry, None, None) for entry in outs]

    def spec(_, block, index):
        if block is None:
            return pl.BlockSpec(memory_space=pltpu.VMEM)
        return pl.BlockSpec(memory_space=pltpu.HBM) if block == HBM else pl.BlockSpec(block, index)

    def placed(x, block, _):
        return x if block is None else pltpu.with_memory_space_constraint(x, pltpu.HBM)

    def run(sc, *refs):
        kernel(sc, *refs[: len(ins)], *refs[len(ins) + len(after) :])

    run_kernel = pl.pallas_call(
        run,
        name=kernel_name(kernel),
        grid_spec=pltpu.PrefetchScalarGridSpec(
            num_scalar_prefetch=1,
            grid=(grid,),
            in_specs=[spec(*entry) for entry in ins]
            + [pl.BlockSpec(memory_space=pl.ANY)] * len(after),
            out_specs=[spec(*entry) for entry in outs],
            scratch_shapes=list(scratch),
        ),
        out_shape=[entry[0] for entry in outs],
        compiler_params=pltpu.CompilerParams(vmem_limit_bytes=vmem * MIB),
        cost_estimate=pl.CostEstimate(flops=work, bytes_accessed=0, transcendentals=0),
    )
    return list(run_kernel(scalars, *[placed(*entry) for entry in ins], *after))


def out(shape, dtype=BF):
    return jax.ShapeDtypeStruct(shape, dtype)


def written(shape, dtype=BF):
    return (pltpu.HBM(shape, dtype), shape, lambda i, s: (0,) * len(shape))


def with_token(kernel, *refs):
    kernel(*refs[:-1])
    refs[-1][...] = jnp.zeros_like(refs[-1])


def aligned(start, size, unit):
    return pl.ds(pl.multiple_of(start, unit), size)


def head_means(width):
    row = lax.broadcasted_iota(jnp.int32, (width, width), 0)
    col = lax.broadcasted_iota(jnp.int32, (width, width), 1)
    return jnp.where(row // HD == col // HD, 1.0 / HD, 0.0).astype(BF)


def per_head(x, means):
    width = means.shape[0]
    parts = [mm(x[:, j : j + width].astype(BF), means) for j in range(0, x.shape[1], width)]
    return jnp.concatenate(parts, axis=1)


CORE, SIDE, ON_LEFT, ODD, DEST = 0, 1, 2, 3, 4


def weights_kernel(sc, joined, bias, wf, b_out):
    cols = aligned(pl.program_id(0) * 2 * UNIT, 2 * UNIT, 128)
    for core in range(2):

        @pl.when(sc[CORE] == core)
        def _():
            lo, hi = core * UNIT, (2 + core) * UNIT
            w = joined[...]
            wf[:, cols] = jnp.concatenate([w[:, lo : lo + UNIT], w[:, hi : hi + UNIT]], axis=1)
            b = bias[...]
            b_out[:, cols] = jnp.concatenate([b[:, lo : lo + UNIT], b[:, hi : hi + UNIT]], axis=1)


def split_ids(ids):
    high = jnp.floor(ids * (1.0 / 256))
    return [(ids - 256.0 * high).astype(BF), high.astype(BF)]


def joined_ids(low, high):
    return low.astype(F32) + 256.0 * high.astype(F32)


def row_messages(sc, top, bottom):
    odd = sc[ODD] == 1
    return jnp.where(odd, top, bottom), jnp.where(odd, bottom, top)


def project_kernel(
    sc, xo, xt, io, it, joined, dense, gain, qg, kg, normed, qs, kv, hats, roots, ids, row_a, row_b, wqkv, wd, sems
):
    means = head_means(4 * HD)
    own = xo.shape[0]
    width = qs.shape[1]
    heads = width // HD
    copies = []
    for k in range(3):
        cols = aligned((2 * k + sc[CORE]) * width, width, 128)
        copies.append((joined.at[:, cols], wqkv.at[:, k * width : (k + 1) * width]))
    for k in range(dense.shape[0]):
        copies.append((dense.at[k, sc[CORE]], wd.at[k * UNIT : (k + 1) * UNIT, :]))
    copies = [pltpu.make_async_copy(a, b, sems.at[n]) for n, (a, b) in enumerate(copies)]
    for copy in copies:
        copy.start()
    gains = jnp.concatenate([qg[...]] * heads + [kg[...]] * heads, axis=1)
    block = 256
    for half, ref in enumerate((xo, xt)):
        start = (sc[CORE] if half == 0 else 1 - sc[CORE]) * own
        for i in range(own // block):
            x = ref[i * block : (i + 1) * block, :].astype(F32)
            rows = aligned(start + i * block, block, block)
            center = x - jnp.mean(x, axis=1, keepdims=True)
            spread = jnp.mean(center * center, axis=1, keepdims=True)
            n = (center * lax.rsqrt(spread + EPSILON) * gain[...]).astype(BF)
            normed[rows, :] = n
            if half == 0 and i == 0:
                for copy in copies[:3]:
                    copy.wait()
            part = mm(n, wqkv[:, : 2 * width])
            center = part - per_head(part, means)
            root = lax.rsqrt(per_head(center * center, means) + EPSILON)
            hat = center * root
            hats[rows, :] = hat.astype(BF)
            roots[rows, :] = root.astype(BF)
            low = (hat * gains).astype(BF)
            qs[rows, :] = low[:, :width] * jnp.asarray(HD**-0.5, BF)
            values = mm(n, wqkv[:, 2 * width :]).astype(BF)
            for p in range(width // 128):
                kv[rows, 256 * p : 256 * p + 128] = low[:, width + 128 * p : width + 128 * p + 128]
                kv[rows, 256 * p + 128 : 256 * p + 256] = values[:, 128 * p : 128 * p + 128]
    edge, chip = RADIUS * io.shape[1], kv.shape[0]
    row_a[:edge, :], row_b[:edge, :] = row_messages(sc, kv[:edge, :], kv[chip - edge :, :])
    size = io.shape[0]
    for half, ref in enumerate((io, it)):
        start = (sc[CORE] if half == 0 else 1 - sc[CORE]) * size
        value = ref[...].astype(F32) + 1.0
        zeros = jnp.zeros((size, ids.shape[1] - value.shape[1]), F32)
        ids[aligned(start, size, size), :] = jnp.concatenate([value, zeros], axis=1)
    zeros = jnp.zeros((16 - 8, 128), BF)
    id_a, id_b = row_messages(sc, ids[:8, :], ids[2 * size - 8 :, :])
    for ref, values in ((row_a, id_a), (row_b, id_b)):
        ref[edge:, :] = jnp.zeros((16, ref.shape[1]), BF)
        for j, piece in enumerate(split_ids(values)):
            ref[edge:, 128 * j : 128 * j + 128] = jnp.concatenate([piece, zeros], axis=0)
    for copy in copies[3:]:
        copy.wait()


def cotangent_kernel(sc, go, gt, mixer, g_out, gm, gsum):
    own = go.shape[0]
    for half, ref in enumerate((go, gt)):
        start = (sc[CORE] if half == 0 else 1 - sc[CORE]) * own
        rows = aligned(start, own, own)
        g = ref[...]
        g_out[rows, :] = g
        gm[rows, :] = mm(g, mixer[...], 1, 1).astype(BF)
    gsum[...] = jnp.sum(go[...].astype(F32), axis=0, keepdims=True)


def hidden_kernel(sc, n_ref, g_ref, wf, wd, bias, hidden, gpre, hsum):
    wide = wf.shape[1]
    dense = wd[...]
    block = 256
    total = jnp.zeros((1, wide), F32)
    for i in range(n_ref.shape[0] // block):
        rows = slice(i * block, (i + 1) * block)
        pre = mm(n_ref[rows, :], wf[...]) + bias[...]
        gd = mm(g_ref[rows, :], dense, 1, 1)
        a, b = 0.7978845608, 0.044715
        sq = pre * pre
        t = jnp.tanh(a * pre * (1.0 + b * sq))
        half = 0.5 * (1.0 + t)
        hidden[rows, :] = (pre * half).astype(BF)
        slope = half + (0.5 * a) * pre * (1.0 - t * t) * (1.0 + 3.0 * b * sq)
        gp = gd * slope
        gpre[rows, :] = gp.astype(BF)
        total = total + jnp.sum(gp, axis=0, keepdims=True)
    hsum[...] = total


def dense_grad_kernel(sc, h_ref, g_ref, near_keep, far_keep, near_send, far_send, scr):
    wide, d = scr.shape
    step = wide // 3
    half = d // 2
    for j in range(3):
        cols = slice(j * step, (j + 1) * step)
        scr[cols, :] = mm(h_ref[:, cols], g_ref[...], 0, 0).astype(BF)
    mine = aligned(sc[SIDE] * half, half, 128)
    other = aligned((1 - sc[SIDE]) * half, half, 128)
    for rel in range(8):
        rows = aligned(sc[DEST + rel] * UNIT, UNIT, 64)
        keep, send = (near_keep, near_send) if rel < 4 else (far_keep, far_send)
        keep[rel % 4] = scr[rows, mine]
        send[rel % 4] = scr[rows, other]


def scatter_rows(sc, scr, keep, *sends):
    size = scr.shape[0] // 8
    each = 4 // len(sends)
    for rel in range(8):
        block = scr[aligned(sc[DEST + rel] * size, size, 32), :]
        if rel < 4:
            keep[rel, :size, :] = block
        else:
            sends[(rel - 4) // each][(rel - 4) % each, :size, :] = block


def joined_grad_kernel(sc, n_ref, gp_ref, keep, send, scr):
    step = scr.shape[1] // 3
    for j in range(3):
        cols = slice(j * step, (j + 1) * step)
        scr[:, cols] = mm(n_ref[...], gp_ref[:, cols], 0, 0).astype(BF)
    scatter_rows(sc, scr, keep, send)


def back_output_kernel(sc, h_ref, wd, keep, send):
    own = keep.shape[0]
    dense = wd[...]
    keep[...] = mm(h_ref[aligned(sc[CORE] * own, own, own), :], dense).astype(BF)
    send[...] = mm(h_ref[aligned((1 - sc[CORE]) * own, own, own), :], dense).astype(BF)


def back_normed_kernel(sc, gp_ref, wf, keep, send):
    own = keep.shape[0]
    mine, theirs = gp_ref[aligned(sc[CORE] * own, own, own), :], gp_ref[aligned((1 - sc[CORE]) * own, own, own), :]
    keep[...] = mm(mine, wf[...], 1, 1).astype(BF)
    send[...] = mm(theirs, wf[...], 1, 1).astype(BF)


def edge_picks(rows, first, count):
    msg = lax.broadcasted_iota(jnp.int32, (count, rows), 0)
    tok = lax.broadcasted_iota(jnp.int32, (count, rows), 1)
    return jnp.where(tok == msg // 3 * 16 + first + msg % 3, 1.0, 0.0).astype(BF)


def slot_places(count, slots, first):
    slot = lax.broadcasted_iota(jnp.int32, (slots, count), 0)
    msg = lax.broadcasted_iota(jnp.int32, (slots, count), 1)
    return jnp.where(slot == msg // 3 * HALO_SLOTS + first + msg % 3, 1.0, 0.0).astype(BF)


def extend_kernel(sc, *refs, edges):
    kv, row_a, row_b, ids, ko, ids_ext, *msgs = refs
    edge, own = row_a.shape[0] - 16, kv.shape[0]
    top, bottom = row_messages(sc, row_a[...], row_b[...])
    ko[:edge, :] = top[:edge]
    ko[edge : edge + own, :] = kv[...]
    ko[edge + own :, :] = bottom[:edge]
    size = ids.shape[0]
    ids_ext[...] = jnp.zeros_like(ids_ext)
    ids_ext[:RADIUS, :] = joined_ids(top[edge:, :128], top[edge:, 128:256])[8 - RADIUS : 8]
    ids_ext[RADIUS : RADIUS + size, :] = ids[...]
    ids_ext[RADIUS + size : 2 * RADIUS + size, :] = joined_ids(
        bottom[edge:, :128], bottom[edge:, 128:256]
    )[:RADIUS]
    count = msgs[0].shape[0] - 16
    for msg, first in zip(msgs, edges):
        left, right = ids_ext[...], pltpu.roll(ids_ext[...], 128 - 13, 1)
        if first is None:
            shifted = jnp.where(sc[ON_LEFT] == 1, right, left)
            first = 13 * sc[ON_LEFT]
        else:
            shifted = right if first else left
        msg[:count, :] = mm(edge_picks(ko.shape[0], first, count), ko[...]).astype(BF)
        msg[count:, :] = jnp.zeros((16, msg.shape[1]), BF)
        turned = jnp.transpose(shifted)[:8]
        msg[count:, : turned.shape[1]] = jnp.concatenate(split_ids(turned), axis=0)


def slots_kernel(sc, *refs, places):
    moves = len(places)
    msgs, ids_ext, kh, mask, ids = refs[:moves], *refs[moves:]
    count = msgs[0].shape[0] - 16
    total = 0.0
    all_ids = ids_ext[...]
    for msg, first in zip(msgs, places):
        pieces = msg[count:, :128]
        turned = jnp.transpose(joined_ids(pieces[:8], pieces[8:]))[: ids.shape[0]]
        turned = jnp.concatenate(
            [turned[:, :RADIUS], jnp.zeros((ids.shape[0], 128 - RADIUS), F32)], axis=1
        )
        left, right = pltpu.roll(turned, 16, 1), pltpu.roll(turned, 19, 1)
        if first is None:
            all_ids = all_ids + jnp.where(sc[ON_LEFT] == 1, right, left)
            first = 3 * sc[ON_LEFT]
        else:
            all_ids = all_ids + (right if first else left)
        total = total + mm(slot_places(count, kh.shape[0], first), msg[:count, :])
    kh[...] = total.astype(BF)
    ids[...] = all_ids
    write_mask(ids, mask)


def write_mask(ids, bias):
    lane = lax.broadcasted_iota(jnp.int32, (STRIP * 16, KEYS), 1)
    query = lax.broadcasted_iota(jnp.int32, (STRIP * 16, KEYS), 0)
    inner = lane < 160
    halo = lane - 160
    slot = halo % HALO_SLOTS
    key_row = jnp.where(inner, lane // 16, halo // HALO_SLOTS)
    key_col = jnp.where(inner, lane % 16, jnp.where(slot < 3, slot - 3, slot + 13))
    row_gap = key_row - query // 16
    col_gap = key_col - query % 16
    reach = (
        (row_gap >= 0)
        & (row_gap <= 2 * RADIUS)
        & (col_gap >= -RADIUS)
        & (col_gap <= RADIUS)
        & (inner | (slot < 6))
    )
    itself = inner & (row_gap == RADIUS) & (col_gap == 0)
    lane16 = lax.broadcasted_iota(jnp.int32, (16, KEYS), 1)
    window = jnp.zeros((16, KEYS), F32)
    for i in range(STRIP + 2 * RADIUS):
        part = jnp.concatenate(
            [ids[pl.ds(i, 16, stride=STRIP), :], jnp.zeros((16, KEYS - 128), F32)], axis=1
        )
        own = jnp.where(lane16 < 16, part, 0.0)
        side = jnp.where(lane16 >= 16, part, 0.0)
        if i > 0:
            own = pltpu.roll(own, 16 * i, 1)
        side = pltpu.roll(side, 144 + HALO_SLOTS * i, 1)
        window = window + own + side
    for s in range(16):
        row = jnp.broadcast_to(window[s : s + 1, :], (STRIP * 16, KEYS))
        mine = jnp.sum(jnp.where(itself, row, 0.0), axis=1, keepdims=True)
        bias[s * 64 : (s + 1) * 64, :] = jnp.where(reach & (row == mine), 0.0, -1e30).astype(BF)


def attention_kernel(sc, q_ref, gm_ref, ko, kh, bias, mixed, dq, dko_out, dkh_out, dko, dkh, *, pair):
    dko[...] = jnp.zeros_like(dko)
    dkh[...] = jnp.zeros_like(dkh)
    lane = lax.broadcasted_iota(jnp.int32, (64, 128), 1)
    low = lane < HD
    zero = jnp.zeros((64, 128), BF)
    lanes = slice(128 * pair, 128 * pair + 128)
    k_lanes = slice(256 * pair, 256 * pair + 128)
    v_lanes = slice(256 * pair + 128, 256 * pair + 256)

    def both(x):
        return jnp.concatenate([jnp.where(low, x, zero), jnp.where(low, zero, x)], axis=0)

    for first in range(0, 16, GROUP):
        strips = []
        for s in range(first, first + GROUP):
            rows = slice(s * 64, (s + 1) * 64)
            inner = slice(s * 64, s * 64 + 160)
            side = slice(s * 32, s * 32 + 96)
            strips.append((rows, inner, side))
        q2 = [both(q_ref[rows, lanes]) for rows, _, _ in strips]
        gm2 = [both(gm_ref[rows, lanes]) for rows, _, _ in strips]
        k = [jnp.concatenate([ko[i, k_lanes], kh[j, k_lanes]], axis=0) for _, i, j in strips]
        v = [jnp.concatenate([ko[i, v_lanes], kh[j, v_lanes]], axis=0) for _, i, j in strips]
        b = [bias[rows, :].astype(F32) for rows, _, _ in strips]
        scores = [mm(x, y, 1, 1) for x, y in zip(q2, k)]
        dp = [mm(x, y, 1, 1) for x, y in zip(gm2, v)]
        probs = []
        for x, y in zip(scores, b):
            weights = jnp.exp(x + jnp.concatenate([y, y], axis=0))
            probs.append(weights * (1.0 / jnp.sum(weights, axis=1, keepdims=True)))
        ds = []
        for x, y in zip(probs, dp):
            balance = jnp.sum(x * y, axis=1, keepdims=True)
            ds.append((x * (y - balance)).astype(BF))
        probs = [x.astype(BF) for x in probs]
        o = [mm(x, y) for x, y in zip(probs, v)]
        d = [mm(x, y) for x, y in zip(ds, k)]
        dk = [mm(x, y, 0, 0) for x, y in zip(ds, q2)]
        dv = [mm(x, y, 0, 0) for x, y in zip(probs, gm2)]
        for n, (rows, inner, side) in enumerate(strips):
            mixed[rows, :] = jnp.where(low, o[n][:64], o[n][64:]).astype(BF)
            dq[rows, :] = (jnp.where(low, d[n][:64], d[n][64:]) * (HD**-0.5)).astype(BF)
            dko[inner, :128] += dk[n][:160]
            dkh[side, :128] += dk[n][160:]
            dko[inner, 128:] += dv[n][:160]
            dkh[side, 128:] += dv[n][160:]
    dko_out[...] = dko[...].astype(BF)
    dkh_out[...] = dkh[...].astype(BF)


def unslot_kernel(sc, *refs, parts, places):
    dkh, msgs = refs[:parts], refs[parts:]
    for msg, first in zip(msgs, places):
        first = 3 * sc[ON_LEFT] if first is None else first
        places_of = slot_places(msg.shape[0], dkh[0].shape[0], first)
        for p, ref in enumerate(dkh):
            msg[:, 256 * p : 256 * p + 256] = mm(places_of, ref[...], 0, 0).astype(BF)


def fold_kernel(sc, passing, *refs, parts, counts, edges):
    dko, refs = refs[:parts], refs[parts:]
    groups, refs = refs[: len(counts) * len(edges)], refs[len(counts) * len(edges) :]
    row_a, row_b, center, passed = refs
    passed[...] = passing[...]
    rows = dko[0].shape[0]
    edge = row_a.shape[0]
    count = groups[0].shape[0]
    picks = []
    for first in edges:
        picks.append(edge_picks(rows, 13 * sc[ON_LEFT] if first is None else first, count))
    p = 0
    for n, size in enumerate(counts):
        for j in range(size):
            total = dko[p][...].astype(F32)
            for e, pick in enumerate(picks):
                msg = groups[n * len(edges) + e]
                total = total + mm(pick, msg[:, 256 * j : 256 * j + 256], 0, 0)
            lanes = slice(256 * p, 256 * p + 256)
            low = total.astype(BF)
            row_a[:, lanes], row_b[:, lanes] = row_messages(sc, low[:edge], low[rows - edge :])
            center[:, lanes] = low[edge : rows - edge]
            p += 1


def norm_back(grad, hat, root, gains, means):
    u = [gains * x for x in grad]
    mean = [per_head(x, means) for x in u]
    along = [per_head(x * y, means) for x, y in zip(u, hat)]
    back = [
        ((x - m - h * y) * r).astype(BF) for x, m, h, y, r in zip(u, mean, hat, along, root)
    ]
    total = sum(jnp.sum(x * h, axis=0, keepdims=True) for x, h in zip(grad, hat))
    return back, total


def q_back_kernel(sc, dq0, dq1, dq2, hats, roots, qg, n_ref, gj, sums, keep, send, scr):
    means = head_means(2 * HD)
    width = gj.shape[1]
    gains = jnp.concatenate([qg[...]] * (width // HD), axis=1)
    block = 256
    blocks = [slice(i, i + block) for i in range(0, gj.shape[0], block)]
    grad = [
        jnp.concatenate([dq0[rows, :], dq1[rows, :], dq2[rows, :]], axis=1).astype(F32)
        for rows in blocks
    ]
    hat = [hats[rows, :width].astype(F32) for rows in blocks]
    root = [roots[rows, :width].astype(F32) for rows in blocks]
    back, sums[...] = norm_back(grad, hat, root, gains, means)
    for rows, x in zip(blocks, back):
        gj[rows, :] = x
    scr[...] = mm(n_ref[...], jnp.concatenate(back, axis=0), 0, 0).astype(BF)
    scatter_rows(sc, scr, keep, send)


def kv_back_kernel(
    sc, dkv, row_a, row_b, hats, roots, kg, n_ref, m_near, m_far, gj, sums, keep, send_a, send_b, scr
):
    means = head_means(2 * HD)
    tokens = dkv.shape[0]
    edge = row_a.shape[0]
    width = hats.shape[1] // 2
    gains = jnp.concatenate([kg[...]] * (width // HD), axis=1)
    block = 256
    top, bottom = row_messages(sc, row_a[...].astype(F32), row_b[...].astype(F32))
    blocks = [slice(i, i + block) for i in range(0, tokens, block)]
    grads = [dkv[rows, :].astype(F32) for rows in blocks]
    grads[0] = jnp.concatenate([grads[0][:edge] + top, grads[0][edge:]], axis=0)
    grads[-1] = jnp.concatenate([grads[-1][:-edge], grads[-1][-edge:] + bottom], axis=0)

    def lanes(x, shift):
        return jnp.concatenate(
            [x[:, 256 * p + shift : 256 * p + shift + 128] for p in range(width // 128)], axis=1
        )

    grad = [lanes(x, 0) for x in grads]
    values = [lanes(x, 128).astype(BF) for x in grads]
    hat = [hats[rows, width:].astype(F32) for rows in blocks]
    root = [roots[rows, width:].astype(F32) for rows in blocks]
    back, sums[...] = norm_back(grad, hat, root, gains, means)
    for rows, x, y in zip(blocks, back, values):
        gj[rows, :width] = x
        gj[rows, width:] = y
    for j, x in enumerate((back, values)):
        cols = slice(j * width, (j + 1) * width)
        scr[:, cols] = mm(n_ref[...], jnp.concatenate(x, axis=0), 0, 0).astype(BF)
    scatter_rows(sc, scr, keep, send_a, send_b)
    part = scr.shape[0] // 8
    for k in range(4):
        target, n = (send_a, send_b)[k // 2], k % 2
        for ref, place, values in ((keep, k, m_near[k]), (target, n, m_far[k])):
            values = values.astype(F32)
            size = values.shape[0] // 2
            block = jnp.concatenate([values[:size], values[size:]], axis=1)
            rest = jnp.zeros((MIXER_ROWS - size, block.shape[1]), F32)
            ref[place, part : part + MIXER_ROWS, :] = jnp.concatenate([block, rest], axis=0).astype(BF)


def normed_back_kernel(sc, gq, gkv, wqkv, keep_in, send_in, n_ref, gain, keep, send, gsum):
    own = keep.shape[0]
    width = gq.shape[1]
    shares = []
    for start, before, after in ((sc[CORE], keep_in, keep), (1 - sc[CORE], send_in, send)):
        rows = aligned(start * own, own, own)
        total = before[...].astype(F32) + mm(gq[rows, :], wqkv[:, :width], 1, 1)
        total = total + mm(gkv[rows, :], wqkv[:, width:], 1, 1)
        shares.append(jnp.sum(total * n_ref[rows, :].astype(F32), axis=0, keepdims=True))
        after[...] = total.astype(after.dtype)
    gsum[...] = (shares[0] + shares[1]) / gain[...]


def mixer_grad_kernel(sc, m0, m1, m2, o0, o1, o2, g_ref, passing, mixed, other, keep, send, passed, scr):
    passed[...] = passing[...]
    for p, (m, o) in enumerate(((m0, o0), (m1, o1), (m2, o2))):
        mixed[:, 128 * p : 128 * p + 128] = m[...]
        other[:, 128 * p : 128 * p + 128] = o[...]
    width = mixed.shape[1]
    scr[aligned(sc[CORE] * width, width, 128), :] = mm(mixed[...], g_ref[...], 0, 0).astype(BF)
    scr[aligned((1 - sc[CORE]) * width, width, 128), :] = mm(other[...], g_ref[...], 0, 0).astype(BF)
    size = scr.shape[0] // 16
    mine = aligned(sc[SIDE] * width, width, 128)
    theirs = aligned((1 - sc[SIDE]) * width, width, 128)
    for rel in range(8):
        rows = aligned((2 * sc[DEST + rel] + sc[CORE]) * size, size, 16)
        keep[rel] = scr[rows, mine]
        send[rel] = scr[rows, theirs]


def result_kernel(sc, x, mixed, other, mixer_a, mixer_b, keep, received, bias, result):
    own = x.shape[0]
    mine = aligned(sc[CORE] * own, own, own)
    total = x[...].astype(F32) + bias[...] + keep[...].astype(F32) + received[...].astype(F32)
    total = total + mm(mixed[mine, :], mixer_a[...]) + mm(other[mine, :], mixer_b[...])
    result[...] = total.astype(BF)


def tokens_grad_kernel(sc, x_ref, g_ref, keep, received, gain, grad):
    x = x_ref[...].astype(F32)
    gn = keep[...].astype(F32) + received[...].astype(F32)
    center = x - jnp.mean(x, axis=1, keepdims=True)
    rs = lax.rsqrt(jnp.mean(center * center, axis=1, keepdims=True) + EPSILON)
    hat = center * rs
    u = gain[...] * gn
    back = u - jnp.mean(u, axis=1, keepdims=True) - hat * jnp.mean(u * hat, axis=1, keepdims=True)
    grad[...] = (g_ref[...].astype(F32) + back * rs).astype(BF)


def wide_sum(terms):
    total = terms[0].astype(F32)
    for term in terms[1:]:
        total = total + term.astype(F32)
    return total


def sum_kernel(sc, *refs, plan):
    count = len(refs) - len(plan)
    for target, terms in zip(refs[count:], plan):
        values = [refs[n][...] if k is None else refs[n][k] for n, k in terms]
        target[...] = wide_sum(values).astype(target.dtype)


def split(x):
    high = x.astype(BF)
    return jnp.concatenate([high, (x - high.astype(F32)).astype(BF)], axis=0)


def joint(x):
    size = x.shape[0] // 2
    return x[:size].astype(F32) + x[size:].astype(F32)


def z1_kernel(sc, kv, kv_got, small, hop, out_ref):
    size = kv.shape[1]
    for k in range(2):
        out_ref[k * size : (k + 1) * size, :] = wide_sum([kv[k], kv_got[k]]).astype(BF)
    out_ref[2 * size :, :] = split(small[...] + hop[...])


def z2_kernel(sc, kv, kv_got, sent, got, keep, out_ref):
    size = keep.shape[0]
    for k in range(2):
        value = wide_sum([kv[2 + k], kv_got[k, :size, :], got[k * size : (k + 1) * size, :]])
        if k == 0:
            keep[...] = value
        else:
            out_ref[:size, :] = value.astype(BF)
    total = joint(sent[2 * size :, :]) + joint(got[2 * size :, :])
    out_ref[size:, :] = split(total)


def joined_sides_kernel(sc, kv, sent, got, q, q_got, f, f_got, keep, send, mixer):
    rows = kv.shape[0]
    total = kv[...] + got[:rows, :].astype(F32)
    small = joint(sent[rows:, :]) + joint(got[rows:, :])
    part, width = f.shape[0], mixer.shape[1]
    size = mixer.shape[0] // 2
    m = total[part : part + size]
    mixer[...] = jnp.concatenate([m[:, :width], m[:, width:]], axis=0)
    joined = jnp.concatenate(
        [wide_sum([q[...], q_got[...]]), total[:part], wide_sum([f[...], f_got[...]])], axis=1
    )
    half = joined.shape[1] // 2
    small = split(small)
    for side in range(2):

        @pl.when(sc[SIDE] == side)
        def _():
            keep[...] = joined[:, side * half : (side + 1) * half]
            send[:part, :] = joined[:, (1 - side) * half : (2 - side) * half].astype(BF)

    send[part:, :] = jnp.concatenate(
        [small, jnp.zeros((small.shape[0], half - small.shape[1]), BF)], axis=1
    )


def joined_cores_kernel(sc, kept, sent, received, mine, send, small, scr):
    part = kept.shape[0]
    scr[...] = kept[...] + received[:part, :].astype(F32)
    size, wide = mine.shape[0], small.shape[1]
    mine[...] = scr[aligned(sc[CORE] * size, size, 8), :]
    send[...] = scr[aligned((1 - sc[CORE]) * size, size, 8), :].astype(BF)
    small[...] = joint(sent[part:, :wide]) + joint(received[part:, :wide])


def assemble_kernel(sc, mine, theirs, final):
    width = 384
    for core in range(2):
        first, second = (mine, theirs) if core == 0 else (theirs, mine)
        for side in range(2):

            @pl.when((sc[CORE] == core) & (sc[SIDE] == side))
            def _():
                a, b = first[...].astype(F32), second[...].astype(F32)
                size, count = (width, 3) if side == 0 else (UNIT, 7)
                cuts = [slice(j * size, (j + 1) * size) for j in range(count)]
                if side == 0:
                    cuts.append(slice(3 * width, a.shape[1]))
                final[...] = jnp.concatenate([x[:, cut] for cut in cuts for x in (a, b)], axis=1)


def pack_kernel(sc, hsum, gsum, nsum, qsum, ksum, small, scr):
    scr[...] = jnp.zeros_like(scr)
    row = 2 * hsum.shape[1] // 128
    for ref in (gsum, nsum, qsum, ksum):
        for j in range(ref.shape[1] // 128):
            scr[row : row + 1, :] = ref[:, 128 * j : 128 * j + 128]
            row += 1
    count = hsum.shape[1] // 128
    for j in range(count):
        scr[pl.ds(sc[CORE] * count + j, 1), :] = hsum[:, 128 * j : 128 * j + 128]
    small[...] = jnp.concatenate([scr[j : j + 8, :] for j in range(0, 48, 8)], axis=1)


def unpack_kernel(sc, *refs):
    *terms, hidden, output, norm, query, key = refs
    small = wide_sum([ref[...] for ref in terms])
    small = jnp.concatenate([small[:, j : j + 128] for j in range(0, small.shape[1], 128)], axis=0)
    count = hidden.shape[1] // 256
    cores = []
    for core in range(2):
        rows = [small[core * count + j : core * count + j + 1, :] for j in range(count)]
        cores.append(jnp.concatenate(rows, axis=1))
    blocks = []
    for j in range(cores[0].shape[1] // UNIT):
        blocks += [x[:, j * UNIT : (j + 1) * UNIT] for x in cores]
    hidden[...] = jnp.concatenate(blocks, axis=1)
    row = 2 * count
    for ref in (output, norm):
        for j in range(ref.shape[1] // 128):
            ref[:, 128 * j : 128 * j + 128] = small[row : row + 1, :]
            row += 1
    for ref in (query, key):
        total = jnp.sum(small[row : row + 3, :], axis=0, keepdims=True)
        ref[...] = total[:, :HD] + total[:, HD:]
        row += 3


def per_device(
    tokens,
    image_ids,
    joined_weight,
    hidden_bias,
    mixer_weight,
    dense_weight,
    output_bias,
    norm_gain,
    query_gain,
    key_gain,
    cotangent,
):
    tile_rows, tile_cols, d = tokens.shape
    own = tile_rows * tile_cols
    chip = 2 * own
    ff = dense_weight.shape[0]
    half_ff = ff // 2
    width = d // 2
    row_count, col_count = lax.axis_size("rows"), lax.axis_size("cols")
    fast = (row_count, col_count) == (16, 2)
    row, col = lax.axis_index("rows"), lax.axis_index("cols")
    core, place = row % 2, row // 2

    def pairs(move):
        listed = []
        for i in range(row_count):
            target = move(i // 2, i % 2)
            if 0 <= target[0] < row_count // 2:
                listed.append((i, 2 * target[0] + target[1]))
        return listed

    core_swap = pairs(lambda r, c: (r, 1 - c))
    x_swap = pairs(lambda r, c: (r ^ 1, c))

    def turn(x, by):
        return lax.ppermute(x, "rows", pairs(lambda r, c: ((r + 2 * by) % (row_count // 2), c)))

    def swap(x):
        return lax.ppermute(x, "rows", core_swap)

    def cross_x(x):
        return lax.ppermute(x, "rows", x_swap)

    rightward = [(i, i + 1) for i in range(col_count - 1)]
    leftward = [(i + 1, i) for i in range(col_count - 1)]
    col_swap = rightward + leftward

    def cross_cols(x):
        return lax.ppermute(x, "cols", col_swap)

    if col_count == 2:
        col_moves = [(None, col_swap, None, col_swap)]
    else:
        col_moves = [(0, leftward, 3, rightward), (13, rightward, 0, leftward)]
    edges = tuple(move[0] for move in col_moves)
    places = tuple(move[2] for move in col_moves)

    if fast:
        z, x = place // 2, place % 2
        dests = [2 * (z ^ Z_ORDER[k % 4]) + (x ^ (k // 4)) for k in range(8)]
        side = col
    else:
        dests = [jnp.int32(k) for k in range(8)]
        side = jnp.int32(0)
    sc = jnp.stack([core, side, (col == 0).astype(jnp.int32), place % 2] + dests)
    sc = sc.astype(jnp.int32)

    def swap_rows(a, b):
        odd_swap = pairs(lambda r, c: (r - 1 + 2 * (r % 2), c))
        return cross_x(a), lax.ppermute(b, "rows", odd_swap)

    x_own = tokens.reshape(own, d)
    g_own = cotangent.reshape(own, d)
    x_other, g_other = swap(x_own), swap(g_own)
    ids_other = swap(image_ids)

    gain = norm_gain.reshape(1, d)
    qg, kg = query_gain.reshape(1, HD), key_gain.reshape(1, HD)
    steps = ff // (4 * UNIT)
    edge, part = RADIUS * tile_cols, d // 8
    ext_rows = 2 * tile_rows + 2 * RADIUS
    count, slots, ko_rows, id_rows = 224, 576, ext_rows * tile_cols, 80
    moves = len(col_moves)
    half = (3 * width + half_ff) // 2
    z_rows = part + MIXER_ROWS

    def mixer_block(which):
        return (mixer_weight, (width, d), lambda i, s: ((s[CORE] + which) % 2, 0))

    v = types.SimpleNamespace(g=g_other)
    last = []

    def step(ties, work, kernel, ins, outs, scratch=(), grid=1, token=False):
        given = [entry[0] if isinstance(entry, tuple) else entry for entry in ins]
        wait = [x for x in last + ties if not any(x is y for y in given)]
        if token:
            kernel, outs = functools.partial(with_token, kernel), outs + [out((8, 128), F32)]
        values = call(
            kernel, sc, ins, outs, scratch=scratch, after=wait, grid=grid, work=work * 10**6
        )
        last[:] = values[-1:] if token else values[:1]
        return values[:-1] if token else values

    def sums(ties, work, arrays, plan, dtype=BF):
        shapes = []
        for terms in plan:
            n, k = terms[0]
            shape = arrays[n].shape
            if isinstance(k, slice):
                shape = (len(range(*k.indices(shape[0]))),) + shape[1:]
            elif k is not None:
                shape = shape[1:]
            shapes.append(out(shape, dtype))
        return step(
            ties, work, functools.partial(sum_kernel, plan=plan), arrays, shapes, token=dtype == F32
        )

    def near_z(x):
        return lax.ppermute(x, "rows", pairs(lambda r, c: (r ^ 2, c)))

    def far_z(x):
        return lax.ppermute(x, "rows", pairs(lambda r, c: (r ^ 4, c)))

    def weights(ties, work):
        v.wf, v.bias = step(
            ties,
            work,
            weights_kernel,
            [
                (joined_weight, (d, 4 * UNIT), lambda i, s: (0, 3 + i)),
                (hidden_bias.reshape(1, ff), (1, 4 * UNIT), lambda i, s: (0, i)),
            ],
            [out((d, half_ff)), out((1, half_ff), F32)],
            grid=steps,
        )

    def project(ties, work):
        dense_blocks = dense_weight.reshape(2 * steps, 2, UNIT, d)
        normed, qs, kv, hats, roots, ids, row_a, row_b, wqkv, wd = step(
            ties,
            work,
            project_kernel,
            [x_own, x_other, image_ids, ids_other]
            + [(joined_weight, HBM, None), (dense_blocks, HBM, None), gain, qg, kg],
            [out((chip, d)), out((chip, width)), out((chip, d)), out((chip, d)), out((chip, d))]
            + [out((2 * tile_rows, 128), F32)]
            + [out((edge + 16, d))] * 2
            + [out((d, 3 * width)), out((half_ff, d))],
            scratch=[pltpu.SemaphoreType.DMA((3 + 2 * steps,))],
        )
        vars(v).update(normed=normed, qs=qs, kv=kv, hats=hats, roots=roots, ids=ids, wqkv=wqkv, wd=wd)
        v.row_a, v.row_b = swap_rows(row_a, row_b)

    def cotangent_step(ties, work):
        v.g_all, v.gm, v.gsum = step(
            ties,
            work,
            cotangent_kernel,
            [g_own, g_other, mixer_block(0)],
            [out((chip, d)), out((chip, width)), out((1, d), F32)],
        )

    def hidden(ties, work):
        v.hidden, v.gpre, v.hsum = step(
            ties,
            work,
            hidden_kernel,
            [v.normed, v.g_all, v.wf, v.wd, v.bias],
            [out((chip, half_ff)), out((chip, half_ff)), out((1, half_ff), F32)],
        )

    def extend(ties, work):
        v.ko, v.ids_ext, *msgs = step(
            ties,
            work,
            functools.partial(extend_kernel, edges=edges),
            [v.kv, v.row_a, v.row_b, v.ids],
            [out((ko_rows, d)), out((id_rows, 128), F32)] + [out((count + 16, d))] * moves,
        )
        v.cols = [lax.ppermute(msg, "cols", move[1]) for msg, move in zip(msgs, col_moves)]

    def joined_grad(ties, work):
        v.jf, v.jf_x = step(
            ties,
            work,
            joined_grad_kernel,
            [v.normed, v.gpre],
            [out((4, part, half_ff))] * 2,
            scratch=[pltpu.VMEM((d, half_ff), BF)],
        )
        if fast:
            v.jf_x = cross_x(v.jf_x)

    def dense_grad(ties, work):
        v.near, v.far, v.near_y, v.far_y = step(
            ties,
            work,
            dense_grad_kernel,
            [v.hidden, v.g_all],
            [out((4, UNIT, width))] * 4,
            scratch=[pltpu.VMEM((half_ff, d), BF)],
        )
        if fast:
            v.far_y = cross_cols(v.far_y)

    def slots_step(ties, work):
        v.kh, v.mask = step(
            ties,
            work,
            functools.partial(slots_kernel, places=places),
            v.cols + [v.ids_ext],
            [out((slots, d)), out((chip, KEYS))],
            scratch=[pltpu.VMEM((id_rows, 128), F32)],
        )

    mixed, mixed_other, dq, dko, dkh = [], [], [], [], []

    def attention(pair, ties, work):
        results = step(
            ties,
            work,
            functools.partial(attention_kernel, pair=pair),
            [v.qs, v.gm, v.ko, v.kh, v.mask],
            [out((chip, 128)), out((chip, 128)), out((ko_rows, 256)), out((slots, 256))],
            scratch=[pltpu.VMEM((ko_rows, 256), F32), pltpu.VMEM((slots, 256), F32)],
        )
        for values, value in zip((mixed, dq, dko, dkh), results):
            values.append(value)
        mixed_other.append(swap(results[0]))

    def jf_z1(ties, work):
        halves = [[(0, part), (1, part)] for part in (slice(0, 2), slice(2, 4))]
        first, v.jf = sums(
            ties,
            work, [v.jf, v.jf_x], halves)
        v.jf_z1 = near_z(first)

    def jf_z2(ties, work):
        plan = [[(0, k), (1, k)] for k in range(2)]
        v.jf_0, far = sums(
            ties,
            work, [v.jf, v.jf_z1], plan)
        v.jf_z2 = far_z(far)

    def sum_far(ties, work):
        (far,) = sums(
            ties,
            work, [v.far, v.far_y], [[(0, None), (1, None)]])
        v.far_x = cross_x(far)

    def dense_z1(ties, work):
        arrays = [v.near, v.near_y, v.far_x]
        first = slice(0, 2)
        (first,) = sums(
            ties,
            work, arrays, [[(n, first) for n in range(3)]])
        v.dense_z1 = near_z(first)

    def dense_z2(ties, work):
        arrays = [v.near, v.near_y, v.far_x, v.dense_z1]
        plan = [[(0, 2 + k), (1, 2 + k), (2, 2 + k), (3, k)] for k in range(2)]
        v.dense_0, far = sums(
            ties,
            work, arrays, plan)
        v.dense_z2 = far_z(far)

    def dense_out(ties, work):
        (v.dense_sum,) = sums(
            ties,
            work, [v.dense_0, v.dense_z2], [[(0, None), (1, None)]], F32
        )

    def unslot(ties, work):
        msgs = step(
            ties,
            work,
            functools.partial(unslot_kernel, parts=3, places=places),
            dkh,
            [out((count, d))] * moves,
        )
        v.back = [lax.ppermute(msg, "cols", move[3]) for msg, move in zip(msgs, col_moves)]

    def q_back(ties, work):
        v.gq, v.qsum, v.q, v.q_x = step(
            ties,
            work,
            q_back_kernel,
            dq + [v.hats, v.roots, qg, v.normed],
            [out((chip, width)), out((1, width), F32)] + [out((4, part, width))] * 2,
            scratch=[pltpu.VMEM((d, width), BF)],
        )

    def back_normed(ties, work):
        v.gn, v.gn_other = step(
            ties,
            work,
            back_normed_kernel,
            [v.gpre, v.wf],
            [out((own, d)), out((own, d))],
        )

    def fold(ties, work):
        row_a, row_b, v.dkv, v.q_x = step(
            ties,
            work,
            functools.partial(fold_kernel, parts=3, counts=(3,), edges=edges),
            [v.q_x] + dko + v.back,
            [out((edge, d)), out((edge, d)), out((chip, d)), out((4, part, width))],
        )
        v.back_a, v.back_b = swap_rows(row_a, row_b)
        if fast:
            v.q_x = cross_x(v.q_x)

    def mixer_grad(ties, work):
        v.mixed, v.mixed_other, v.m, v.m_y, v.near_y = step(
            ties,
            work,
            mixer_grad_kernel,
            mixed + mixed_other + [v.g_all, v.near_y],
            [out((chip, width))] * 2 + [out((8, part // 2, width))] * 2 + [out((4, UNIT, width))],
            scratch=[pltpu.VMEM((d, d), BF)],
        )
        if fast:
            v.m_y, v.near_y = cross_cols(v.m_y), cross_cols(v.near_y)

    def sum_m(ties, work):
        terms = (0, 1) if fast else (0,)
        plan = [[(n, part) for n in terms] for part in (slice(0, 4), slice(4, 8))]
        v.m_near, v.m_far = sums(
            ties,
            work, [v.m, v.m_y], plan)

    def kv_back(ties, work):
        v.gkv, v.ksum, v.jkv, v.jkv_a, v.jkv_b = step(
            ties,
            work,
            kv_back_kernel,
            [v.dkv, v.back_a, v.back_b, v.hats, v.roots]
            + [kg, v.normed, v.m_near, v.m_far],
            [out((chip, d)), out((1, width), F32)]
            + [out((n, part + MIXER_ROWS + more, d)) for n, more in ((4, 0), (2, 0), (2, SPARE))],
            scratch=[pltpu.VMEM((d, d), BF)],
        )
        if fast:
            v.jkv_b, v.jkv_a = cross_x(v.jkv_b), cross_x(v.jkv_a)

    def q_z1(ties, work):
        halves = [[(0, half), (1, half)] for half in (slice(0, 2), slice(2, 4))]
        first, v.q = sums(
            ties,
            work, [v.q, v.q_x], halves)
        v.q_z1 = near_z(first)

    def q_z2(ties, work):
        v.q_0, far = sums(
            ties,
            work, [v.q, v.q_z1], [[(0, k), (1, k)] for k in range(2)])
        v.q_z2 = far_z(far)

    def jkv_z1(ties, work):
        (first,) = step(
            ties,
            work,
            z1_kernel,
            [v.jkv, v.jkv_a, v.small, v.hop],
            [out((2 * z_rows + 16, d))],
        )
        v.sent, v.jkv_z1 = first, near_z(first)

    def jkv_z2(ties, work):
        arrays = [v.jkv, v.jkv_b, v.sent, v.jkv_z1]
        v.jkv_0, far = step(
            ties,
            work,
            z2_kernel,
            arrays,
            [out((z_rows, d), F32), out((z_rows + 16, d))],
        )
        v.sent, v.jkv_z2 = far, far_z(far)

    def back_output(ties, work):
        v.p, p_send = step(
            ties,
            work,
            back_output_kernel,
            [v.hidden, v.wd],
            [out((own, d)), out((own, d))],
        )
        v.p_other = swap(p_send)

    def normed_back(ties, work):
        v.gn, gn_send, v.nsum = step(
            ties,
            work,
            normed_back_kernel,
            [v.gq, v.gkv, v.wqkv, v.gn, v.gn_other, v.normed] + [gain],
            [out((own, d)), out((own, d)), out((1, d), F32)],
        )
        v.gn_other = swap(gn_send)

    def result_step(ties, work):
        (v.result,) = step(
            ties,
            work,
            result_kernel,
            [x_own, v.mixed, v.mixed_other, mixer_block(0), mixer_block(1)]
            + [v.p, v.p_other, output_bias.reshape(1, d)],
            [written((own, d))],
            token=True,
        )

    def tokens_step(ties, work):
        (v.tokens_grad,) = step(
            ties,
            work,
            tokens_grad_kernel,
            [x_own, g_own, v.gn, v.gn_other, gain],
            [written((own, d))],
            token=True,
        )

    def pack(ties, work):
        (v.small,) = step(
            ties,
            work,
            pack_kernel,
            [v.hsum, v.gsum, v.nsum, v.qsum, v.ksum],
            [out((8, d), F32)],
            scratch=[pltpu.VMEM((48, 128), F32)],
        )
        if fast:
            v.hop = swap(v.small)

    def unpack(ties, work):
        if not fast:
            v.small = lax.psum(v.small, ("rows", "cols"))
        values = step(
            ties,
            work,
            unpack_kernel,
            [v.small] + ([v.hop] if fast else []),
            [out((1, n), F32) for n in (ff, d, d, HD, HD)],
        )
        v.sums = [value.reshape(-1) for value in values]

    def sides(ties, work):
        arrays = [v.jkv_0, v.sent, v.jkv_z2, v.q_0, v.q_z2, v.jf_0, v.jf_z2]
        v.kept, v.sent, v.mixer_sum = step(
            ties,
            work,
            joined_sides_kernel,
            arrays,
            [out((part, half), F32), out((part + 16, half)), written((part // 2, width), F32)],
        )
        v.sides = cross_cols(v.sent)

    def cores(ties, work):
        v.mine, sent, v.small = step(
            ties,
            work,
            joined_cores_kernel,
            [v.kept, v.sent, v.sides],
            [out((part // 2, half), F32), out((part // 2, half)), out((8, d), F32)],
            scratch=[pltpu.VMEM((part, half), F32)],
        )
        v.cores = swap(sent)
        v.hop = cross_x(v.small)

    def assemble(ties, work):
        (v.joined_sum,) = step(
            ties,
            work, assemble_kernel, [v.mine, v.cores], [written((part // 2, 2 * half), F32)]
        )

    weights([], 5000)
    project([], 5000)
    cotangent_step([], 5000)
    extend([], 5000)
    hidden([], 5000)
    joined_grad([], 5000)
    dense_grad([], 5000)
    slots_step([], 5000)
    attention(0, [], 300)
    attention(1, [], 300)
    attention(2, [mixed_other[0]] if fast else [], 300)
    unslot([mixed_other[1], v.far_y] if fast else [], 1000)
    q_back([mixed_other[2]] if fast else [], 300)
    mixer_grad([], 300)
    if fast:
        jf_z1([], 1000)
    back_normed([], 300)
    fold([], 1000)
    back_output([], 100)
    sum_m([], 100)
    kv_back([], 5000)
    if fast:
        jf_z2([], 1000)
    normed_back([], 5000)
    pack([], 1000)
    if fast:
        q_z1([], 1000)
        sum_far([], 1000)
        jkv_z1([v.jf_z2, v.q_z1], 1000)
        q_z2([], 1000)
        jkv_z2([], 1000)
        dense_z1([], 1000)
        sides([], 5000)
    tokens_step([], 5000)
    if fast:
        dense_z2([], 1000)
    result_step([], 5000)
    if fast:
        cores([], 5000)
        dense_out([], 1000)
        assemble([], 5000)
    unpack([], 5000)

    if not fast:

        def spread_core(x, axis):
            x = jnp.expand_dims(x, axis)
            is_mine = jnp.arange(2).reshape([2 if i == axis else 1 for i in range(x.ndim)]) == core
            return jnp.where(is_mine, x, jnp.zeros_like(x))

        def reduce(x):
            x = lax.psum_scatter(x, "rows", scatter_dimension=0, tiled=True)
            return lax.psum_scatter(x, "cols", scatter_dimension=1, tiled=True).astype(F32)

        def in_order(*arrays):
            return jnp.concatenate(arrays, axis=0)

        near = jnp.concatenate([v.near, v.near_y], axis=2)
        far = jnp.concatenate([v.far, v.far_y], axis=2)
        v.dense_sum = reduce(spread_core(in_order(near, far), 1).reshape(ff, d))
        m = jnp.concatenate([v.m, v.m_y], axis=2)
        v.mixer_sum = reduce(spread_core(m, 1).reshape(d, d))
        jkv = in_order(*[x[:, :part] for x in (v.jkv, v.jkv_a, v.jkv_b)])
        jq = in_order(v.q, v.q_x).reshape(d, 1, width)
        jkv = jkv.reshape(d, 2, width)
        jf = in_order(v.jf, v.jf_x).reshape(d, ff // (2 * UNIT), UNIT)
        qkv = spread_core(jnp.concatenate([jq, jkv], axis=1), 2).reshape(d, 3 * d)
        joined = jnp.concatenate([qkv, spread_core(jf, 2).reshape(d, ff)], axis=1)
        v.joined_sum = reduce(joined)

    hidden_sum, output_sum, gain_sum, query_sum, key_sum = v.sums
    shape = (tile_rows, tile_cols, d)
    return (
        v.result.reshape(shape),
        v.tokens_grad.reshape(shape),
        v.joined_sum,
        hidden_sum,
        v.mixer_sum,
        v.dense_sum,
        output_sum,
        gain_sum,
        query_sum,
        key_sum,
    )


def solution(mesh):
    tiles, everywhere, blocks = P("rows", "cols", None), P(), P("rows", "cols")
    return jax.shard_map(
        per_device,
        mesh=mesh,
        in_specs=(tiles, blocks) + (everywhere,) * 8 + (tiles,),
        out_specs=(tiles, tiles, blocks, P(), blocks, blocks, P(), P(), P(), P()),
        check_vma=False,
    )
```

```python
import functools
import types

import jax
import jax.numpy as jnp
from jax import lax
from jax.experimental import pallas as pl
from jax.experimental.pallas import tpu as pltpu
from jax.sharding import PartitionSpec as P

H = 12
HD = 64
RADIUS = 3
EPSILON = 1e-06
BF = jnp.bfloat16
F32 = jnp.float32
MIB = 1024 * 1024

UNIT = 192
STRIP = 4
KEYS = 256
HALO_SLOTS = 8
MIXER_ROWS = 32
SPARE = 64
GROUP = 8
Z_ORDER = (1, 3, 0, 2)


def mm(a, b, ca=1, cb=0):
    return lax.dot_general(a, b, (((ca,), (cb,)), ((), ())), preferred_element_type=F32)


HBM = "hbm"


def kernel_name(kernel):
    while isinstance(kernel, functools.partial):
        kernel = kernel.args[0] if kernel.args else kernel.func
    return kernel.__name__


def call(kernel, scalars, ins, outs, scratch=(), vmem=16, after=(), grid=1, work=0):
    ins = [entry if isinstance(entry, tuple) else (entry, None, None) for entry in ins]
    outs = [entry if isinstance(entry, tuple) else (entry, None, None) for entry in outs]

    def spec(_, block, index):
        if block is None:
            return pl.BlockSpec(memory_space=pltpu.VMEM)
        return pl.BlockSpec(memory_space=pltpu.HBM) if block == HBM else pl.BlockSpec(block, index)

    def placed(x, block, _):
        return x if block is None else pltpu.with_memory_space_constraint(x, pltpu.HBM)

    def run(sc, *refs):
        kernel(sc, *refs[: len(ins)], *refs[len(ins) + len(after) :])

    run_kernel = pl.pallas_call(
        run,
        name=kernel_name(kernel),
        grid_spec=pltpu.PrefetchScalarGridSpec(
            num_scalar_prefetch=1,
            grid=(grid,),
            in_specs=[spec(*entry) for entry in ins]
            + [pl.BlockSpec(memory_space=pl.ANY)] * len(after),
            out_specs=[spec(*entry) for entry in outs],
            scratch_shapes=list(scratch),
        ),
        out_shape=[entry[0] for entry in outs],
        compiler_params=pltpu.CompilerParams(vmem_limit_bytes=vmem * MIB),
        cost_estimate=pl.CostEstimate(flops=work, bytes_accessed=0, transcendentals=0),
    )
    return list(run_kernel(scalars, *[placed(*entry) for entry in ins], *after))


def out(shape, dtype=BF):
    return jax.ShapeDtypeStruct(shape, dtype)


def written(shape, dtype=BF):
    return (pltpu.HBM(shape, dtype), shape, lambda i, s: (0,) * len(shape))


def with_token(kernel, *refs):
    kernel(*refs[:-1])
    refs[-1][...] = jnp.zeros_like(refs[-1])


def aligned(start, size, unit):
    return pl.ds(pl.multiple_of(start, unit), size)


def head_means(width):
    row = lax.broadcasted_iota(jnp.int32, (width, width), 0)
    col = lax.broadcasted_iota(jnp.int32, (width, width), 1)
    return jnp.where(row // HD == col // HD, 1.0 / HD, 0.0).astype(BF)


def per_head(x, means):
    width = means.shape[0]
    parts = [mm(x[:, j : j + width].astype(BF), means) for j in range(0, x.shape[1], width)]
    return jnp.concatenate(parts, axis=1)


CORE, SIDE, ON_LEFT, ODD, DEST = 0, 1, 2, 3, 4


def weights_kernel(sc, joined, bias, wf, b_out):
    cols = aligned(pl.program_id(0) * 2 * UNIT, 2 * UNIT, 128)
    for core in range(2):

        @pl.when(sc[CORE] == core)
        def _():
            lo, hi = core * UNIT, (2 + core) * UNIT
            w = joined[...]
            wf[:, cols] = jnp.concatenate([w[:, lo : lo + UNIT], w[:, hi : hi + UNIT]], axis=1)
            b = bias[...]
            b_out[:, cols] = jnp.concatenate([b[:, lo : lo + UNIT], b[:, hi : hi + UNIT]], axis=1)


def split_ids(ids):
    high = jnp.floor(ids * (1.0 / 256))
    return [(ids - 256.0 * high).astype(BF), high.astype(BF)]


def joined_ids(low, high):
    return low.astype(F32) + 256.0 * high.astype(F32)


def row_messages(sc, top, bottom):
    odd = sc[ODD] == 1
    return jnp.where(odd, top, bottom), jnp.where(odd, bottom, top)


def project_kernel(
    sc, xo, xt, io, it, joined, dense, gain, qg, kg, normed, qs, kv, hats, roots, ids, row_a, row_b, wqkv, wd, sems
):
    means = head_means(4 * HD)
    own = xo.shape[0]
    width = qs.shape[1]
    heads = width // HD
    copies = []
    for k in range(3):
        cols = aligned((2 * k + sc[CORE]) * width, width, 128)
        copies.append((joined.at[:, cols], wqkv.at[:, k * width : (k + 1) * width]))
    for k in range(dense.shape[0]):
        copies.append((dense.at[k, sc[CORE]], wd.at[k * UNIT : (k + 1) * UNIT, :]))
    copies = [pltpu.make_async_copy(a, b, sems.at[n]) for n, (a, b) in enumerate(copies)]
    for copy in copies:
        copy.start()
    gains = jnp.concatenate([qg[...]] * heads + [kg[...]] * heads, axis=1)
    block = 256
    for half, ref in enumerate((xo, xt)):
        start = (sc[CORE] if half == 0 else 1 - sc[CORE]) * own
        for i in range(own // block):
            x = ref[i * block : (i + 1) * block, :].astype(F32)
            rows = aligned(start + i * block, block, block)
            center = x - jnp.mean(x, axis=1, keepdims=True)
            spread = jnp.mean(center * center, axis=1, keepdims=True)
            n = (center * lax.rsqrt(spread + EPSILON) * gain[...]).astype(BF)
            normed[rows, :] = n
            if half == 0 and i == 0:
                for copy in copies[:3]:
                    copy.wait()
            part = mm(n, wqkv[:, : 2 * width])
            center = part - per_head(part, means)
            root = lax.rsqrt(per_head(center * center, means) + EPSILON)
            hat = center * root
            hats[rows, :] = hat.astype(BF)
            roots[rows, :] = root.astype(BF)
            low = (hat * gains).astype(BF)
            qs[rows, :] = low[:, :width] * jnp.asarray(HD**-0.5, BF)
            values = mm(n, wqkv[:, 2 * width :]).astype(BF)
            for p in range(width // 128):
                kv[rows, 256 * p : 256 * p + 128] = low[:, width + 128 * p : width + 128 * p + 128]
                kv[rows, 256 * p + 128 : 256 * p + 256] = values[:, 128 * p : 128 * p + 128]
    edge, chip = RADIUS * io.shape[1], kv.shape[0]
    row_a[:edge, :], row_b[:edge, :] = row_messages(sc, kv[:edge, :], kv[chip - edge :, :])
    size = io.shape[0]
    for half, ref in enumerate((io, it)):
        start = (sc[CORE] if half == 0 else 1 - sc[CORE]) * size
        value = ref[...].astype(F32) + 1.0
        zeros = jnp.zeros((size, ids.shape[1] - value.shape[1]), F32)
        ids[aligned(start, size, size), :] = jnp.concatenate([value, zeros], axis=1)
    zeros = jnp.zeros((16 - 8, 128), BF)
    id_a, id_b = row_messages(sc, ids[:8, :], ids[2 * size - 8 :, :])
    for ref, values in ((row_a, id_a), (row_b, id_b)):
        ref[edge:, :] = jnp.zeros((16, ref.shape[1]), BF)
        for j, piece in enumerate(split_ids(values)):
            ref[edge:, 128 * j : 128 * j + 128] = jnp.concatenate([piece, zeros], axis=0)
    for copy in copies[3:]:
        copy.wait()


def cotangent_kernel(sc, go, gt, mixer, g_out, gm, gsum):
    own = go.shape[0]
    for half, ref in enumerate((go, gt)):
        start = (sc[CORE] if half == 0 else 1 - sc[CORE]) * own
        rows = aligned(start, own, own)
        g = ref[...]
        g_out[rows, :] = g
        gm[rows, :] = mm(g, mixer[...], 1, 1).astype(BF)
    gsum[...] = jnp.sum(go[...].astype(F32), axis=0, keepdims=True)


def hidden_kernel(sc, n_ref, g_ref, wf, wd, bias, hidden, gpre, hsum):
    wide = wf.shape[1]
    dense = wd[...]
    block = 256
    total = jnp.zeros((1, wide), F32)
    for i in range(n_ref.shape[0] // block):
        rows = slice(i * block, (i + 1) * block)
        pre = mm(n_ref[rows, :], wf[...]) + bias[...]
        gd = mm(g_ref[rows, :], dense, 1, 1)
        a, b = 0.7978845608, 0.044715
        sq = pre * pre
        t = jnp.tanh(a * pre * (1.0 + b * sq))
        half = 0.5 * (1.0 + t)
        hidden[rows, :] = (pre * half).astype(BF)
        slope = half + (0.5 * a) * pre * (1.0 - t * t) * (1.0 + 3.0 * b * sq)
        gp = gd * slope
        gpre[rows, :] = gp.astype(BF)
        total = total + jnp.sum(gp, axis=0, keepdims=True)
    hsum[...] = total


def dense_grad_kernel(sc, h_ref, g_ref, near_keep, far_keep, near_send, far_send, scr):
    wide, d = scr.shape
    step = wide // 3
    half = d // 2
    for j in range(3):
        cols = slice(j * step, (j + 1) * step)
        scr[cols, :] = mm(h_ref[:, cols], g_ref[...], 0, 0).astype(BF)
    mine = aligned(sc[SIDE] * half, half, 128)
    other = aligned((1 - sc[SIDE]) * half, half, 128)
    for rel in range(8):
        rows = aligned(sc[DEST + rel] * UNIT, UNIT, 64)
        keep, send = (near_keep, near_send) if rel < 4 else (far_keep, far_send)
        keep[rel % 4] = scr[rows, mine]
        send[rel % 4] = scr[rows, other]


def scatter_rows(sc, scr, keep, *sends):
    size = scr.shape[0] // 8
    each = 4 // len(sends)
    for rel in range(8):
        block = scr[aligned(sc[DEST + rel] * size, size, 32), :]
        if rel < 4:
            keep[rel, :size, :] = block
        else:
            sends[(rel - 4) // each][(rel - 4) % each, :size, :] = block


def joined_grad_kernel(sc, n_ref, gp_ref, keep, send, scr):
    step = scr.shape[1] // 3
    for j in range(3):
        cols = slice(j * step, (j + 1) * step)
        scr[:, cols] = mm(n_ref[...], gp_ref[:, cols], 0, 0).astype(BF)
    scatter_rows(sc, scr, keep, send)


def back_output_kernel(sc, h_ref, wd, keep, send):
    own = keep.shape[0]
    dense = wd[...]
    keep[...] = mm(h_ref[aligned(sc[CORE] * own, own, own), :], dense).astype(BF)
    send[...] = mm(h_ref[aligned((1 - sc[CORE]) * own, own, own), :], dense).astype(BF)


def back_normed_kernel(sc, gp_ref, wf, keep, send):
    own = keep.shape[0]
    mine, theirs = gp_ref[aligned(sc[CORE] * own, own, own), :], gp_ref[aligned((1 - sc[CORE]) * own, own, own), :]
    keep[...] = mm(mine, wf[...], 1, 1).astype(BF)
    send[...] = mm(theirs, wf[...], 1, 1).astype(BF)


def edge_picks(rows, first, count):
    msg = lax.broadcasted_iota(jnp.int32, (count, rows), 0)
    tok = lax.broadcasted_iota(jnp.int32, (count, rows), 1)
    return jnp.where(tok == msg // 3 * 16 + first + msg % 3, 1.0, 0.0).astype(BF)


def slot_places(count, slots, first):
    slot = lax.broadcasted_iota(jnp.int32, (slots, count), 0)
    msg = lax.broadcasted_iota(jnp.int32, (slots, count), 1)
    return jnp.where(slot == msg // 3 * HALO_SLOTS + first + msg % 3, 1.0, 0.0).astype(BF)


def extend_kernel(sc, *refs, edges):
    kv, row_a, row_b, ids, ko, ids_ext, *msgs = refs
    edge, own = row_a.shape[0] - 16, kv.shape[0]
    top, bottom = row_messages(sc, row_a[...], row_b[...])
    ko[:edge, :] = top[:edge]
    ko[edge : edge + own, :] = kv[...]
    ko[edge + own :, :] = bottom[:edge]
    size = ids.shape[0]
    ids_ext[...] = jnp.zeros_like(ids_ext)
    ids_ext[:RADIUS, :] = joined_ids(top[edge:, :128], top[edge:, 128:256])[8 - RADIUS : 8]
    ids_ext[RADIUS : RADIUS + size, :] = ids[...]
    ids_ext[RADIUS + size : 2 * RADIUS + size, :] = joined_ids(
        bottom[edge:, :128], bottom[edge:, 128:256]
    )[:RADIUS]
    count = msgs[0].shape[0] - 16
    for msg, first in zip(msgs, edges):
        left, right = ids_ext[...], pltpu.roll(ids_ext[...], 128 - 13, 1)
        if first is None:
            shifted = jnp.where(sc[ON_LEFT] == 1, right, left)
            first = 13 * sc[ON_LEFT]
        else:
            shifted = right if first else left
        msg[:count, :] = mm(edge_picks(ko.shape[0], first, count), ko[...]).astype(BF)
        msg[count:, :] = jnp.zeros((16, msg.shape[1]), BF)
        turned = jnp.transpose(shifted)[:8]
        msg[count:, : turned.shape[1]] = jnp.concatenate(split_ids(turned), axis=0)


def slots_kernel(sc, *refs, places):
    moves = len(places)
    msgs, ids_ext, kh, mask, ids = refs[:moves], *refs[moves:]
    count = msgs[0].shape[0] - 16
    total = 0.0
    all_ids = ids_ext[...]
    for msg, first in zip(msgs, places):
        pieces = msg[count:, :128]
        turned = jnp.transpose(joined_ids(pieces[:8], pieces[8:]))[: ids.shape[0]]
        turned = jnp.concatenate(
            [turned[:, :RADIUS], jnp.zeros((ids.shape[0], 128 - RADIUS), F32)], axis=1
        )
        left, right = pltpu.roll(turned, 16, 1), pltpu.roll(turned, 19, 1)
        if first is None:
            all_ids = all_ids + jnp.where(sc[ON_LEFT] == 1, right, left)
            first = 3 * sc[ON_LEFT]
        else:
            all_ids = all_ids + (right if first else left)
        total = total + mm(slot_places(count, kh.shape[0], first), msg[:count, :])
    kh[...] = total.astype(BF)
    ids[...] = all_ids
    write_mask(ids, mask)


def write_mask(ids, bias):
    lane = lax.broadcasted_iota(jnp.int32, (STRIP * 16, KEYS), 1)
    query = lax.broadcasted_iota(jnp.int32, (STRIP * 16, KEYS), 0)
    inner = lane < 160
    halo = lane - 160
    slot = halo % HALO_SLOTS
    key_row = jnp.where(inner, lane // 16, halo // HALO_SLOTS)
    key_col = jnp.where(inner, lane % 16, jnp.where(slot < 3, slot - 3, slot + 13))
    row_gap = key_row - query // 16
    col_gap = key_col - query % 16
    reach = (
        (row_gap >= 0)
        & (row_gap <= 2 * RADIUS)
        & (col_gap >= -RADIUS)
        & (col_gap <= RADIUS)
        & (inner | (slot < 6))
    )
    itself = inner & (row_gap == RADIUS) & (col_gap == 0)
    lane16 = lax.broadcasted_iota(jnp.int32, (16, KEYS), 1)
    window = jnp.zeros((16, KEYS), F32)
    for i in range(STRIP + 2 * RADIUS):
        part = jnp.concatenate(
            [ids[pl.ds(i, 16, stride=STRIP), :], jnp.zeros((16, KEYS - 128), F32)], axis=1
        )
        own = jnp.where(lane16 < 16, part, 0.0)
        side = jnp.where(lane16 >= 16, part, 0.0)
        if i > 0:
            own = pltpu.roll(own, 16 * i, 1)
        side = pltpu.roll(side, 144 + HALO_SLOTS * i, 1)
        window = window + own + side
    for s in range(16):
        row = jnp.broadcast_to(window[s : s + 1, :], (STRIP * 16, KEYS))
        mine = jnp.sum(jnp.where(itself, row, 0.0), axis=1, keepdims=True)
        bias[s * 64 : (s + 1) * 64, :] = jnp.where(reach & (row == mine), 0.0, -1e30).astype(BF)


def attention_kernel(sc, q_ref, gm_ref, ko, kh, bias, mixed, dq, dko_out, dkh_out, dko, dkh, *, pair):
    dko[...] = jnp.zeros_like(dko)
    dkh[...] = jnp.zeros_like(dkh)
    lane = lax.broadcasted_iota(jnp.int32, (64, 128), 1)
    low = lane < HD
    zero = jnp.zeros((64, 128), BF)
    lanes = slice(128 * pair, 128 * pair + 128)
    k_lanes = slice(256 * pair, 256 * pair + 128)
    v_lanes = slice(256 * pair + 128, 256 * pair + 256)

    def both(x):
        return jnp.concatenate([jnp.where(low, x, zero), jnp.where(low, zero, x)], axis=0)

    for first in range(0, 16, GROUP):
        strips = []
        for s in range(first, first + GROUP):
            rows = slice(s * 64, (s + 1) * 64)
            inner = slice(s * 64, s * 64 + 160)
            side = slice(s * 32, s * 32 + 96)
            strips.append((rows, inner, side))
        q2 = [both(q_ref[rows, lanes]) for rows, _, _ in strips]
        gm2 = [both(gm_ref[rows, lanes]) for rows, _, _ in strips]
        k = [jnp.concatenate([ko[i, k_lanes], kh[j, k_lanes]], axis=0) for _, i, j in strips]
        v = [jnp.concatenate([ko[i, v_lanes], kh[j, v_lanes]], axis=0) for _, i, j in strips]
        b = [bias[rows, :].astype(F32) for rows, _, _ in strips]
        scores = [mm(x, y, 1, 1) for x, y in zip(q2, k)]
        dp = [mm(x, y, 1, 1) for x, y in zip(gm2, v)]
        probs = []
        for x, y in zip(scores, b):
            weights = jnp.exp(x + jnp.concatenate([y, y], axis=0))
            probs.append(weights * (1.0 / jnp.sum(weights, axis=1, keepdims=True)))
        ds = []
        for x, y in zip(probs, dp):
            balance = jnp.sum(x * y, axis=1, keepdims=True)
            ds.append((x * (y - balance)).astype(BF))
        probs = [x.astype(BF) for x in probs]
        o = [mm(x, y) for x, y in zip(probs, v)]
        d = [mm(x, y) for x, y in zip(ds, k)]
        dk = [mm(x, y, 0, 0) for x, y in zip(ds, q2)]
        dv = [mm(x, y, 0, 0) for x, y in zip(probs, gm2)]
        for n, (rows, inner, side) in enumerate(strips):
            mixed[rows, :] = jnp.where(low, o[n][:64], o[n][64:]).astype(BF)
            dq[rows, :] = (jnp.where(low, d[n][:64], d[n][64:]) * (HD**-0.5)).astype(BF)
            dko[inner, :128] += dk[n][:160]
            dkh[side, :128] += dk[n][160:]
            dko[inner, 128:] += dv[n][:160]
            dkh[side, 128:] += dv[n][160:]
    dko_out[...] = dko[...].astype(BF)
    dkh_out[...] = dkh[...].astype(BF)


def unslot_kernel(sc, *refs, parts, places):
    dkh, msgs = refs[:parts], refs[parts:]
    for msg, first in zip(msgs, places):
        first = 3 * sc[ON_LEFT] if first is None else first
        places_of = slot_places(msg.shape[0], dkh[0].shape[0], first)
        for p, ref in enumerate(dkh):
            msg[:, 256 * p : 256 * p + 256] = mm(places_of, ref[...], 0, 0).astype(BF)


def fold_kernel(sc, passing, *refs, parts, counts, edges):
    dko, refs = refs[:parts], refs[parts:]
    groups, refs = refs[: len(counts) * len(edges)], refs[len(counts) * len(edges) :]
    row_a, row_b, center, passed = refs
    passed[...] = passing[...]
    rows = dko[0].shape[0]
    edge = row_a.shape[0]
    count = groups[0].shape[0]
    picks = []
    for first in edges:
        picks.append(edge_picks(rows, 13 * sc[ON_LEFT] if first is None else first, count))
    p = 0
    for n, size in enumerate(counts):
        for j in range(size):
            total = dko[p][...].astype(F32)
            for e, pick in enumerate(picks):
                msg = groups[n * len(edges) + e]
                total = total + mm(pick, msg[:, 256 * j : 256 * j + 256], 0, 0)
            lanes = slice(256 * p, 256 * p + 256)
            low = total.astype(BF)
            row_a[:, lanes], row_b[:, lanes] = row_messages(sc, low[:edge], low[rows - edge :])
            center[:, lanes] = low[edge : rows - edge]
            p += 1


def norm_back(grad, hat, root, gains, means):
    u = [gains * x for x in grad]
    mean = [per_head(x, means) for x in u]
    along = [per_head(x * y, means) for x, y in zip(u, hat)]
    back = [
        ((x - m - h * y) * r).astype(BF) for x, m, h, y, r in zip(u, mean, hat, along, root)
    ]
    total = sum(jnp.sum(x * h, axis=0, keepdims=True) for x, h in zip(grad, hat))
    return back, total


def q_back_kernel(sc, dq0, dq1, dq2, hats, roots, qg, n_ref, gj, sums, keep, send, scr):
    means = head_means(2 * HD)
    width = gj.shape[1]
    gains = jnp.concatenate([qg[...]] * (width // HD), axis=1)
    block = 256
    blocks = [slice(i, i + block) for i in range(0, gj.shape[0], block)]
    grad = [
        jnp.concatenate([dq0[rows, :], dq1[rows, :], dq2[rows, :]], axis=1).astype(F32)
        for rows in blocks
    ]
    hat = [hats[rows, :width].astype(F32) for rows in blocks]
    root = [roots[rows, :width].astype(F32) for rows in blocks]
    back, sums[...] = norm_back(grad, hat, root, gains, means)
    for rows, x in zip(blocks, back):
        gj[rows, :] = x
    scr[...] = mm(n_ref[...], jnp.concatenate(back, axis=0), 0, 0).astype(BF)
    scatter_rows(sc, scr, keep, send)


def kv_back_kernel(
    sc, dkv, row_a, row_b, hats, roots, kg, n_ref, m_near, m_far, gj, sums, keep, send_a, send_b, scr
):
    means = head_means(2 * HD)
    tokens = dkv.shape[0]
    edge = row_a.shape[0]
    width = hats.shape[1] // 2
    gains = jnp.concatenate([kg[...]] * (width // HD), axis=1)
    block = 256
    top, bottom = row_messages(sc, row_a[...].astype(F32), row_b[...].astype(F32))
    blocks = [slice(i, i + block) for i in range(0, tokens, block)]
    grads = [dkv[rows, :].astype(F32) for rows in blocks]
    grads[0] = jnp.concatenate([grads[0][:edge] + top, grads[0][edge:]], axis=0)
    grads[-1] = jnp.concatenate([grads[-1][:-edge], grads[-1][-edge:] + bottom], axis=0)

    def lanes(x, shift):
        return jnp.concatenate(
            [x[:, 256 * p + shift : 256 * p + shift + 128] for p in range(width // 128)], axis=1
        )

    grad = [lanes(x, 0) for x in grads]
    values = [lanes(x, 128).astype(BF) for x in grads]
    hat = [hats[rows, width:].astype(F32) for rows in blocks]
    root = [roots[rows, width:].astype(F32) for rows in blocks]
    back, sums[...] = norm_back(grad, hat, root, gains, means)
    for rows, x, y in zip(blocks, back, values):
        gj[rows, :width] = x
        gj[rows, width:] = y
    for j, x in enumerate((back, values)):
        cols = slice(j * width, (j + 1) * width)
        scr[:, cols] = mm(n_ref[...], jnp.concatenate(x, axis=0), 0, 0).astype(BF)
    scatter_rows(sc, scr, keep, send_a, send_b)
    part = scr.shape[0] // 8
    for k in range(4):
        target, n = (send_a, send_b)[k // 2], k % 2
        for ref, place, values in ((keep, k, m_near[k]), (target, n, m_far[k])):
            values = values.astype(F32)
            size = values.shape[0] // 2
            block = jnp.concatenate([values[:size], values[size:]], axis=1)
            rest = jnp.zeros((MIXER_ROWS - size, block.shape[1]), F32)
            ref[place, part : part + MIXER_ROWS, :] = jnp.concatenate([block, rest], axis=0).astype(BF)


def normed_back_kernel(sc, gq, gkv, wqkv, keep_in, send_in, n_ref, gain, keep, send, gsum):
    own = keep.shape[0]
    width = gq.shape[1]
    shares = []
    for start, before, after in ((sc[CORE], keep_in, keep), (1 - sc[CORE], send_in, send)):
        rows = aligned(start * own, own, own)
        total = before[...].astype(F32) + mm(gq[rows, :], wqkv[:, :width], 1, 1)
        total = total + mm(gkv[rows, :], wqkv[:, width:], 1, 1)
        shares.append(jnp.sum(total * n_ref[rows, :].astype(F32), axis=0, keepdims=True))
        after[...] = total.astype(after.dtype)
    gsum[...] = (shares[0] + shares[1]) / gain[...]


def mixer_grad_kernel(sc, m0, m1, m2, o0, o1, o2, g_ref, passing, mixed, other, keep, send, passed, scr):
    passed[...] = passing[...]
    for p, (m, o) in enumerate(((m0, o0), (m1, o1), (m2, o2))):
        mixed[:, 128 * p : 128 * p + 128] = m[...]
        other[:, 128 * p : 128 * p + 128] = o[...]
    width = mixed.shape[1]
    scr[aligned(sc[CORE] * width, width, 128), :] = mm(mixed[...], g_ref[...], 0, 0).astype(BF)
    scr[aligned((1 - sc[CORE]) * width, width, 128), :] = mm(other[...], g_ref[...], 0, 0).astype(BF)
    size = scr.shape[0] // 16
    mine = aligned(sc[SIDE] * width, width, 128)
    theirs = aligned((1 - sc[SIDE]) * width, width, 128)
    for rel in range(8):
        rows = aligned((2 * sc[DEST + rel] + sc[CORE]) * size, size, 16)
        keep[rel] = scr[rows, mine]
        send[rel] = scr[rows, theirs]


def result_kernel(sc, x, mixed, other, mixer_a, mixer_b, keep, received, bias, result):
    own = x.shape[0]
    mine = aligned(sc[CORE] * own, own, own)
    total = x[...].astype(F32) + bias[...] + keep[...].astype(F32) + received[...].astype(F32)
    total = total + mm(mixed[mine, :], mixer_a[...]) + mm(other[mine, :], mixer_b[...])
    result[...] = total.astype(BF)


def tokens_grad_kernel(sc, x_ref, g_ref, keep, received, gain, grad):
    x = x_ref[...].astype(F32)
    gn = keep[...].astype(F32) + received[...].astype(F32)
    center = x - jnp.mean(x, axis=1, keepdims=True)
    rs = lax.rsqrt(jnp.mean(center * center, axis=1, keepdims=True) + EPSILON)
    hat = center * rs
    u = gain[...] * gn
    back = u - jnp.mean(u, axis=1, keepdims=True) - hat * jnp.mean(u * hat, axis=1, keepdims=True)
    grad[...] = (g_ref[...].astype(F32) + back * rs).astype(BF)


def wide_sum(terms):
    total = terms[0].astype(F32)
    for term in terms[1:]:
        total = total + term.astype(F32)
    return total


def sum_kernel(sc, *refs, plan):
    count = len(refs) - len(plan)
    for target, terms in zip(refs[count:], plan):
        values = [refs[n][...] if k is None else refs[n][k] for n, k in terms]
        target[...] = wide_sum(values).astype(target.dtype)


def split(x):
    high = x.astype(BF)
    return jnp.concatenate([high, (x - high.astype(F32)).astype(BF)], axis=0)


def joint(x):
    size = x.shape[0] // 2
    return x[:size].astype(F32) + x[size:].astype(F32)


def z1_kernel(sc, kv, kv_got, small, hop, out_ref):
    size = kv.shape[1]
    for k in range(2):
        out_ref[k * size : (k + 1) * size, :] = wide_sum([kv[k], kv_got[k]]).astype(BF)
    out_ref[2 * size :, :] = split(small[...] + hop[...])


def z2_kernel(sc, kv, kv_got, sent, got, keep, out_ref):
    size = keep.shape[0]
    for k in range(2):
        value = wide_sum([kv[2 + k], kv_got[k, :size, :], got[k * size : (k + 1) * size, :]])
        if k == 0:
            keep[...] = value
        else:
            out_ref[:size, :] = value.astype(BF)
    total = joint(sent[2 * size :, :]) + joint(got[2 * size :, :])
    out_ref[size:, :] = split(total)


def joined_sides_kernel(sc, kv, sent, got, q, q_got, f, f_got, keep, send, mixer):
    rows = kv.shape[0]
    total = kv[...] + got[:rows, :].astype(F32)
    small = joint(sent[rows:, :]) + joint(got[rows:, :])
    part, width = f.shape[0], mixer.shape[1]
    size = mixer.shape[0] // 2
    m = total[part : part + size]
    mixer[...] = jnp.concatenate([m[:, :width], m[:, width:]], axis=0)
    joined = jnp.concatenate(
        [wide_sum([q[...], q_got[...]]), total[:part], wide_sum([f[...], f_got[...]])], axis=1
    )
    half = joined.shape[1] // 2
    small = split(small)
    for side in range(2):

        @pl.when(sc[SIDE] == side)
        def _():
            keep[...] = joined[:, side * half : (side + 1) * half]
            send[:part, :] = joined[:, (1 - side) * half : (2 - side) * half].astype(BF)

    send[part:, :] = jnp.concatenate(
        [small, jnp.zeros((small.shape[0], half - small.shape[1]), BF)], axis=1
    )


def joined_cores_kernel(sc, kept, sent, received, mine, send, small, scr):
    part = kept.shape[0]
    scr[...] = kept[...] + received[:part, :].astype(F32)
    size, wide = mine.shape[0], small.shape[1]
    mine[...] = scr[aligned(sc[CORE] * size, size, 8), :]
    send[...] = scr[aligned((1 - sc[CORE]) * size, size, 8), :].astype(BF)
    small[...] = joint(sent[part:, :wide]) + joint(received[part:, :wide])


def assemble_kernel(sc, mine, theirs, final):
    width = 384
    for core in range(2):
        first, second = (mine, theirs) if core == 0 else (theirs, mine)
        for side in range(2):

            @pl.when((sc[CORE] == core) & (sc[SIDE] == side))
            def _():
                a, b = first[...].astype(F32), second[...].astype(F32)
                size, count = (width, 3) if side == 0 else (UNIT, 7)
                cuts = [slice(j * size, (j + 1) * size) for j in range(count)]
                if side == 0:
                    cuts.append(slice(3 * width, a.shape[1]))
                final[...] = jnp.concatenate([x[:, cut] for cut in cuts for x in (a, b)], axis=1)


def pack_kernel(sc, hsum, gsum, nsum, qsum, ksum, small, scr):
    scr[...] = jnp.zeros_like(scr)
    row = 2 * hsum.shape[1] // 128
    for ref in (gsum, nsum, qsum, ksum):
        for j in range(ref.shape[1] // 128):
            scr[row : row + 1, :] = ref[:, 128 * j : 128 * j + 128]
            row += 1
    count = hsum.shape[1] // 128
    for j in range(count):
        scr[pl.ds(sc[CORE] * count + j, 1), :] = hsum[:, 128 * j : 128 * j + 128]
    small[...] = jnp.concatenate([scr[j : j + 8, :] for j in range(0, 48, 8)], axis=1)


def unpack_kernel(sc, *refs):
    *terms, hidden, output, norm, query, key = refs
    small = wide_sum([ref[...] for ref in terms])
    small = jnp.concatenate([small[:, j : j + 128] for j in range(0, small.shape[1], 128)], axis=0)
    count = hidden.shape[0] // 2
    cores = []
    for core in range(2):
        rows = [small[core * count + j : core * count + j + 1, :] for j in range(count)]
        cores.append(jnp.concatenate(rows, axis=1))
    blocks = []
    for j in range(cores[0].shape[1] // UNIT):
        blocks += [x[:, j * UNIT : (j + 1) * UNIT] for x in cores]
    total = jnp.concatenate(blocks, axis=1)
    for j in range(2 * count):
        hidden[j : j + 1, :] = total[:, 128 * j : 128 * j + 128]
    row = 2 * count
    for ref in (output, norm):
        ref[...] = small[row : row + ref.shape[0], :]
        row += ref.shape[0]
    for ref in (query, key):
        total = jnp.sum(small[row : row + 3, :], axis=0, keepdims=True)
        ref[...] = total[:, :HD] + total[:, HD:]
        row += 3


def per_device(
    tokens,
    image_ids,
    joined_weight,
    hidden_bias,
    mixer_weight,
    dense_weight,
    output_bias,
    norm_gain,
    query_gain,
    key_gain,
    cotangent,
):
    tile_rows, tile_cols, d = tokens.shape
    own = tile_rows * tile_cols
    chip = 2 * own
    ff = dense_weight.shape[0]
    half_ff = ff // 2
    width = d // 2
    row_count, col_count = lax.axis_size("rows"), lax.axis_size("cols")
    fast = (row_count, col_count) == (16, 2)
    row, col = lax.axis_index("rows"), lax.axis_index("cols")
    core, place = row % 2, row // 2

    def pairs(move):
        listed = []
        for i in range(row_count):
            target = move(i // 2, i % 2)
            if 0 <= target[0] < row_count // 2:
                listed.append((i, 2 * target[0] + target[1]))
        return listed

    core_swap = pairs(lambda r, c: (r, 1 - c))
    x_swap = pairs(lambda r, c: (r ^ 1, c))

    def swap(x):
        return lax.ppermute(x, "rows", core_swap)

    def cross_x(x):
        return lax.ppermute(x, "rows", x_swap)

    rightward = [(i, i + 1) for i in range(col_count - 1)]
    leftward = [(i + 1, i) for i in range(col_count - 1)]
    col_swap = rightward + leftward

    def cross_cols(x):
        return lax.ppermute(x, "cols", col_swap)

    if col_count == 2:
        col_moves = [(None, col_swap, None, col_swap)]
    else:
        col_moves = [(0, leftward, 3, rightward), (13, rightward, 0, leftward)]
    edges = tuple(move[0] for move in col_moves)
    places = tuple(move[2] for move in col_moves)

    if fast:
        z, x = place // 2, place % 2
        dests = [2 * (z ^ Z_ORDER[k % 4]) + (x ^ (k // 4)) for k in range(8)]
        side = col
    else:
        dests = [jnp.int32(k) for k in range(8)]
        side = jnp.int32(0)
    sc = jnp.stack([core, side, (col == 0).astype(jnp.int32), place % 2] + dests)
    sc = sc.astype(jnp.int32)

    def swap_rows(a, b):
        odd_swap = pairs(lambda r, c: (r - 1 + 2 * (r % 2), c))
        return cross_x(a), lax.ppermute(b, "rows", odd_swap)

    x_own = tokens.reshape(own, d)
    g_own = cotangent.reshape(own, d)
    x_other, g_other = swap(x_own), swap(g_own)
    ids_other = swap(image_ids)

    gain = norm_gain.reshape(1, d)
    qg, kg = query_gain.reshape(1, HD), key_gain.reshape(1, HD)
    steps = ff // (4 * UNIT)
    edge, part = RADIUS * tile_cols, d // 8
    ext_rows = 2 * tile_rows + 2 * RADIUS
    count, slots, ko_rows, id_rows = 224, 576, ext_rows * tile_cols, 80
    moves = len(col_moves)
    half = (3 * width + half_ff) // 2
    z_rows = part + MIXER_ROWS

    def mixer_block(which):
        return (mixer_weight, (width, d), lambda i, s: ((s[CORE] + which) % 2, 0))

    v = types.SimpleNamespace(g=g_other)
    last = []

    def step(ties, work, kernel, ins, outs, scratch=(), grid=1, token=False):
        given = [entry[0] if isinstance(entry, tuple) else entry for entry in ins]
        wait = [x for x in last + ties if not any(x is y for y in given)]
        if token:
            kernel, outs = functools.partial(with_token, kernel), outs + [out((8, 128), F32)]
        values = call(
            kernel, sc, ins, outs, scratch=scratch, after=wait, grid=grid, work=work * 10**6
        )
        last[:] = values[-1:] if token else values[:1]
        return values[:-1] if token else values

    def sums(ties, work, arrays, plan, dtype=BF):
        shapes = []
        for terms in plan:
            n, k = terms[0]
            shape = arrays[n].shape
            if isinstance(k, slice):
                shape = (len(range(*k.indices(shape[0]))),) + shape[1:]
            elif k is not None:
                shape = shape[1:]
            shapes.append(out(shape, dtype))
        return step(
            ties, work, functools.partial(sum_kernel, plan=plan), arrays, shapes, token=dtype == F32
        )

    def near_z(x):
        return lax.ppermute(x, "rows", pairs(lambda r, c: (r ^ 2, c)))

    def far_z(x):
        return lax.ppermute(x, "rows", pairs(lambda r, c: (r ^ 4, c)))

    def weights(ties, work):
        v.wf, v.bias = step(
            ties,
            work,
            weights_kernel,
            [
                (joined_weight, (d, 4 * UNIT), lambda i, s: (0, 3 + i)),
                (hidden_bias.reshape(1, ff), (1, 4 * UNIT), lambda i, s: (0, i)),
            ],
            [out((d, half_ff)), out((1, half_ff), F32)],
            grid=steps,
        )

    def project(ties, work):
        dense_blocks = dense_weight.reshape(2 * steps, 2, UNIT, d)
        normed, qs, kv, hats, roots, ids, row_a, row_b, wqkv, wd = step(
            ties,
            work,
            project_kernel,
            [x_own, x_other, image_ids, ids_other]
            + [(joined_weight, HBM, None), (dense_blocks, HBM, None), gain, qg, kg],
            [out((chip, d)), out((chip, width)), out((chip, d)), out((chip, d)), out((chip, d))]
            + [out((2 * tile_rows, 128), F32)]
            + [out((edge + 16, d))] * 2
            + [out((d, 3 * width)), out((half_ff, d))],
            scratch=[pltpu.SemaphoreType.DMA((3 + 2 * steps,))],
        )
        vars(v).update(normed=normed, qs=qs, kv=kv, hats=hats, roots=roots, ids=ids, wqkv=wqkv, wd=wd)
        v.row_a, v.row_b = swap_rows(row_a, row_b)

    def cotangent_step(ties, work):
        v.g_all, v.gm, v.gsum = step(
            ties,
            work,
            cotangent_kernel,
            [g_own, g_other, mixer_block(0)],
            [out((chip, d)), out((chip, width)), out((1, d), F32)],
        )

    def hidden(ties, work):
        v.hidden, v.gpre, v.hsum = step(
            ties,
            work,
            hidden_kernel,
            [v.normed, v.g_all, v.wf, v.wd, v.bias],
            [out((chip, half_ff)), out((chip, half_ff)), out((1, half_ff), F32)],
        )

    def extend(ties, work):
        v.ko, v.ids_ext, *msgs = step(
            ties,
            work,
            functools.partial(extend_kernel, edges=edges),
            [v.kv, v.row_a, v.row_b, v.ids],
            [out((ko_rows, d)), out((id_rows, 128), F32)] + [out((count + 16, d))] * moves,
        )
        v.cols = [lax.ppermute(msg, "cols", move[1]) for msg, move in zip(msgs, col_moves)]

    def joined_grad(ties, work):
        v.jf, v.jf_x = step(
            ties,
            work,
            joined_grad_kernel,
            [v.normed, v.gpre],
            [out((4, part, half_ff))] * 2,
            scratch=[pltpu.VMEM((d, half_ff), BF)],
        )
        if fast:
            v.jf_x = cross_x(v.jf_x)

    def dense_grad(ties, work):
        v.near, v.far, v.near_y, v.far_y = step(
            ties,
            work,
            dense_grad_kernel,
            [v.hidden, v.g_all],
            [out((4, UNIT, width))] * 4,
            scratch=[pltpu.VMEM((half_ff, d), BF)],
        )
        if fast:
            v.far_y = cross_cols(v.far_y)

    def slots_step(ties, work):
        v.kh, v.mask = step(
            ties,
            work,
            functools.partial(slots_kernel, places=places),
            v.cols + [v.ids_ext],
            [out((slots, d)), out((chip, KEYS))],
            scratch=[pltpu.VMEM((id_rows, 128), F32)],
        )

    mixed, mixed_other, dq, dko, dkh = [], [], [], [], []

    def attention(pair, ties, work):
        results = step(
            ties,
            work,
            functools.partial(attention_kernel, pair=pair),
            [v.qs, v.gm, v.ko, v.kh, v.mask],
            [out((chip, 128)), out((chip, 128)), out((ko_rows, 256)), out((slots, 256))],
            scratch=[pltpu.VMEM((ko_rows, 256), F32), pltpu.VMEM((slots, 256), F32)],
        )
        for values, value in zip((mixed, dq, dko, dkh), results):
            values.append(value)
        mixed_other.append(swap(results[0]))

    def jf_z1(ties, work):
        halves = [[(0, part), (1, part)] for part in (slice(0, 2), slice(2, 4))]
        first, v.jf = sums(
            ties,
            work, [v.jf, v.jf_x], halves)
        v.jf_z1 = near_z(first)

    def jf_z2(ties, work):
        plan = [[(0, k), (1, k)] for k in range(2)]
        v.jf_0, far = sums(
            ties,
            work, [v.jf, v.jf_z1], plan)
        v.jf_z2 = far_z(far)

    def sum_far(ties, work):
        (far,) = sums(
            ties,
            work, [v.far, v.far_y], [[(0, None), (1, None)]])
        v.far_x = cross_x(far)

    def dense_z1(ties, work):
        arrays = [v.near, v.near_y, v.far_x]
        first = slice(0, 2)
        (first,) = sums(
            ties,
            work, arrays, [[(n, first) for n in range(3)]])
        v.dense_z1 = near_z(first)

    def dense_z2(ties, work):
        arrays = [v.near, v.near_y, v.far_x, v.dense_z1]
        plan = [[(0, 2 + k), (1, 2 + k), (2, 2 + k), (3, k)] for k in range(2)]
        v.dense_0, far = sums(
            ties,
            work, arrays, plan)
        v.dense_z2 = far_z(far)

    def dense_out(ties, work):
        (v.dense_sum,) = sums(
            ties,
            work, [v.dense_0, v.dense_z2], [[(0, None), (1, None)]], F32
        )

    def unslot(ties, work):
        msgs = step(
            ties,
            work,
            functools.partial(unslot_kernel, parts=3, places=places),
            dkh,
            [out((count, d))] * moves,
        )
        v.back = [lax.ppermute(msg, "cols", move[3]) for msg, move in zip(msgs, col_moves)]

    def q_back(ties, work):
        v.gq, v.qsum, v.q, v.q_x = step(
            ties,
            work,
            q_back_kernel,
            dq + [v.hats, v.roots, qg, v.normed],
            [out((chip, width)), out((1, width), F32)] + [out((4, part, width))] * 2,
            scratch=[pltpu.VMEM((d, width), BF)],
        )

    def back_normed(ties, work):
        v.gn, v.gn_other = step(
            ties,
            work,
            back_normed_kernel,
            [v.gpre, v.wf],
            [out((own, d)), out((own, d))],
        )

    def fold(ties, work):
        row_a, row_b, v.dkv, v.q_x = step(
            ties,
            work,
            functools.partial(fold_kernel, parts=3, counts=(3,), edges=edges),
            [v.q_x] + dko + v.back,
            [out((edge, d)), out((edge, d)), out((chip, d)), out((4, part, width))],
        )
        v.back_a, v.back_b = swap_rows(row_a, row_b)
        if fast:
            v.q_x = cross_x(v.q_x)

    def mixer_grad(ties, work):
        v.mixed, v.mixed_other, v.m, v.m_y, v.near_y = step(
            ties,
            work,
            mixer_grad_kernel,
            mixed + mixed_other + [v.g_all, v.near_y],
            [out((chip, width))] * 2 + [out((8, part // 2, width))] * 2 + [out((4, UNIT, width))],
            scratch=[pltpu.VMEM((d, d), BF)],
        )
        if fast:
            v.m_y, v.near_y = cross_cols(v.m_y), cross_cols(v.near_y)

    def sum_m(ties, work):
        terms = (0, 1) if fast else (0,)
        plan = [[(n, part) for n in terms] for part in (slice(0, 4), slice(4, 8))]
        v.m_near, v.m_far = sums(
            ties,
            work, [v.m, v.m_y], plan)

    def kv_back(ties, work):
        v.gkv, v.ksum, v.jkv, v.jkv_a, v.jkv_b = step(
            ties,
            work,
            kv_back_kernel,
            [v.dkv, v.back_a, v.back_b, v.hats, v.roots]
            + [kg, v.normed, v.m_near, v.m_far],
            [out((chip, d)), out((1, width), F32)]
            + [out((n, part + MIXER_ROWS + more, d)) for n, more in ((4, 0), (2, 0), (2, SPARE))],
            scratch=[pltpu.VMEM((d, d), BF)],
        )
        if fast:
            v.jkv_b, v.jkv_a = cross_x(v.jkv_b), cross_x(v.jkv_a)

    def q_z1(ties, work):
        halves = [[(0, half), (1, half)] for half in (slice(0, 2), slice(2, 4))]
        first, v.q = sums(
            ties,
            work, [v.q, v.q_x], halves)
        v.q_z1 = near_z(first)

    def q_z2(ties, work):
        v.q_0, far = sums(
            ties,
            work, [v.q, v.q_z1], [[(0, k), (1, k)] for k in range(2)])
        v.q_z2 = far_z(far)

    def jkv_z1(ties, work):
        (first,) = step(
            ties,
            work,
            z1_kernel,
            [v.jkv, v.jkv_a, v.small, v.hop],
            [out((2 * z_rows + 16, d))],
        )
        v.sent, v.jkv_z1 = first, near_z(first)

    def jkv_z2(ties, work):
        arrays = [v.jkv, v.jkv_b, v.sent, v.jkv_z1]
        v.jkv_0, far = step(
            ties,
            work,
            z2_kernel,
            arrays,
            [out((z_rows, d), F32), out((z_rows + 16, d))],
        )
        v.sent, v.jkv_z2 = far, far_z(far)

    def back_output(ties, work):
        v.p, p_send = step(
            ties,
            work,
            back_output_kernel,
            [v.hidden, v.wd],
            [out((own, d)), out((own, d))],
        )
        v.p_other = swap(p_send)

    def normed_back(ties, work):
        v.gn, gn_send, v.nsum = step(
            ties,
            work,
            normed_back_kernel,
            [v.gq, v.gkv, v.wqkv, v.gn, v.gn_other, v.normed] + [gain],
            [out((own, d)), out((own, d)), out((1, d), F32)],
        )
        v.gn_other = swap(gn_send)

    def result_step(ties, work):
        (v.result,) = step(
            ties,
            work,
            result_kernel,
            [x_own, v.mixed, v.mixed_other, mixer_block(0), mixer_block(1)]
            + [v.p, v.p_other, output_bias.reshape(1, d)],
            [written((own, d))],
            token=True,
        )

    def tokens_step(ties, work):
        (v.tokens_grad,) = step(
            ties,
            work,
            tokens_grad_kernel,
            [x_own, g_own, v.gn, v.gn_other, gain],
            [written((own, d))],
            token=True,
        )

    def pack(ties, work):
        (v.small,) = step(
            ties,
            work,
            pack_kernel,
            [v.hsum, v.gsum, v.nsum, v.qsum, v.ksum],
            [out((8, d), F32)],
            scratch=[pltpu.VMEM((48, 128), F32)],
        )
        if fast:
            v.hop = swap(v.small)

    def unpack(ties, work):
        if not fast:
            v.small = lax.psum(v.small, ("rows", "cols"))
        values = step(
            ties,
            work,
            unpack_kernel,
            [v.small] + ([v.hop] if fast else []),
            [out((n // 128, 128), F32) for n in (ff, d, d)] + [out((1, HD), F32)] * 2,
        )
        v.sums = [value.reshape(-1) for value in values]

    def sides(ties, work):
        arrays = [v.jkv_0, v.sent, v.jkv_z2, v.q_0, v.q_z2, v.jf_0, v.jf_z2]
        v.kept, v.sent, v.mixer_sum = step(
            ties,
            work,
            joined_sides_kernel,
            arrays,
            [out((part, half), F32), out((part + 16, half)), written((part // 2, width), F32)],
        )
        v.sides = cross_cols(v.sent)

    def cores(ties, work):
        v.mine, sent, v.small = step(
            ties,
            work,
            joined_cores_kernel,
            [v.kept, v.sent, v.sides],
            [out((part // 2, half), F32), out((part // 2, half)), out((8, d), F32)],
            scratch=[pltpu.VMEM((part, half), F32)],
        )
        v.cores = swap(sent)
        v.hop = cross_x(v.small)

    def assemble(ties, work):
        (v.joined_sum,) = step(
            ties,
            work,
            assemble_kernel,
            [v.mine, v.cores],
            [written((part // 2, 2 * half), F32)],
            token=True,
        )

    weights([], 5000)
    project([], 5000)
    cotangent_step([], 5000)
    extend([], 5000)
    hidden([], 5000)
    joined_grad([], 5000)
    dense_grad([], 5000)
    slots_step([], 5000)
    attention(0, [], 300)
    attention(1, [], 300)
    attention(2, [mixed_other[0]] if fast else [], 300)
    unslot([v.far_y] if fast else [], 1000)
    q_back([mixed_other[2]] if fast else [], 300)
    mixer_grad([], 300)
    if fast:
        jf_z1([], 1000)
    back_normed([], 300)
    fold([], 1000)
    back_output([], 100)
    sum_m([], 100)
    kv_back([], 5000)
    if fast:
        jf_z2([], 1000)
    normed_back([], 5000)
    pack([], 1000)
    if fast:
        q_z1([], 1000)
        sum_far([], 1000)
        jkv_z1([v.jf_z2, v.q_z1], 1000)
        q_z2([], 1000)
        jkv_z2([v.q_z2], 1000)
        dense_z1([], 1000)
        sides([], 5000)
    tokens_step([], 5000)
    if fast:
        dense_z2([], 1000)
    result_step([], 5000)
    if fast:
        cores([], 5000)
        dense_out([], 1000)
        assemble([], 5000)
    unpack([], 5000)

    if not fast:

        def spread_core(x, axis):
            x = jnp.expand_dims(x, axis)
            is_mine = jnp.arange(2).reshape([2 if i == axis else 1 for i in range(x.ndim)]) == core
            return jnp.where(is_mine, x, jnp.zeros_like(x))

        def reduce(x):
            x = lax.psum_scatter(x, "rows", scatter_dimension=0, tiled=True)
            return lax.psum_scatter(x, "cols", scatter_dimension=1, tiled=True).astype(F32)

        def in_order(*arrays):
            return jnp.concatenate(arrays, axis=0)

        near = jnp.concatenate([v.near, v.near_y], axis=2)
        far = jnp.concatenate([v.far, v.far_y], axis=2)
        v.dense_sum = reduce(spread_core(in_order(near, far), 1).reshape(ff, d))
        m = jnp.concatenate([v.m, v.m_y], axis=2)
        v.mixer_sum = reduce(spread_core(m, 1).reshape(d, d))
        jkv = in_order(*[x[:, :part] for x in (v.jkv, v.jkv_a, v.jkv_b)])
        jq = in_order(v.q, v.q_x).reshape(d, 1, width)
        jkv = jkv.reshape(d, 2, width)
        jf = in_order(v.jf, v.jf_x).reshape(d, ff // (2 * UNIT), UNIT)
        qkv = spread_core(jnp.concatenate([jq, jkv], axis=1), 2).reshape(d, 3 * d)
        joined = jnp.concatenate([qkv, spread_core(jf, 2).reshape(d, ff)], axis=1)
        v.joined_sum = reduce(joined)

    hidden_sum, output_sum, gain_sum, query_sum, key_sum = v.sums
    shape = (tile_rows, tile_cols, d)
    return (
        v.result.reshape(shape),
        v.tokens_grad.reshape(shape),
        v.joined_sum,
        hidden_sum,
        v.mixer_sum,
        v.dense_sum,
        output_sum,
        gain_sum,
        query_sum,
        key_sum,
    )


def solution(mesh):
    tiles, everywhere, blocks = P("rows", "cols", None), P(), P("rows", "cols")
    return jax.shard_map(
        per_device,
        mesh=mesh,
        in_specs=(tiles, blocks) + (everywhere,) * 8 + (tiles,),
        out_specs=(tiles, tiles, blocks, P(), blocks, blocks, P(), P(), P(), P()),
        check_vma=False,
    )
```

```python
import functools
import types

import jax
import jax.numpy as jnp
from jax import lax
from jax.experimental import pallas as pl
from jax.experimental.pallas import tpu as pltpu
from jax.sharding import PartitionSpec as P

H = 12
HD = 64
RADIUS = 3
EPSILON = 1e-06
BF = jnp.bfloat16
F32 = jnp.float32
MIB = 1024 * 1024

UNIT = 192
STRIP = 4
KEYS = 256
HALO_SLOTS = 8
MIXER_ROWS = 32
SPARE = 64
GROUP = 16
Z_ORDER = (1, 3, 0, 2)


def mm(a, b, ca=1, cb=0):
    return lax.dot_general(a, b, (((ca,), (cb,)), ((), ())), preferred_element_type=F32)


HBM = "hbm"


def kernel_name(kernel):
    while isinstance(kernel, functools.partial):
        kernel = kernel.args[0] if kernel.args else kernel.func
    return kernel.__name__


def call(kernel, scalars, ins, outs, scratch=(), vmem=16, after=(), grid=1, work=0):
    ins = [entry if isinstance(entry, tuple) else (entry, None, None) for entry in ins]
    outs = [entry if isinstance(entry, tuple) else (entry, None, None) for entry in outs]

    def spec(_, block, index):
        if block is None:
            return pl.BlockSpec(memory_space=pltpu.VMEM)
        return pl.BlockSpec(memory_space=pltpu.HBM) if block == HBM else pl.BlockSpec(block, index)

    def placed(x, block, _):
        return x if block is None else pltpu.with_memory_space_constraint(x, pltpu.HBM)

    def run(sc, *refs):
        kernel(sc, *refs[: len(ins)], *refs[len(ins) + len(after) :])

    run_kernel = pl.pallas_call(
        run,
        name=kernel_name(kernel),
        grid_spec=pltpu.PrefetchScalarGridSpec(
            num_scalar_prefetch=1,
            grid=(grid,),
            in_specs=[spec(*entry) for entry in ins]
            + [pl.BlockSpec(memory_space=pl.ANY)] * len(after),
            out_specs=[spec(*entry) for entry in outs],
            scratch_shapes=list(scratch),
        ),
        out_shape=[entry[0] for entry in outs],
        compiler_params=pltpu.CompilerParams(vmem_limit_bytes=vmem * MIB),
        cost_estimate=pl.CostEstimate(flops=work, bytes_accessed=0, transcendentals=0),
    )
    return list(run_kernel(scalars, *[placed(*entry) for entry in ins], *after))


def out(shape, dtype=BF):
    return jax.ShapeDtypeStruct(shape, dtype)


def written(shape, dtype=BF):
    return (pltpu.HBM(shape, dtype), shape, lambda i, s: (0,) * len(shape))


def with_token(kernel, *refs):
    kernel(*refs[:-1])
    refs[-1][...] = jnp.zeros_like(refs[-1])


def aligned(start, size, unit):
    return pl.ds(pl.multiple_of(start, unit), size)


def head_means(width):
    row = lax.broadcasted_iota(jnp.int32, (width, width), 0)
    col = lax.broadcasted_iota(jnp.int32, (width, width), 1)
    return jnp.where(row // HD == col // HD, 1.0 / HD, 0.0).astype(BF)


def per_head(x, means):
    width = means.shape[0]
    parts = [mm(x[:, j : j + width].astype(BF), means) for j in range(0, x.shape[1], width)]
    return jnp.concatenate(parts, axis=1)


CORE, SIDE, ON_LEFT, ODD, DEST = 0, 1, 2, 3, 4


def weights_kernel(sc, joined, bias, wf, b_out):
    cols = aligned(pl.program_id(0) * 2 * UNIT, 2 * UNIT, 128)
    for core in range(2):

        @pl.when(sc[CORE] == core)
        def _():
            lo, hi = core * UNIT, (2 + core) * UNIT
            w = joined[...]
            wf[:, cols] = jnp.concatenate([w[:, lo : lo + UNIT], w[:, hi : hi + UNIT]], axis=1)
            b = bias[...]
            b_out[:, cols] = jnp.concatenate([b[:, lo : lo + UNIT], b[:, hi : hi + UNIT]], axis=1)


def split_ids(ids):
    high = jnp.floor(ids * (1.0 / 256))
    return [(ids - 256.0 * high).astype(BF), high.astype(BF)]


def joined_ids(low, high):
    return low.astype(F32) + 256.0 * high.astype(F32)


def row_messages(sc, top, bottom):
    odd = sc[ODD] == 1
    return jnp.where(odd, top, bottom), jnp.where(odd, bottom, top)


def project_kernel(
    sc, xo, xt, io, it, joined, dense, gain, qg, kg, normed, qs, kv, hats, roots, ids, row_a, row_b, wqkv, wd, sems
):
    means = head_means(4 * HD)
    own = xo.shape[0]
    width = qs.shape[1]
    heads = width // HD
    copies = []
    for k in range(3):
        cols = aligned((2 * k + sc[CORE]) * width, width, 128)
        copies.append((joined.at[:, cols], wqkv.at[:, k * width : (k + 1) * width]))
    for k in range(dense.shape[0]):
        copies.append((dense.at[k, sc[CORE]], wd.at[k * UNIT : (k + 1) * UNIT, :]))
    copies = [pltpu.make_async_copy(a, b, sems.at[n]) for n, (a, b) in enumerate(copies)]
    for copy in copies:
        copy.start()
    gains = jnp.concatenate([qg[...]] * heads + [kg[...]] * heads, axis=1)
    block = 256
    for half, ref in enumerate((xo, xt)):
        start = (sc[CORE] if half == 0 else 1 - sc[CORE]) * own
        for i in range(own // block):
            x = ref[i * block : (i + 1) * block, :].astype(F32)
            rows = aligned(start + i * block, block, block)
            center = x - jnp.mean(x, axis=1, keepdims=True)
            spread = jnp.mean(center * center, axis=1, keepdims=True)
            n = (center * lax.rsqrt(spread + EPSILON) * gain[...]).astype(BF)
            normed[rows, :] = n
            if half == 0 and i == 0:
                for copy in copies[:3]:
                    copy.wait()
            part = mm(n, wqkv[:, : 2 * width])
            center = part - per_head(part, means)
            root = lax.rsqrt(per_head(center * center, means) + EPSILON)
            hat = center * root
            hats[rows, :] = hat.astype(BF)
            roots[rows, :] = root.astype(BF)
            low = (hat * gains).astype(BF)
            qs[rows, :] = low[:, :width] * jnp.asarray(HD**-0.5, BF)
            values = mm(n, wqkv[:, 2 * width :]).astype(BF)
            for p in range(width // 128):
                kv[rows, 256 * p : 256 * p + 128] = low[:, width + 128 * p : width + 128 * p + 128]
                kv[rows, 256 * p + 128 : 256 * p + 256] = values[:, 128 * p : 128 * p + 128]
    edge, chip = RADIUS * io.shape[1], kv.shape[0]
    row_a[:edge, :], row_b[:edge, :] = row_messages(sc, kv[:edge, :], kv[chip - edge :, :])
    size = io.shape[0]
    for half, ref in enumerate((io, it)):
        start = (sc[CORE] if half == 0 else 1 - sc[CORE]) * size
        value = ref[...].astype(F32) + 1.0
        zeros = jnp.zeros((size, ids.shape[1] - value.shape[1]), F32)
        ids[aligned(start, size, size), :] = jnp.concatenate([value, zeros], axis=1)
    zeros = jnp.zeros((16 - 8, 128), BF)
    id_a, id_b = row_messages(sc, ids[:8, :], ids[2 * size - 8 :, :])
    for ref, values in ((row_a, id_a), (row_b, id_b)):
        ref[edge:, :] = jnp.zeros((16, ref.shape[1]), BF)
        for j, piece in enumerate(split_ids(values)):
            ref[edge:, 128 * j : 128 * j + 128] = jnp.concatenate([piece, zeros], axis=0)
    for copy in copies[3:]:
        copy.wait()


def cotangent_kernel(sc, go, gt, mixer, g_out, gm, gsum):
    own = go.shape[0]
    for half, ref in enumerate((go, gt)):
        start = (sc[CORE] if half == 0 else 1 - sc[CORE]) * own
        rows = aligned(start, own, own)
        g = ref[...]
        g_out[rows, :] = g
        gm[rows, :] = mm(g, mixer[...], 1, 1).astype(BF)
    gsum[...] = jnp.sum(go[...].astype(F32), axis=0, keepdims=True)


def hidden_kernel(sc, n_ref, g_ref, wf, wd, bias, hidden, gpre, hsum):
    wide = wf.shape[1]
    dense = wd[...]
    block = 256
    total = jnp.zeros((1, wide), F32)
    for i in range(n_ref.shape[0] // block):
        rows = slice(i * block, (i + 1) * block)
        pre = mm(n_ref[rows, :], wf[...]) + bias[...]
        gd = mm(g_ref[rows, :], dense, 1, 1)
        a, b = 0.7978845608, 0.044715
        sq = pre * pre
        t = jnp.tanh(a * pre * (1.0 + b * sq))
        half = 0.5 * (1.0 + t)
        hidden[rows, :] = (pre * half).astype(BF)
        slope = half + (0.5 * a) * pre * (1.0 - t * t) * (1.0 + 3.0 * b * sq)
        gp = gd * slope
        gpre[rows, :] = gp.astype(BF)
        total = total + jnp.sum(gp, axis=0, keepdims=True)
    hsum[...] = total


def dense_grad_kernel(sc, h_ref, g_ref, near_keep, far_keep, near_send, far_send, scr):
    wide, d = scr.shape
    step = wide // 3
    half = d // 2
    for j in range(3):
        cols = slice(j * step, (j + 1) * step)
        scr[cols, :] = mm(h_ref[:, cols], g_ref[...], 0, 0).astype(BF)
    mine = aligned(sc[SIDE] * half, half, 128)
    other = aligned((1 - sc[SIDE]) * half, half, 128)
    for rel in range(8):
        rows = aligned(sc[DEST + rel] * UNIT, UNIT, 64)
        keep, send = (near_keep, near_send) if rel < 4 else (far_keep, far_send)
        keep[rel % 4] = scr[rows, mine]
        send[rel % 4] = scr[rows, other]


def scatter_rows(sc, scr, keep, *sends):
    size = scr.shape[0] // 8
    each = 4 // len(sends)
    for rel in range(8):
        block = scr[aligned(sc[DEST + rel] * size, size, 32), :]
        if rel < 4:
            keep[rel, :size, :] = block
        else:
            sends[(rel - 4) // each][(rel - 4) % each, :size, :] = block


def joined_grad_kernel(sc, n_ref, gp_ref, keep, send, scr):
    step = scr.shape[1] // 3
    for j in range(3):
        cols = slice(j * step, (j + 1) * step)
        scr[:, cols] = mm(n_ref[...], gp_ref[:, cols], 0, 0).astype(BF)
    scatter_rows(sc, scr, keep, send)


def back_output_kernel(sc, h_ref, wd, keep, send):
    own = keep.shape[0]
    dense = wd[...]
    keep[...] = mm(h_ref[aligned(sc[CORE] * own, own, own), :], dense).astype(BF)
    send[...] = mm(h_ref[aligned((1 - sc[CORE]) * own, own, own), :], dense).astype(BF)


def back_normed_kernel(sc, gp_ref, wf, keep, send):
    own = keep.shape[0]
    mine, theirs = gp_ref[aligned(sc[CORE] * own, own, own), :], gp_ref[aligned((1 - sc[CORE]) * own, own, own), :]
    keep[...] = mm(mine, wf[...], 1, 1).astype(BF)
    send[...] = mm(theirs, wf[...], 1, 1).astype(BF)


def edge_picks(rows, first, count):
    msg = lax.broadcasted_iota(jnp.int32, (count, rows), 0)
    tok = lax.broadcasted_iota(jnp.int32, (count, rows), 1)
    return jnp.where(tok == msg // 3 * 16 + first + msg % 3, 1.0, 0.0).astype(BF)


def slot_places(count, slots, first):
    slot = lax.broadcasted_iota(jnp.int32, (slots, count), 0)
    msg = lax.broadcasted_iota(jnp.int32, (slots, count), 1)
    return jnp.where(slot == msg // 3 * HALO_SLOTS + first + msg % 3, 1.0, 0.0).astype(BF)


def extend_kernel(sc, *refs, edges):
    kv, row_a, row_b, ids, ko, ids_ext, *msgs = refs
    edge, own = row_a.shape[0] - 16, kv.shape[0]
    top, bottom = row_messages(sc, row_a[...], row_b[...])
    ko[:edge, :] = top[:edge]
    ko[edge : edge + own, :] = kv[...]
    ko[edge + own :, :] = bottom[:edge]
    size = ids.shape[0]
    ids_ext[...] = jnp.zeros_like(ids_ext)
    ids_ext[:RADIUS, :] = joined_ids(top[edge:, :128], top[edge:, 128:256])[8 - RADIUS : 8]
    ids_ext[RADIUS : RADIUS + size, :] = ids[...]
    ids_ext[RADIUS + size : 2 * RADIUS + size, :] = joined_ids(
        bottom[edge:, :128], bottom[edge:, 128:256]
    )[:RADIUS]
    count = msgs[0].shape[0] - 16
    for msg, first in zip(msgs, edges):
        left, right = ids_ext[...], pltpu.roll(ids_ext[...], 128 - 13, 1)
        if first is None:
            shifted = jnp.where(sc[ON_LEFT] == 1, right, left)
            first = 13 * sc[ON_LEFT]
        else:
            shifted = right if first else left
        msg[:count, :] = mm(edge_picks(ko.shape[0], first, count), ko[...]).astype(BF)
        msg[count:, :] = jnp.zeros((16, msg.shape[1]), BF)
        turned = jnp.transpose(shifted)[:8]
        msg[count:, : turned.shape[1]] = jnp.concatenate(split_ids(turned), axis=0)


def slots_kernel(sc, *refs, places):
    moves = len(places)
    msgs, ids_ext, kh, mask, ids = refs[:moves], *refs[moves:]
    count = msgs[0].shape[0] - 16
    total = 0.0
    all_ids = ids_ext[...]
    for msg, first in zip(msgs, places):
        pieces = msg[count:, :128]
        turned = jnp.transpose(joined_ids(pieces[:8], pieces[8:]))[: ids.shape[0]]
        turned = jnp.concatenate(
            [turned[:, :RADIUS], jnp.zeros((ids.shape[0], 128 - RADIUS), F32)], axis=1
        )
        left, right = pltpu.roll(turned, 16, 1), pltpu.roll(turned, 19, 1)
        if first is None:
            all_ids = all_ids + jnp.where(sc[ON_LEFT] == 1, right, left)
            first = 3 * sc[ON_LEFT]
        else:
            all_ids = all_ids + (right if first else left)
        total = total + mm(slot_places(count, kh.shape[0], first), msg[:count, :])
    kh[...] = total.astype(BF)
    ids[...] = all_ids
    write_mask(ids, mask)


def write_mask(ids, bias):
    lane = lax.broadcasted_iota(jnp.int32, (STRIP * 16, KEYS), 1)
    query = lax.broadcasted_iota(jnp.int32, (STRIP * 16, KEYS), 0)
    inner = lane < 160
    halo = lane - 160
    slot = halo % HALO_SLOTS
    key_row = jnp.where(inner, lane // 16, halo // HALO_SLOTS)
    key_col = jnp.where(inner, lane % 16, jnp.where(slot < 3, slot - 3, slot + 13))
    row_gap = key_row - query // 16
    col_gap = key_col - query % 16
    reach = (
        (row_gap >= 0)
        & (row_gap <= 2 * RADIUS)
        & (col_gap >= -RADIUS)
        & (col_gap <= RADIUS)
        & (inner | (slot < 6))
    )
    itself = inner & (row_gap == RADIUS) & (col_gap == 0)
    lane16 = lax.broadcasted_iota(jnp.int32, (16, KEYS), 1)
    window = jnp.zeros((16, KEYS), F32)
    for i in range(STRIP + 2 * RADIUS):
        part = jnp.concatenate(
            [ids[pl.ds(i, 16, stride=STRIP), :], jnp.zeros((16, KEYS - 128), F32)], axis=1
        )
        own = jnp.where(lane16 < 16, part, 0.0)
        side = jnp.where(lane16 >= 16, part, 0.0)
        if i > 0:
            own = pltpu.roll(own, 16 * i, 1)
        side = pltpu.roll(side, 144 + HALO_SLOTS * i, 1)
        window = window + own + side
    for s in range(16):
        row = jnp.broadcast_to(window[s : s + 1, :], (STRIP * 16, KEYS))
        mine = jnp.sum(jnp.where(itself, row, 0.0), axis=1, keepdims=True)
        bias[s * 64 : (s + 1) * 64, :] = jnp.where(reach & (row == mine), 0.0, -1e30).astype(BF)


def attention_kernel(sc, q_ref, gm_ref, ko, kh, bias, mixed, dq, dko_out, dkh_out, dko, dkh, *, pair):
    dko[...] = jnp.zeros_like(dko)
    dkh[...] = jnp.zeros_like(dkh)
    lane = lax.broadcasted_iota(jnp.int32, (64, 128), 1)
    low = lane < HD
    zero = jnp.zeros((64, 128), BF)
    lanes = slice(128 * pair, 128 * pair + 128)
    k_lanes = slice(256 * pair, 256 * pair + 128)
    v_lanes = slice(256 * pair + 128, 256 * pair + 256)

    def both(x):
        return jnp.concatenate([jnp.where(low, x, zero), jnp.where(low, zero, x)], axis=0)

    for first in range(0, 16, GROUP):
        strips = []
        for s in range(first, first + GROUP):
            rows = slice(s * 64, (s + 1) * 64)
            inner = slice(s * 64, s * 64 + 160)
            side = slice(s * 32, s * 32 + 96)
            strips.append((rows, inner, side))
        q2 = [both(q_ref[rows, lanes]) for rows, _, _ in strips]
        gm2 = [both(gm_ref[rows, lanes]) for rows, _, _ in strips]
        k = [jnp.concatenate([ko[i, k_lanes], kh[j, k_lanes]], axis=0) for _, i, j in strips]
        v = [jnp.concatenate([ko[i, v_lanes], kh[j, v_lanes]], axis=0) for _, i, j in strips]
        b = [bias[rows, :].astype(F32) for rows, _, _ in strips]
        scores = [mm(x, y, 1, 1) for x, y in zip(q2, k)]
        dp = [mm(x, y, 1, 1) for x, y in zip(gm2, v)]
        probs = []
        for x, y in zip(scores, b):
            weights = jnp.exp(x + jnp.concatenate([y, y], axis=0))
            probs.append(weights * (1.0 / jnp.sum(weights, axis=1, keepdims=True)))
        ds = []
        for x, y in zip(probs, dp):
            balance = jnp.sum(x * y, axis=1, keepdims=True)
            ds.append((x * (y - balance)).astype(BF))
        probs = [x.astype(BF) for x in probs]
        o = [mm(x, y) for x, y in zip(probs, v)]
        d = [mm(x, y) for x, y in zip(ds, k)]
        dk = [mm(x, y, 0, 0) for x, y in zip(ds, q2)]
        dv = [mm(x, y, 0, 0) for x, y in zip(probs, gm2)]
        for n, (rows, inner, side) in enumerate(strips):
            mixed[rows, :] = jnp.where(low, o[n][:64], o[n][64:]).astype(BF)
            dq[rows, :] = (jnp.where(low, d[n][:64], d[n][64:]) * (HD**-0.5)).astype(BF)
            dko[inner, :128] += dk[n][:160]
            dkh[side, :128] += dk[n][160:]
            dko[inner, 128:] += dv[n][:160]
            dkh[side, 128:] += dv[n][160:]
    dko_out[...] = dko[...].astype(BF)
    dkh_out[...] = dkh[...].astype(BF)


def unslot_kernel(sc, *refs, parts, places):
    dkh, msgs = refs[:parts], refs[parts:]
    for msg, first in zip(msgs, places):
        first = 3 * sc[ON_LEFT] if first is None else first
        places_of = slot_places(msg.shape[0], dkh[0].shape[0], first)
        for p, ref in enumerate(dkh):
            msg[:, 256 * p : 256 * p + 256] = mm(places_of, ref[...], 0, 0).astype(BF)


def fold_kernel(sc, passing, *refs, parts, counts, edges):
    dko, refs = refs[:parts], refs[parts:]
    groups, refs = refs[: len(counts) * len(edges)], refs[len(counts) * len(edges) :]
    row_a, row_b, center, passed = refs
    passed[...] = passing[...]
    rows = dko[0].shape[0]
    edge = row_a.shape[0]
    count = groups[0].shape[0]
    picks = []
    for first in edges:
        picks.append(edge_picks(rows, 13 * sc[ON_LEFT] if first is None else first, count))
    p = 0
    for n, size in enumerate(counts):
        for j in range(size):
            total = dko[p][...].astype(F32)
            for e, pick in enumerate(picks):
                msg = groups[n * len(edges) + e]
                total = total + mm(pick, msg[:, 256 * j : 256 * j + 256], 0, 0)
            lanes = slice(256 * p, 256 * p + 256)
            low = total.astype(BF)
            row_a[:, lanes], row_b[:, lanes] = row_messages(sc, low[:edge], low[rows - edge :])
            center[:, lanes] = low[edge : rows - edge]
            p += 1


def norm_back(grad, hat, root, gains, means):
    u = [gains * x for x in grad]
    mean = [per_head(x, means) for x in u]
    along = [per_head(x * y, means) for x, y in zip(u, hat)]
    back = [
        ((x - m - h * y) * r).astype(BF) for x, m, h, y, r in zip(u, mean, hat, along, root)
    ]
    total = sum(jnp.sum(x * h, axis=0, keepdims=True) for x, h in zip(grad, hat))
    return back, total


def q_back_kernel(sc, dq0, dq1, dq2, hats, roots, qg, n_ref, gj, sums, keep, send, scr):
    means = head_means(2 * HD)
    width = gj.shape[1]
    gains = jnp.concatenate([qg[...]] * (width // HD), axis=1)
    block = 256
    blocks = [slice(i, i + block) for i in range(0, gj.shape[0], block)]
    grad = [
        jnp.concatenate([dq0[rows, :], dq1[rows, :], dq2[rows, :]], axis=1).astype(F32)
        for rows in blocks
    ]
    hat = [hats[rows, :width].astype(F32) for rows in blocks]
    root = [roots[rows, :width].astype(F32) for rows in blocks]
    back, sums[...] = norm_back(grad, hat, root, gains, means)
    for rows, x in zip(blocks, back):
        gj[rows, :] = x
    scr[...] = mm(n_ref[...], jnp.concatenate(back, axis=0), 0, 0).astype(BF)
    scatter_rows(sc, scr, keep, send)


def kv_back_kernel(
    sc, dkv, row_a, row_b, hats, roots, kg, n_ref, m_near, m_far, gj, sums, keep, send_a, send_b, scr
):
    means = head_means(2 * HD)
    tokens = dkv.shape[0]
    edge = row_a.shape[0]
    width = hats.shape[1] // 2
    gains = jnp.concatenate([kg[...]] * (width // HD), axis=1)
    block = 256
    top, bottom = row_messages(sc, row_a[...].astype(F32), row_b[...].astype(F32))
    blocks = [slice(i, i + block) for i in range(0, tokens, block)]
    grads = [dkv[rows, :].astype(F32) for rows in blocks]
    grads[0] = jnp.concatenate([grads[0][:edge] + top, grads[0][edge:]], axis=0)
    grads[-1] = jnp.concatenate([grads[-1][:-edge], grads[-1][-edge:] + bottom], axis=0)

    def lanes(x, shift):
        return jnp.concatenate(
            [x[:, 256 * p + shift : 256 * p + shift + 128] for p in range(width // 128)], axis=1
        )

    grad = [lanes(x, 0) for x in grads]
    values = [lanes(x, 128).astype(BF) for x in grads]
    hat = [hats[rows, width:].astype(F32) for rows in blocks]
    root = [roots[rows, width:].astype(F32) for rows in blocks]
    back, sums[...] = norm_back(grad, hat, root, gains, means)
    for rows, x, y in zip(blocks, back, values):
        gj[rows, :width] = x
        gj[rows, width:] = y
    for j, x in enumerate((back, values)):
        cols = slice(j * width, (j + 1) * width)
        scr[:, cols] = mm(n_ref[...], jnp.concatenate(x, axis=0), 0, 0).astype(BF)
    scatter_rows(sc, scr, keep, send_a, send_b)
    part = scr.shape[0] // 8
    for k in range(4):
        target, n = (send_a, send_b)[k // 2], k % 2
        for ref, place, values in ((keep, k, m_near[k]), (target, n, m_far[k])):
            values = values.astype(F32)
            size = values.shape[0] // 2
            block = jnp.concatenate([values[:size], values[size:]], axis=1)
            rest = jnp.zeros((MIXER_ROWS - size, block.shape[1]), F32)
            ref[place, part : part + MIXER_ROWS, :] = jnp.concatenate([block, rest], axis=0).astype(BF)


def normed_back_kernel(sc, gq, gkv, wqkv, keep_in, send_in, n_ref, gain, keep, send, gsum):
    own = keep.shape[0]
    width = gq.shape[1]
    shares = []
    for start, before, after in ((sc[CORE], keep_in, keep), (1 - sc[CORE], send_in, send)):
        rows = aligned(start * own, own, own)
        total = before[...].astype(F32) + mm(gq[rows, :], wqkv[:, :width], 1, 1)
        total = total + mm(gkv[rows, :], wqkv[:, width:], 1, 1)
        shares.append(jnp.sum(total * n_ref[rows, :].astype(F32), axis=0, keepdims=True))
        after[...] = total.astype(after.dtype)
    gsum[...] = (shares[0] + shares[1]) / gain[...]


def mixer_grad_kernel(sc, m0, m1, m2, o0, o1, o2, g_ref, passing, mixed, other, keep, send, passed, scr):
    passed[...] = passing[...]
    for p, (m, o) in enumerate(((m0, o0), (m1, o1), (m2, o2))):
        mixed[:, 128 * p : 128 * p + 128] = m[...]
        other[:, 128 * p : 128 * p + 128] = o[...]
    width = mixed.shape[1]
    scr[aligned(sc[CORE] * width, width, 128), :] = mm(mixed[...], g_ref[...], 0, 0).astype(BF)
    scr[aligned((1 - sc[CORE]) * width, width, 128), :] = mm(other[...], g_ref[...], 0, 0).astype(BF)
    size = scr.shape[0] // 16
    mine = aligned(sc[SIDE] * width, width, 128)
    theirs = aligned((1 - sc[SIDE]) * width, width, 128)
    for rel in range(8):
        rows = aligned((2 * sc[DEST + rel] + sc[CORE]) * size, size, 16)
        keep[rel] = scr[rows, mine]
        send[rel] = scr[rows, theirs]


def result_kernel(sc, x, mixed, other, mixer_a, mixer_b, keep, received, bias, result):
    own = x.shape[0]
    mine = aligned(sc[CORE] * own, own, own)
    total = x[...].astype(F32) + bias[...] + keep[...].astype(F32) + received[...].astype(F32)
    total = total + mm(mixed[mine, :], mixer_a[...]) + mm(other[mine, :], mixer_b[...])
    result[...] = total.astype(BF)


def tokens_grad_kernel(sc, x_ref, g_ref, keep, received, gain, grad):
    x = x_ref[...].astype(F32)
    gn = keep[...].astype(F32) + received[...].astype(F32)
    center = x - jnp.mean(x, axis=1, keepdims=True)
    rs = lax.rsqrt(jnp.mean(center * center, axis=1, keepdims=True) + EPSILON)
    hat = center * rs
    u = gain[...] * gn
    back = u - jnp.mean(u, axis=1, keepdims=True) - hat * jnp.mean(u * hat, axis=1, keepdims=True)
    grad[...] = (g_ref[...].astype(F32) + back * rs).astype(BF)


def wide_sum(terms):
    total = terms[0].astype(F32)
    for term in terms[1:]:
        total = total + term.astype(F32)
    return total


def sum_kernel(sc, *refs, plan):
    count = len(refs) - len(plan)
    for target, terms in zip(refs[count:], plan):
        values = [refs[n][...] if k is None else refs[n][k] for n, k in terms]
        target[...] = wide_sum(values).astype(target.dtype)


def split(x):
    high = x.astype(BF)
    return jnp.concatenate([high, (x - high.astype(F32)).astype(BF)], axis=0)


def joint(x):
    size = x.shape[0] // 2
    return x[:size].astype(F32) + x[size:].astype(F32)


def z1_kernel(sc, kv, kv_got, small, hop, out_ref):
    size = kv.shape[1]
    for k in range(2):
        out_ref[k * size : (k + 1) * size, :] = wide_sum([kv[k], kv_got[k]]).astype(BF)
    out_ref[2 * size :, :] = split(small[...] + hop[...])


def z2_kernel(sc, kv, kv_got, sent, got, keep, out_ref):
    size = keep.shape[0]
    for k in range(2):
        value = wide_sum([kv[2 + k], kv_got[k, :size, :], got[k * size : (k + 1) * size, :]])
        if k == 0:
            keep[...] = value
        else:
            out_ref[:size, :] = value.astype(BF)
    total = joint(sent[2 * size :, :]) + joint(got[2 * size :, :])
    out_ref[size:, :] = split(total)


def joined_sides_kernel(sc, kv, sent, got, q, q_got, f, f_got, keep, send, mixer):
    rows = kv.shape[0]
    total = kv[...] + got[:rows, :].astype(F32)
    small = joint(sent[rows:, :]) + joint(got[rows:, :])
    part, width = f.shape[0], mixer.shape[1]
    size = mixer.shape[0] // 2
    m = total[part : part + size]
    mixer[...] = jnp.concatenate([m[:, :width], m[:, width:]], axis=0)
    joined = jnp.concatenate(
        [wide_sum([q[...], q_got[...]]), total[:part], wide_sum([f[...], f_got[...]])], axis=1
    )
    half = joined.shape[1] // 2
    small = split(small)
    for side in range(2):

        @pl.when(sc[SIDE] == side)
        def _():
            keep[...] = joined[:, side * half : (side + 1) * half]
            send[:part, :] = joined[:, (1 - side) * half : (2 - side) * half].astype(BF)

    send[part:, :] = jnp.concatenate(
        [small, jnp.zeros((small.shape[0], half - small.shape[1]), BF)], axis=1
    )


def joined_cores_kernel(sc, kept, sent, received, mine, send, small, scr):
    part = kept.shape[0]
    scr[...] = kept[...] + received[:part, :].astype(F32)
    size, wide = mine.shape[0], small.shape[1]
    mine[...] = scr[aligned(sc[CORE] * size, size, 8), :]
    send[...] = scr[aligned((1 - sc[CORE]) * size, size, 8), :].astype(BF)
    small[...] = joint(sent[part:, :wide]) + joint(received[part:, :wide])


def assemble_kernel(sc, mine, theirs, final):
    width = 384
    for core in range(2):
        first, second = (mine, theirs) if core == 0 else (theirs, mine)
        for side in range(2):

            @pl.when((sc[CORE] == core) & (sc[SIDE] == side))
            def _():
                a, b = first[...].astype(F32), second[...].astype(F32)
                size, count = (width, 3) if side == 0 else (UNIT, 7)
                cuts = [slice(j * size, (j + 1) * size) for j in range(count)]
                if side == 0:
                    cuts.append(slice(3 * width, a.shape[1]))
                final[...] = jnp.concatenate([x[:, cut] for cut in cuts for x in (a, b)], axis=1)


def pack_kernel(sc, hsum, gsum, nsum, qsum, ksum, small, scr):
    scr[...] = jnp.zeros_like(scr)
    row = 2 * hsum.shape[1] // 128
    for ref in (gsum, nsum, qsum, ksum):
        for j in range(ref.shape[1] // 128):
            scr[row : row + 1, :] = ref[:, 128 * j : 128 * j + 128]
            row += 1
    count = hsum.shape[1] // 128
    for j in range(count):
        scr[pl.ds(sc[CORE] * count + j, 1), :] = hsum[:, 128 * j : 128 * j + 128]
    small[...] = jnp.concatenate([scr[j : j + 8, :] for j in range(0, 48, 8)], axis=1)


def unpack_kernel(sc, *refs):
    *terms, hidden, output, norm, query, key = refs
    small = wide_sum([ref[...] for ref in terms])
    small = jnp.concatenate([small[:, j : j + 128] for j in range(0, small.shape[1], 128)], axis=0)
    count = hidden.shape[0] // 2
    cores = []
    for core in range(2):
        rows = [small[core * count + j : core * count + j + 1, :] for j in range(count)]
        cores.append(jnp.concatenate(rows, axis=1))
    blocks = []
    for j in range(cores[0].shape[1] // UNIT):
        blocks += [x[:, j * UNIT : (j + 1) * UNIT] for x in cores]
    total = jnp.concatenate(blocks, axis=1)
    for j in range(2 * count):
        hidden[j : j + 1, :] = total[:, 128 * j : 128 * j + 128]
    row = 2 * count
    for ref in (output, norm):
        ref[...] = small[row : row + ref.shape[0], :]
        row += ref.shape[0]
    for ref in (query, key):
        total = jnp.sum(small[row : row + 3, :], axis=0, keepdims=True)
        ref[...] = total[:, :HD] + total[:, HD:]
        row += 3


def per_device(
    tokens,
    image_ids,
    joined_weight,
    hidden_bias,
    mixer_weight,
    dense_weight,
    output_bias,
    norm_gain,
    query_gain,
    key_gain,
    cotangent,
):
    tile_rows, tile_cols, d = tokens.shape
    own = tile_rows * tile_cols
    chip = 2 * own
    ff = dense_weight.shape[0]
    half_ff = ff // 2
    width = d // 2
    row_count, col_count = lax.axis_size("rows"), lax.axis_size("cols")
    fast = (row_count, col_count) == (16, 2)
    row, col = lax.axis_index("rows"), lax.axis_index("cols")
    core, place = row % 2, row // 2

    def pairs(move):
        listed = []
        for i in range(row_count):
            target = move(i // 2, i % 2)
            if 0 <= target[0] < row_count // 2:
                listed.append((i, 2 * target[0] + target[1]))
        return listed

    core_swap = pairs(lambda r, c: (r, 1 - c))
    x_swap = pairs(lambda r, c: (r ^ 1, c))

    def swap(x):
        return lax.ppermute(x, "rows", core_swap)

    def cross_x(x):
        return lax.ppermute(x, "rows", x_swap)

    rightward = [(i, i + 1) for i in range(col_count - 1)]
    leftward = [(i + 1, i) for i in range(col_count - 1)]
    col_swap = rightward + leftward

    def cross_cols(x):
        return lax.ppermute(x, "cols", col_swap)

    if col_count == 2:
        col_moves = [(None, col_swap, None, col_swap)]
    else:
        col_moves = [(0, leftward, 3, rightward), (13, rightward, 0, leftward)]
    edges = tuple(move[0] for move in col_moves)
    places = tuple(move[2] for move in col_moves)

    if fast:
        z, x = place // 2, place % 2
        dests = [2 * (z ^ Z_ORDER[k % 4]) + (x ^ (k // 4)) for k in range(8)]
        side = col
    else:
        dests = [jnp.int32(k) for k in range(8)]
        side = jnp.int32(0)
    sc = jnp.stack([core, side, (col == 0).astype(jnp.int32), place % 2] + dests)
    sc = sc.astype(jnp.int32)

    def swap_rows(a, b):
        odd_swap = pairs(lambda r, c: (r - 1 + 2 * (r % 2), c))
        return cross_x(a), lax.ppermute(b, "rows", odd_swap)

    x_own = tokens.reshape(own, d)
    g_own = cotangent.reshape(own, d)
    x_other, g_other = swap(x_own), swap(g_own)
    ids_other = swap(image_ids)

    gain = norm_gain.reshape(1, d)
    qg, kg = query_gain.reshape(1, HD), key_gain.reshape(1, HD)
    steps = ff // (4 * UNIT)
    edge, part = RADIUS * tile_cols, d // 8
    ext_rows = 2 * tile_rows + 2 * RADIUS
    count, slots, ko_rows, id_rows = 224, 576, ext_rows * tile_cols, 80
    moves = len(col_moves)
    half = (3 * width + half_ff) // 2
    z_rows = part + MIXER_ROWS

    def mixer_block(which):
        return (mixer_weight, (width, d), lambda i, s: ((s[CORE] + which) % 2, 0))

    v = types.SimpleNamespace(g=g_other)
    last = []

    def step(ties, work, kernel, ins, outs, scratch=(), grid=1, token=False):
        given = [entry[0] if isinstance(entry, tuple) else entry for entry in ins]
        wait = [x for x in last + ties if not any(x is y for y in given)]
        if token:
            kernel, outs = functools.partial(with_token, kernel), outs + [out((8, 128), F32)]
        values = call(
            kernel, sc, ins, outs, scratch=scratch, after=wait, grid=grid, work=work * 10**6
        )
        last[:] = values[-1:] if token else values[:1]
        return values[:-1] if token else values

    def sums(ties, work, arrays, plan, dtype=BF):
        shapes = []
        for terms in plan:
            n, k = terms[0]
            shape = arrays[n].shape
            if isinstance(k, slice):
                shape = (len(range(*k.indices(shape[0]))),) + shape[1:]
            elif k is not None:
                shape = shape[1:]
            shapes.append(out(shape, dtype))
        return step(
            ties, work, functools.partial(sum_kernel, plan=plan), arrays, shapes, token=dtype == F32
        )

    def near_z(x):
        return lax.ppermute(x, "rows", pairs(lambda r, c: (r ^ 2, c)))

    def far_z(x):
        return lax.ppermute(x, "rows", pairs(lambda r, c: (r ^ 4, c)))

    def weights(ties, work):
        v.wf, v.bias = step(
            ties,
            work,
            weights_kernel,
            [
                (joined_weight, (d, 4 * UNIT), lambda i, s: (0, 3 + i)),
                (hidden_bias.reshape(1, ff), (1, 4 * UNIT), lambda i, s: (0, i)),
            ],
            [out((d, half_ff)), out((1, half_ff), F32)],
            grid=steps,
        )

    def project(ties, work):
        dense_blocks = dense_weight.reshape(2 * steps, 2, UNIT, d)
        normed, qs, kv, hats, roots, ids, row_a, row_b, wqkv, wd = step(
            ties,
            work,
            project_kernel,
            [x_own, x_other, image_ids, ids_other]
            + [(joined_weight, HBM, None), (dense_blocks, HBM, None), gain, qg, kg],
            [out((chip, d)), out((chip, width)), out((chip, d)), out((chip, d)), out((chip, d))]
            + [out((2 * tile_rows, 128), F32)]
            + [out((edge + 16, d))] * 2
            + [out((d, 3 * width)), out((half_ff, d))],
            scratch=[pltpu.SemaphoreType.DMA((3 + 2 * steps,))],
        )
        vars(v).update(normed=normed, qs=qs, kv=kv, hats=hats, roots=roots, ids=ids, wqkv=wqkv, wd=wd)
        v.row_a, v.row_b = swap_rows(row_a, row_b)

    def cotangent_step(ties, work):
        v.g_all, v.gm, v.gsum = step(
            ties,
            work,
            cotangent_kernel,
            [g_own, g_other, mixer_block(0)],
            [out((chip, d)), out((chip, width)), out((1, d), F32)],
        )

    def hidden(ties, work):
        v.hidden, v.gpre, v.hsum = step(
            ties,
            work,
            hidden_kernel,
            [v.normed, v.g_all, v.wf, v.wd, v.bias],
            [out((chip, half_ff)), out((chip, half_ff)), out((1, half_ff), F32)],
        )

    def extend(ties, work):
        v.ko, v.ids_ext, *msgs = step(
            ties,
            work,
            functools.partial(extend_kernel, edges=edges),
            [v.kv, v.row_a, v.row_b, v.ids],
            [out((ko_rows, d)), out((id_rows, 128), F32)] + [out((count + 16, d))] * moves,
        )
        v.cols = [lax.ppermute(msg, "cols", move[1]) for msg, move in zip(msgs, col_moves)]

    def joined_grad(ties, work):
        v.jf, v.jf_x = step(
            ties,
            work,
            joined_grad_kernel,
            [v.normed, v.gpre],
            [out((4, part, half_ff))] * 2,
            scratch=[pltpu.VMEM((d, half_ff), BF)],
        )
        if fast:
            v.jf_x = cross_x(v.jf_x)

    def dense_grad(ties, work):
        v.near, v.far, v.near_y, v.far_y = step(
            ties,
            work,
            dense_grad_kernel,
            [v.hidden, v.g_all],
            [out((4, UNIT, width))] * 4,
            scratch=[pltpu.VMEM((half_ff, d), BF)],
        )
        if fast:
            v.far_y = cross_cols(v.far_y)

    def slots_step(ties, work):
        v.kh, v.mask = step(
            ties,
            work,
            functools.partial(slots_kernel, places=places),
            v.cols + [v.ids_ext],
            [out((slots, d)), out((chip, KEYS))],
            scratch=[pltpu.VMEM((id_rows, 128), F32)],
        )

    mixed, mixed_other, dq, dko, dkh = [], [], [], [], []

    def attention(pair, ties, work):
        results = step(
            ties,
            work,
            functools.partial(attention_kernel, pair=pair),
            [v.qs, v.gm, v.ko, v.kh, v.mask],
            [out((chip, 128)), out((chip, 128)), out((ko_rows, 256)), out((slots, 256))],
            scratch=[pltpu.VMEM((ko_rows, 256), F32), pltpu.VMEM((slots, 256), F32)],
        )
        for values, value in zip((mixed, dq, dko, dkh), results):
            values.append(value)
        mixed_other.append(swap(results[0]))

    def jf_z1(ties, work):
        halves = [[(0, part), (1, part)] for part in (slice(0, 2), slice(2, 4))]
        first, v.jf = sums(
            ties,
            work, [v.jf, v.jf_x], halves)
        v.jf_z1 = near_z(first)

    def jf_z2(ties, work):
        plan = [[(0, k), (1, k)] for k in range(2)]
        v.jf_0, far = sums(
            ties,
            work, [v.jf, v.jf_z1], plan)
        v.jf_z2 = far_z(far)

    def sum_far(ties, work):
        (far,) = sums(
            ties,
            work, [v.far, v.far_y], [[(0, None), (1, None)]])
        v.far_x = cross_x(far)

    def dense_z1(ties, work):
        arrays = [v.near, v.near_y, v.far_x]
        first = slice(0, 2)
        (first,) = sums(
            ties,
            work, arrays, [[(n, first) for n in range(3)]])
        v.dense_z1 = near_z(first)

    def dense_z2(ties, work):
        arrays = [v.near, v.near_y, v.far_x, v.dense_z1]
        plan = [[(0, 2 + k), (1, 2 + k), (2, 2 + k), (3, k)] for k in range(2)]
        v.dense_0, far = sums(
            ties,
            work, arrays, plan)
        v.dense_z2 = far_z(far)

    def dense_out(ties, work):
        (v.dense_sum,) = sums(
            ties,
            work, [v.dense_0, v.dense_z2], [[(0, None), (1, None)]], F32
        )

    def unslot(ties, work):
        msgs = step(
            ties,
            work,
            functools.partial(unslot_kernel, parts=3, places=places),
            dkh,
            [out((count, d))] * moves,
        )
        v.back = [lax.ppermute(msg, "cols", move[3]) for msg, move in zip(msgs, col_moves)]

    def q_back(ties, work):
        v.gq, v.qsum, v.q, v.q_x = step(
            ties,
            work,
            q_back_kernel,
            dq + [v.hats, v.roots, qg, v.normed],
            [out((chip, width)), out((1, width), F32)] + [out((4, part, width))] * 2,
            scratch=[pltpu.VMEM((d, width), BF)],
        )

    def back_normed(ties, work):
        v.gn, v.gn_other = step(
            ties,
            work,
            back_normed_kernel,
            [v.gpre, v.wf],
            [out((own, d)), out((own, d))],
        )

    def fold(ties, work):
        row_a, row_b, v.dkv, v.q_x = step(
            ties,
            work,
            functools.partial(fold_kernel, parts=3, counts=(3,), edges=edges),
            [v.q_x] + dko + v.back,
            [out((edge, d)), out((edge, d)), out((chip, d)), out((4, part, width))],
        )
        v.back_a, v.back_b = swap_rows(row_a, row_b)
        if fast:
            v.q_x = cross_x(v.q_x)

    def mixer_grad(ties, work):
        v.mixed, v.mixed_other, v.m, v.m_y, v.near_y = step(
            ties,
            work,
            mixer_grad_kernel,
            mixed + mixed_other + [v.g_all, v.near_y],
            [out((chip, width))] * 2 + [out((8, part // 2, width))] * 2 + [out((4, UNIT, width))],
            scratch=[pltpu.VMEM((d, d), BF)],
        )
        if fast:
            v.m_y, v.near_y = cross_cols(v.m_y), cross_cols(v.near_y)

    def sum_m(ties, work):
        terms = (0, 1) if fast else (0,)
        plan = [[(n, part) for n in terms] for part in (slice(0, 4), slice(4, 8))]
        v.m_near, v.m_far = sums(
            ties,
            work, [v.m, v.m_y], plan)

    def kv_back(ties, work):
        v.gkv, v.ksum, v.jkv, v.jkv_a, v.jkv_b = step(
            ties,
            work,
            kv_back_kernel,
            [v.dkv, v.back_a, v.back_b, v.hats, v.roots]
            + [kg, v.normed, v.m_near, v.m_far],
            [out((chip, d)), out((1, width), F32)]
            + [out((n, part + MIXER_ROWS + more, d)) for n, more in ((4, 0), (2, 0), (2, SPARE))],
            scratch=[pltpu.VMEM((d, d), BF)],
        )
        if fast:
            v.jkv_b, v.jkv_a = cross_x(v.jkv_b), cross_x(v.jkv_a)

    def q_z1(ties, work):
        halves = [[(0, half), (1, half)] for half in (slice(0, 2), slice(2, 4))]
        first, v.q = sums(
            ties,
            work, [v.q, v.q_x], halves)
        v.q_z1 = near_z(first)

    def q_z2(ties, work):
        v.q_0, far = sums(
            ties,
            work, [v.q, v.q_z1], [[(0, k), (1, k)] for k in range(2)])
        v.q_z2 = far_z(far)

    def jkv_z1(ties, work):
        (first,) = step(
            ties,
            work,
            z1_kernel,
            [v.jkv, v.jkv_a, v.small, v.hop],
            [out((2 * z_rows + 16, d))],
        )
        v.sent, v.jkv_z1 = first, near_z(first)

    def jkv_z2(ties, work):
        arrays = [v.jkv, v.jkv_b, v.sent, v.jkv_z1]
        v.jkv_0, far = step(
            ties,
            work,
            z2_kernel,
            arrays,
            [out((z_rows, d), F32), out((z_rows + 16, d))],
        )
        v.sent, v.jkv_z2 = far, far_z(far)

    def back_output(ties, work):
        v.p, p_send = step(
            ties,
            work,
            back_output_kernel,
            [v.hidden, v.wd],
            [out((own, d)), out((own, d))],
        )
        v.p_other = swap(p_send)

    def normed_back(ties, work):
        v.gn, gn_send, v.nsum = step(
            ties,
            work,
            normed_back_kernel,
            [v.gq, v.gkv, v.wqkv, v.gn, v.gn_other, v.normed] + [gain],
            [out((own, d)), out((own, d)), out((1, d), F32)],
        )
        v.gn_other = swap(gn_send)

    def result_step(ties, work):
        (v.result,) = step(
            ties,
            work,
            result_kernel,
            [x_own, v.mixed, v.mixed_other, mixer_block(0), mixer_block(1)]
            + [v.p, v.p_other, output_bias.reshape(1, d)],
            [written((own, d))],
            token=True,
        )

    def tokens_step(ties, work):
        (v.tokens_grad,) = step(
            ties,
            work,
            tokens_grad_kernel,
            [x_own, g_own, v.gn, v.gn_other, gain],
            [written((own, d))],
            token=True,
        )

    def pack(ties, work):
        (v.small,) = step(
            ties,
            work,
            pack_kernel,
            [v.hsum, v.gsum, v.nsum, v.qsum, v.ksum],
            [out((8, d), F32)],
            scratch=[pltpu.VMEM((48, 128), F32)],
        )
        if fast:
            v.hop = swap(v.small)

    def unpack(ties, work):
        if not fast:
            v.small = lax.psum(v.small, ("rows", "cols"))
        values = step(
            ties,
            work,
            unpack_kernel,
            [v.small] + ([v.hop] if fast else []),
            [out((n // 128, 128), F32) for n in (ff, d, d)] + [out((1, HD), F32)] * 2,
        )
        v.sums = [value.reshape(-1) for value in values]

    def sides(ties, work):
        arrays = [v.jkv_0, v.sent, v.jkv_z2, v.q_0, v.q_z2, v.jf_0, v.jf_z2]
        v.kept, v.sent, v.mixer_sum = step(
            ties,
            work,
            joined_sides_kernel,
            arrays,
            [out((part, half), F32), out((part + 16, half)), written((part // 2, width), F32)],
        )
        v.sides = cross_cols(v.sent)

    def cores(ties, work):
        v.mine, sent, v.small = step(
            ties,
            work,
            joined_cores_kernel,
            [v.kept, v.sent, v.sides],
            [out((part // 2, half), F32), out((part // 2, half)), out((8, d), F32)],
            scratch=[pltpu.VMEM((part, half), F32)],
        )
        v.cores = swap(sent)
        v.hop = cross_x(v.small)

    def assemble(ties, work):
        (v.joined_sum,) = step(
            ties,
            work,
            assemble_kernel,
            [v.mine, v.cores],
            [written((part // 2, 2 * half), F32)],
            token=True,
        )

    weights([], 5000)
    project([], 5000)
    cotangent_step([], 5000)
    extend([], 5000)
    hidden([], 5000)
    joined_grad([], 5000)
    dense_grad([], 5000)
    slots_step([], 5000)
    attention(0, [], 300)
    attention(1, [], 300)
    attention(2, [mixed_other[0]] if fast else [], 300)
    unslot([v.far_y] if fast else [], 1000)
    q_back([mixed_other[2]] if fast else [], 300)
    mixer_grad([], 300)
    if fast:
        jf_z1([], 1000)
    back_normed([], 300)
    fold([], 1000)
    back_output([], 100)
    sum_m([], 100)
    kv_back([], 5000)
    if fast:
        jf_z2([], 1000)
    normed_back([], 5000)
    pack([], 1000)
    if fast:
        q_z1([], 1000)
        sum_far([], 1000)
        jkv_z1([v.jf_z2, v.q_z1], 1000)
        q_z2([], 1000)
        jkv_z2([v.q_z2], 1000)
        dense_z1([], 1000)
        sides([], 5000)
    tokens_step([], 5000)
    if fast:
        dense_z2([], 1000)
    result_step([], 5000)
    if fast:
        cores([], 5000)
        dense_out([], 1000)
        assemble([], 5000)
    unpack([], 5000)

    if not fast:

        def spread_core(x, axis):
            x = jnp.expand_dims(x, axis)
            is_mine = jnp.arange(2).reshape([2 if i == axis else 1 for i in range(x.ndim)]) == core
            return jnp.where(is_mine, x, jnp.zeros_like(x))

        def reduce(x):
            x = lax.psum_scatter(x, "rows", scatter_dimension=0, tiled=True)
            return lax.psum_scatter(x, "cols", scatter_dimension=1, tiled=True).astype(F32)

        def in_order(*arrays):
            return jnp.concatenate(arrays, axis=0)

        near = jnp.concatenate([v.near, v.near_y], axis=2)
        far = jnp.concatenate([v.far, v.far_y], axis=2)
        v.dense_sum = reduce(spread_core(in_order(near, far), 1).reshape(ff, d))
        m = jnp.concatenate([v.m, v.m_y], axis=2)
        v.mixer_sum = reduce(spread_core(m, 1).reshape(d, d))
        jkv = in_order(*[x[:, :part] for x in (v.jkv, v.jkv_a, v.jkv_b)])
        jq = in_order(v.q, v.q_x).reshape(d, 1, width)
        jkv = jkv.reshape(d, 2, width)
        jf = in_order(v.jf, v.jf_x).reshape(d, ff // (2 * UNIT), UNIT)
        qkv = spread_core(jnp.concatenate([jq, jkv], axis=1), 2).reshape(d, 3 * d)
        joined = jnp.concatenate([qkv, spread_core(jf, 2).reshape(d, ff)], axis=1)
        v.joined_sum = reduce(joined)

    hidden_sum, output_sum, gain_sum, query_sum, key_sum = v.sums
    shape = (tile_rows, tile_cols, d)
    return (
        v.result.reshape(shape),
        v.tokens_grad.reshape(shape),
        v.joined_sum,
        hidden_sum,
        v.mixer_sum,
        v.dense_sum,
        output_sum,
        gain_sum,
        query_sum,
        key_sum,
    )


def solution(mesh):
    tiles, everywhere, blocks = P("rows", "cols", None), P(), P("rows", "cols")
    return jax.shard_map(
        per_device,
        mesh=mesh,
        in_specs=(tiles, blocks) + (everywhere,) * 8 + (tiles,),
        out_specs=(tiles, tiles, blocks, P(), blocks, blocks, P(), P(), P(), P()),
        check_vma=False,
    )
```
